32 devices in a mesh: rep: 2 (over x), grp: 16 (over z, y, core).
Axes of the slice: x: 2, y: 2, z: 4, core: 2. Of those that a mesh axis runs over, the one named last changes fastest.
Arguments:
- images: bfloat16 [3, 32, 197, 768], P(None, ('rep', 'grp')), may hold values from -6 to 6
- attn_qkv: bfloat16 [768, 2304], P('grp'), may hold values from -0.21875 to 0.21875
- attn_proj: bfloat16 [768, 768], P('grp'), may hold values from -1.25 to 1.25
- router: bfloat16 [768, 16], P('grp'), may hold values from -0.15625 to 0.15625
- gain_attn: bfloat16 [768], P('grp'), may hold values from 0.5 to 1.5
- gain_moe: bfloat16 [768], P('grp'), may hold values from 0.5 to 1.5
- expert_in: bfloat16 [16, 768, 3072], P('grp'), may hold values from -0.21875 to 0.21875
- expert_out: bfloat16 [16, 3072, 768], P('grp'), may hold values from -1.25 to 1.25
- routes: int32 [3, 32, 197, 2], P(None, ('rep', 'grp')), may hold values from 0 to 15, all different within a row
- cotangent: bfloat16 [3, 32, 197, 768], P(None, ('rep', 'grp')), may hold values from -6 to 6
Outputs:
- output: bfloat16 [3, 32, 197, 768], P(None, ('rep', 'grp'))
- grad_images: bfloat16 [3, 32, 197, 768], P(None, ('rep', 'grp'))
- grad_qkv: float32 [768, 2304], P('grp')
- grad_proj: float32 [768, 768], P('grp')
- grad_router: float32 [768, 16], P('grp')
- grad_gain_attn: float32 [768], P('grp')
- grad_gain_moe: float32 [768], P('grp')
- grad_expert_in: float32 [16, 768, 3072], P('grp')
- grad_expert_out: float32 [16, 3072, 768], P('grp')
The draws below stay inside these ranges and needn't reach their ends.
Inputs may be any that keep to these rules, and one draw needn't show every extreme that they name: Each token's two routes name two different experts.
All inputs are finite; a program needn't handle non-finite values.
Results may differ from the reference program's by a relative error of at most 0.023.
Values may be sent and summed in bfloat16 or wider, within the bound.
No kernel may reach another device: no remote copies, remote signals or barrier semaphores. Data moves between devices by JAX's collectives and lax.ppermute only.
A program may use at most 192 MiB of HBM per device.

```python
import jax
import jax.numpy as jnp
from jax import lax

D = 768
HEADS = 12
FF = 3072
EXPERTS = 16
SEQ = 197
IMG_DEV = 1
MICRO = 3
IMAGES = 32
CAP = 32
N_REP = 2
N_GRP = 16


def block_scale(rng, shape, cuts, low, largest):
    factor_of = 1.0
    for axis_at, shards_of in cuts:
        steps = jax.random.uniform(jax.random.fold_in(jax.random.fold_in(rng, 6), axis_at), (shards_of,), jnp.float32, low / len(cuts), largest / len(cuts))
        factor_of = factor_of * jnp.repeat(jnp.exp(steps), shape[axis_at] // shards_of).reshape((-1,) + (1,) * (len(shape) - 1 - axis_at))
    return factor_of


def distinct(stream_key, rows, count, top, lift):
    sequence = jax.random.permutation(jax.random.fold_in(stream_key, 1), count)
    pull = sequence
    for power in range(3):
        pull = pull * pull // count
    pull = pull * lift // count
    tickets = jax.random.randint(jax.random.fold_in(stream_key, 2), (rows, count), 0, 4096) + pull
    holders = jax.random.permutation(jax.random.fold_in(stream_key, 3), rows)[jnp.arange(count) % rows]
    tickets = jnp.where(jnp.arange(rows)[:, None] == holders[None, :], 1 << 14, tickets)
    score = tickets * count + jnp.arange(count)
    return lax.top_k(score.astype(jnp.int32), top)[1].astype(jnp.int32)


def noise(stream_key, dims, scale, bound, split=(), kind=jnp.bfloat16):
    loudness = block_scale(stream_key, dims, split, -0.22, 0.18) if split else 1.0
    values = jax.random.normal(stream_key, dims, jnp.float32) * scale * loudness
    return jnp.minimum(jnp.maximum(values, -bound), bound).astype(kind)


def setup_inputs(seed: int = 0) -> dict:
    streams_of = jax.random.split(jax.random.key(seed), 11)
    images = noise(streams_of[0], (MICRO, IMAGES, SEQ, D), 1.0, 6.0, ((1, 32),))
    attn_qkv = noise(streams_of[1], (D, 3 * D), D ** -0.5, 0.21875, ((0, 16),))
    attn_proj = noise(streams_of[2], (D, D), (D // 32) ** -0.5, 1.25, ((0, 16),))
    router = noise(streams_of[3], (D, EXPERTS), (2 * D) ** -0.5, 0.15625, ((0, 16),))
    gain_attn = jnp.clip(1.0 + 0.1 * jax.random.normal(streams_of[4], (D,), jnp.float32), 0.5, 1.5).astype(jnp.bfloat16)
    gain_moe = jnp.clip(1.0 + 0.1 * jax.random.normal(streams_of[5], (D,), jnp.float32), 0.5, 1.5).astype(jnp.bfloat16)
    expert_in = noise(streams_of[6], (EXPERTS, D, FF), D ** -0.5, 0.21875, ((0, 16),))
    expert_out = noise(streams_of[7], (EXPERTS, FF, D), (max(1, FF * 2 // (EXPERTS * EXPERTS))) ** -0.5, 1.25, ((0, 16),))
    routes = distinct(streams_of[8], MICRO * IMAGES * SEQ, EXPERTS, 2, 1024).reshape((MICRO, IMAGES, SEQ, 2))
    cotangent = noise(streams_of[9], (MICRO, IMAGES, SEQ, D), 1.0, 6.0, ((1, 32),))
    return {"images": images, "attn_qkv": attn_qkv, "attn_proj": attn_proj, "router": router, "gain_attn": gain_attn, "gain_moe": gain_moe, "expert_in": expert_in, "expert_out": expert_out, "routes": routes, "cotangent": cotangent}


@jax.custom_vjp
def low(v):
    return lax.optimization_barrier(v.astype(jnp.bfloat16)).astype(jnp.float32)

@jax.custom_vjp
def low_back(v):
    return v

def low_keep(v):
    return (low(v), None)

def low_pass(kept, grad):
    return (grad,)

def back_keep(v):
    return (v, None)

def back_low(kept, grad):
    return (low(grad),)
low.defvjp(low_keep, low_pass)
low_back.defvjp(back_keep, back_low)
HIGHEST = lax.Precision.HIGHEST
EPSILON = 1e-06

def normalize(values, gain_vector):
    center = values - lax.optimization_barrier(jnp.mean(values, -1, keepdims=True))
    variance = lax.optimization_barrier(jnp.mean(center * center, -1, keepdims=True))
    return center * lax.rsqrt(variance + EPSILON) * gain_vector

def attend(packed):
    images_count = packed.shape[0]
    head_dim = D // HEADS
    pieces = packed.reshape(images_count, SEQ, 3, HEADS, head_dim)
    factor = head_dim ** (-0.5)
    scores = low_back(jnp.einsum('ishd,ithd->ihst', pieces[:, :, 0], pieces[:, :, 1], precision=HIGHEST) * factor)
    weights = low(jax.nn.softmax(scores, axis=-1))
    mixture = jnp.einsum('ihst,ithd->ishd', weights, pieces[:, :, 2], precision=HIGHEST)
    return mixture.reshape(images_count, SEQ, D)

def place_slots(route_block):
    devices = N_REP * N_GRP
    per_device = route_block.reshape(devices, IMG_DEV * SEQ, 2)
    ordering = jnp.swapaxes(per_device, 1, 2).reshape(devices, 2 * IMG_DEV * SEQ)
    onehot = (ordering[:, :, None] == jnp.arange(EXPERTS, dtype=jnp.int32)).astype(jnp.int32)
    before = jnp.cumsum(onehot, axis=1, dtype=jnp.int32) - onehot
    slot_rank = lax.optimization_barrier(jnp.sum(before * onehot, axis=-1, dtype=jnp.int32))
    anchor = jnp.arange(devices, dtype=jnp.int32)[:, None]
    target = jnp.where(slot_rank < CAP, ordering * (devices * CAP) + anchor * CAP + slot_rank, EXPERTS * devices * CAP)
    kept_mask = (slot_rank < CAP).astype(jnp.float32)
    target = jnp.swapaxes(target.reshape(devices, 2, IMG_DEV * SEQ), 1, 2).reshape(-1, 2)
    kept_mask = jnp.swapaxes(kept_mask.reshape(devices, 2, IMG_DEV * SEQ), 1, 2).reshape(-1, 2)
    return (target.astype(jnp.int32), kept_mask)

def forward(tokens, attn_qkv, attn_proj, router, gain_attn, gain_moe, expert_in, expert_out, route_flat, target, kept_mask):
    devices = N_REP * N_GRP
    slots_all = EXPERTS * devices * CAP
    states = tokens.reshape(-1, D)
    normed_one = low(normalize(states, gain_attn))
    packed = low(low_back(jnp.dot(normed_one, attn_qkv, precision=HIGHEST)))
    mixture = lax.map(jax.checkpoint(attend), packed.reshape(devices, IMG_DEV, SEQ, 3 * D))
    mixture = low(low_back(mixture.reshape(-1, D)))
    middle = states + low_back(jnp.dot(mixture, attn_proj, precision=HIGHEST))
    normed_two = low(normalize(middle, gain_moe))
    probabilities = jax.nn.softmax(low_back(jnp.dot(normed_two, router, precision=HIGHEST)), axis=-1)
    gate_values = jnp.take_along_axis(probabilities, route_flat, axis=1)
    buffer = jnp.zeros((slots_all + 1, D), jnp.float32)
    buffer = buffer.at[target[:, 0]].add(normed_two).at[target[:, 1]].add(normed_two)
    buffer = low_back(buffer[:slots_all].reshape(EXPERTS, devices * CAP, D))
    hidden = low_back(jnp.einsum('end,edf->enf', buffer, expert_in, precision=HIGHEST))
    active = low(jax.nn.gelu(hidden, approximate=False))
    result = low(low_back(jnp.einsum('enf,efd->end', active, expert_out, precision=HIGHEST)))
    flat_rows = jnp.concatenate([result.reshape(slots_all, D), jnp.zeros((1, D), jnp.float32)], 0)
    first_term = kept_mask[:, 0:1] * gate_values[:, 0:1] * flat_rows[target[:, 0]]
    second = kept_mask[:, 1:2] * gate_values[:, 1:2] * flat_rows[target[:, 1]]
    return (middle + first_term + second).reshape(tokens.shape)

def reference(images, attn_qkv, attn_proj, router, gain_attn, gain_moe, expert_in, expert_out, routes, cotangent):
    weights = tuple((weight.astype(jnp.float32) for weight in (attn_qkv, attn_proj, router, gain_attn, gain_moe, expert_in, expert_out)))

    def one_batch(totals, micro_batch):
        tokens, route_block, grad_output = micro_batch
        target, kept_mask = place_slots(route_block)
        route_flat = route_block.reshape(-1, 2)

        def evaluate(states, *params):
            return forward(states, *params, route_flat, target, kept_mask)
        output, pullback = jax.vjp(evaluate, tokens.astype(jnp.float32), *weights)
        gradients = pullback(grad_output.astype(jnp.float32))
        totals = tuple((total + gradient for total, gradient in zip(totals, gradients[1:])))
        return (totals, (output.astype(jnp.bfloat16), gradients[0].astype(jnp.bfloat16)))
    initial = tuple((jnp.zeros(weight.shape, jnp.float32) for weight in weights))
    totals, (output, grad_images) = lax.scan(one_batch, initial, (images, routes, cotangent))
    return (output, grad_images, totals[0], totals[1], totals[2], totals[3], totals[4], totals[5], totals[6])
```

```python
import jax
import jax.numpy as jnp
from jax import lax
from jax.sharding import PartitionSpec as P

HEADS = 12
EPSILON = 1e-06
BF = jnp.bfloat16
F32 = jnp.float32


def dot_tn(left, right):
    return lax.dot_general(left, right, (((0,), (0,)), ((), ())), preferred_element_type=F32)


def dot_nt(left, right):
    return lax.dot_general(left, right, (((1,), (1,)), ((), ())), preferred_element_type=F32)


def dot_nn(left, right):
    return jnp.dot(left, right, preferred_element_type=F32)


def normalize(values):
    center = values - jnp.mean(values, -1, keepdims=True)
    inverse = lax.rsqrt(jnp.mean(center * center, -1, keepdims=True) + EPSILON)
    return center * inverse, inverse


def norm_backward(grad_rows, unit_rows, inverse, gain_row):
    scaled = grad_rows * gain_row
    inner = (
        scaled
        - jnp.mean(scaled, -1, keepdims=True)
        - unit_rows * jnp.mean(scaled * unit_rows, -1, keepdims=True)
    )
    return inner * inverse, jnp.sum(grad_rows * unit_rows, 0)


def split_heads(packed):
    seq = packed.shape[0]
    head_dim = packed.shape[1] // (3 * HEADS)
    pieces = packed.reshape(seq, 3, HEADS, head_dim)
    return pieces[:, 0], pieces[:, 1], pieces[:, 2], head_dim ** (-0.5)


def attend_forward(packed):
    query, keys, values, factor = split_heads(packed)
    scores = jnp.einsum("shd,thd->hst", query, keys, preferred_element_type=F32) * factor
    highest = jnp.max(scores, -1, keepdims=True)
    log_total = highest + jnp.log(jnp.sum(jnp.exp(scores - highest), -1, keepdims=True))
    weights = jnp.exp(scores - log_total).astype(BF)
    mixture = jnp.einsum("hst,thd->shd", weights, values, preferred_element_type=F32)
    return mixture.reshape(packed.shape[0], -1).astype(BF), log_total


def attend_backward(packed, log_total, grad_mixture):
    query, keys, values, factor = split_heads(packed)
    scores = jnp.einsum("shd,thd->hst", query, keys, preferred_element_type=F32) * factor
    weights = jnp.exp(scores - log_total)
    low = weights.astype(BF)
    grad_heads = grad_mixture.reshape(query.shape)
    grad_values = jnp.einsum("hst,shd->thd", low, grad_heads, preferred_element_type=F32)
    grad_weights = jnp.einsum("shd,thd->hst", grad_heads, values, preferred_element_type=F32)
    grad_scores = (
        weights * (grad_weights - jnp.sum(grad_weights * weights, -1, keepdims=True))
    ).astype(BF)
    grad_query = jnp.einsum("hst,thd->shd", grad_scores, keys, preferred_element_type=F32) * factor
    grad_keys = jnp.einsum("hst,shd->thd", grad_scores, query, preferred_element_type=F32) * factor
    stacked = jnp.stack([grad_query, grad_keys, grad_values], 1)
    return stacked.reshape(packed.shape[0], -1).astype(BF)


def slot_tables(routes, experts, capacity):
    micro, rows = routes.shape[:2]
    ordering = jnp.concatenate([routes[:, :, 0], routes[:, :, 1]], 1)
    onehot = (ordering[:, :, None] == jnp.arange(experts, dtype=jnp.int32)).astype(BF)
    count = 2 * rows
    earlier = (jnp.arange(count)[:, None] > jnp.arange(count)[None, :]).astype(BF)
    before = jnp.einsum("ab,mbe->mae", earlier, onehot, preferred_element_type=F32)
    rank = jnp.sum(before * onehot, -1).astype(jnp.int32)
    target = jnp.where(rank < capacity, ordering * capacity + rank, -1)
    slots = jnp.arange(experts * capacity, dtype=jnp.int32)[None, :, None]
    first, second = target[:, None, :rows], target[:, None, rows:]
    return ((slots == first) | (slots == second)).astype(BF)


def exchange(blocks):
    return lax.all_to_all(blocks, "grp", split_axis=0, concat_axis=0, tiled=True)


def expert_rows(slots_in, grad_in, weight_in, weight_out, full_router, mine):
    hidden = dot_nn(slots_in, weight_in)
    cumulative = 0.5 * (1.0 + lax.erf(hidden * (0.5**0.5)))
    active = (hidden * cumulative).astype(BF)
    slope = cumulative + hidden * jnp.exp(-0.5 * hidden * hidden) * 0.3989422804014327
    probs = jax.nn.softmax(dot_nn(slots_in, full_router), axis=-1)
    here = (jnp.arange(probs.shape[1], dtype=jnp.int32) == mine).astype(F32)[None]
    gate = jnp.sum(probs * here, -1, keepdims=True)
    grad_result = (gate * grad_in.astype(F32)).astype(BF)
    grad_hidden = (dot_nt(grad_result, weight_out) * slope).astype(BF)
    return active, grad_hidden, grad_result, gate, probs, here


def shards(images, attn_qkv, attn_proj, router, gain_attn, gain_moe, expert_in, expert_out, routes, cotangent):
    experts = lax.axis_size("grp")
    replicas = lax.axis_size("rep")
    mine = lax.axis_index("grp")
    micro_count, _, seq, width = images.shape
    capacity = max(2, 8 * seq * images.shape[1] // (3 * experts))
    weight_in, weight_out = expert_in[0], expert_out[0]
    split = attn_qkv.shape[1]

    tables = slot_tables(routes.reshape(micro_count, seq, 2), experts, capacity)
    grad_y = cotangent.reshape(micro_count, seq, width)

    def pack(m, rows):
        return dot_nn(tables[m], rows).astype(BF).reshape(experts, capacity, width)

    def unpack(m, blocks):
        return dot_tn(tables[m], blocks.reshape(experts * capacity, width))

    dense = jnp.concatenate([attn_qkv, attn_proj], 1)
    small = jnp.concatenate([router, gain_attn[:, None], gain_moe[:, None]], 1)
    small = jnp.pad(small, ((0, 0), (0, 128 - small.shape[1])))
    full = lax.all_gather(jnp.concatenate([dense, small], 1), "grp", axis=0, tiled=True)
    full_qkv = full[:, :split]
    full_proj = full[:, split : split + width]
    full_small = full[:, split + width :]
    full_router = full_small[:, :experts]
    gain_one = full_small[:, experts].astype(F32)[None]
    gain_two = full_small[:, experts + 1].astype(F32)[None]

    grads_in = [exchange(pack(m, grad_y[m])).reshape(-1, width) for m in range(micro_count)]

    saved, slots_in = [], []
    for m in range(micro_count):
        states = images[m].reshape(seq, width).astype(F32)
        unit_one, inverse_one = normalize(states)
        normed_one = (unit_one * gain_one).astype(BF)
        packed = dot_nn(normed_one, full_qkv).astype(BF)
        mixture, log_total = attend_forward(packed)
        middle = states + dot_nn(mixture, full_proj)
        unit_two, inverse_two = normalize(middle)
        normed_two = (unit_two * gain_two).astype(BF)
        slots_in.append(exchange(pack(m, normed_two)).reshape(-1, width))
        saved.append((unit_one, inverse_one, normed_one, packed, mixture, log_total, middle, unit_two, inverse_two))

    in_terms, out_terms = [], []
    router_total = 0.0
    outputs, input_grads = [], []
    backs, results = [], []
    for m in range(micro_count):
        x, g = slots_in[m], grads_in[m]
        active, grad_hidden, grad_result, gate, probs, here = expert_rows(
            x, g, weight_in, weight_out, full_router, mine
        )
        result = dot_nn(active, weight_out)
        grad_gate = jnp.sum(g.astype(F32) * result, -1, keepdims=True)
        grad_logit = (grad_gate * gate * (here - probs)).astype(BF)
        back = dot_nt(grad_hidden, weight_in) + dot_nt(grad_logit, full_router)
        backs.append(exchange(back.astype(BF).reshape(experts, capacity, width)))
        results.append(exchange((gate * result).astype(BF).reshape(experts, capacity, width)))
        router_total = router_total + dot_tn(x, grad_logit)
        in_terms.append((x, grad_hidden))
        out_terms.append((active, grad_result))
        if replicas == 2:
            x, g = lax.ppermute(x, "rep", [(0, 1), (1, 0)]), lax.ppermute(g, "rep", [(0, 1), (1, 0)])
            active, grad_hidden, grad_result, *_ = expert_rows(x, g, weight_in, weight_out, full_router, mine)
            in_terms.append((x, grad_hidden))
            out_terms.append((active, grad_result))

    def total(terms):
        left, right = zip(*terms)
        return dot_tn(jnp.concatenate(left, 0), jnp.concatenate(right, 0))[None]

    grad_in, grad_out = total(in_terms), total(out_terms)
    if replicas != 2:
        grad_in = lax.psum(grad_in.astype(BF), "rep").astype(F32)
        grad_out = lax.psum(grad_out.astype(BF), "rep").astype(F32)

    one_rows, packed_rows, mix_rows, mid_rows = [], [], [], []
    gain_one_total, gain_two_total = 0.0, 0.0
    for m in range(micro_count):
        unit_one, inverse_one, normed_one, packed, mixture, log_total, middle, unit_two, inverse_two = saved[m]
        grad_two = unpack(m, backs[m])
        grad_norm, gain_part = norm_backward(grad_two, unit_two, inverse_two, gain_two)
        gain_two_total = gain_two_total + gain_part
        grad_middle = grad_y[m].astype(F32) + grad_norm
        low = grad_middle.astype(BF)
        grad_mixture = dot_nt(low, full_proj).astype(BF)
        grad_packed = attend_backward(packed, log_total, grad_mixture)
        grad_one = dot_nt(grad_packed, full_qkv)
        grad_norm, gain_part = norm_backward(grad_one, unit_one, inverse_one, gain_one)
        gain_one_total = gain_one_total + gain_part
        input_grads.append((grad_middle + grad_norm).astype(BF).reshape(images.shape[1:]))
        one_rows.append(normed_one)
        packed_rows.append(grad_packed)
        mix_rows.append(mixture)
        mid_rows.append(low)
        outputs.append((middle + unpack(m, results[m])).astype(BF).reshape(images.shape[1:]))

    grad_qkv = dot_tn(jnp.concatenate(one_rows, 0), jnp.concatenate(packed_rows, 0))
    grad_proj = dot_tn(jnp.concatenate(mix_rows, 0), jnp.concatenate(mid_rows, 0))
    tail = jnp.concatenate([router_total, gain_one_total[:, None], gain_two_total[:, None]], 1)
    tail = jnp.pad(tail, ((0, 0), (0, 128 - tail.shape[1])))
    sums = jnp.concatenate([grad_qkv, grad_proj, tail], 1).astype(BF)
    sums = lax.psum_scatter(sums, "grp", scatter_dimension=0, tiled=True)
    sums = lax.psum(sums, "rep").astype(F32)
    return (
        jnp.stack(outputs),
        jnp.stack(input_grads),
        sums[:, :split],
        sums[:, split : split + width],
        sums[:, split + width : split + width + experts],
        sums[:, split + width + experts],
        sums[:, split + width + experts + 1],
        grad_in,
        grad_out,
    )


def solution(mesh):
    tokens = P(None, ("rep", "grp"), None, None)
    rows = P("grp", None)
    expert = P("grp", None, None)
    return jax.shard_map(
        shards,
        mesh=mesh,
        in_specs=(tokens, rows, rows, rows, P("grp"), P("grp"), expert, expert, tokens, tokens),
        out_specs=(tokens, tokens, rows, rows, rows, P("grp"), P("grp"), expert, expert),
        check_vma=False,
    )
```

```python
import functools

import jax
import jax.numpy as jnp
from jax import lax
from jax.experimental import pallas as pl
from jax.experimental.pallas import tpu as pltpu
from jax.sharding import PartitionSpec as P

HEADS = 12
EPSILON = 1e-06
BF = jnp.bfloat16
F32 = jnp.float32
LANES = 128
VMEM = 56 * 2**20


def dot_tn(left, right):
    return lax.dot_general(left, right, (((0,), (0,)), ((), ())), preferred_element_type=F32)


def dot_nt(left, right):
    return lax.dot_general(left, right, (((1,), (1,)), ((), ())), preferred_element_type=F32)


def dot_nn(left, right):
    return jnp.dot(left, right, preferred_element_type=F32)


def normalize(values):
    center = values - jnp.mean(values, -1, keepdims=True)
    inverse = lax.rsqrt(jnp.mean(center * center, -1, keepdims=True) + EPSILON)
    return center * inverse, inverse


def norm_backward(grad_rows, unit_rows, inverse, gain_row):
    scaled = grad_rows * gain_row
    inner = (
        scaled
        - jnp.mean(scaled, -1, keepdims=True)
        - unit_rows * jnp.mean(scaled * unit_rows, -1, keepdims=True)
    )
    return inner * inverse


def call(body, grid, ins, outs, scratch=(), flops=0, moved=0):
    return pl.pallas_call(
        body,
        grid=grid,
        in_specs=[pl.BlockSpec(block, index) for _, block, index in ins],
        out_specs=[pl.BlockSpec(block, index) for _, _, block, index in outs],
        out_shape=[jax.ShapeDtypeStruct(shape, dtype) for shape, dtype, _, _ in outs],
        scratch_shapes=list(scratch),
        compiler_params=pltpu.CompilerParams(vmem_limit_bytes=VMEM),
        cost_estimate=pl.CostEstimate(flops=flops, bytes_accessed=moved, transcendentals=0),
    )(*[array for array, _, _ in ins])


def whole(array):
    return (array, array.shape, lambda i: (0,) * array.ndim)


def made(shape, dtype):
    return (shape, dtype, shape, lambda i: (0,) * len(shape))


def of_micro(array, m):
    lead = array.ndim - 2
    return (array, (None,) * lead + array.shape[-2:], lambda i: (m,) + (0,) * (array.ndim - 1))


def head_mask(width):
    return lax.broadcasted_iota(jnp.int32, (1, LANES), 1) // (width // HEADS)


def softmax(scores):
    top = jnp.exp(scores - jnp.max(scores, -1, keepdims=True))
    return top * (1.0 / jnp.sum(top, -1, keepdims=True))


def gather_kernel(table, rows, out):
    out[...] = dot_nn(table[...], rows[...]).astype(BF).reshape(out.shape)


def forward_kernel(image, table, w_qkv, w_proj, gains, one_o, packed_o, mix_o, middle_o, slots_o):
    width = image.shape[1]
    states = image[...].astype(F32)
    unit, _ = normalize(states)
    one = (unit * gains[0:1]).astype(BF)
    one_o[...] = one
    packed_o[...] = dot_nn(one, w_qkv[...]).astype(BF)
    head = head_mask(width)
    per = LANES * HEADS // width
    factor = (width // HEADS) ** (-0.5)
    for low in range(0, width, LANES):
        query = packed_o[:, low : low + LANES]
        keys = packed_o[:, width + low : width + low + LANES]
        values = packed_o[:, 2 * width + low : 2 * width + low + LANES]
        mixed = 0.0
        for h in range(per):
            mine = (head == h).astype(BF)
            weights = softmax(dot_nt(query * mine, keys) * factor).astype(BF)
            mixed = mixed + dot_nn(weights, values * mine)
        mix_o[:, low : low + LANES] = mixed.astype(BF)
    middle = states + dot_nn(mix_o[...], w_proj[...])
    middle_o[...] = middle
    unit, _ = normalize(middle)
    two = (unit * gains[1:2]).astype(BF)
    slots_o[...] = dot_nn(table[...], two).astype(BF).reshape(slots_o.shape)


def backward_kernel(
    column, image, grad_y, middle, packed, backs, table, w_qkv, w_proj, gains, grad_image_o, grad_packed_o, low_o, tail_o, mixture_s
):
    width = image.shape[1]
    backs = backs[...]
    grad_two = dot_tn(table[...], backs.reshape(-1, width))
    unit, inverse = normalize(middle[...])
    gain_two = grad_two * unit
    grad_middle = grad_y[...].astype(F32) + norm_backward(grad_two, unit, inverse, gains[1:2])
    low_o[...] = grad_middle.astype(BF)
    mixture_s[...] = dot_nt(low_o[...], w_proj[...]).astype(BF)
    head = head_mask(width)
    per = LANES * HEADS // width
    factor = (width // HEADS) ** (-0.5)
    for low in range(0, width, LANES):
        query = packed[:, low : low + LANES]
        keys = packed[:, width + low : width + low + LANES]
        values = packed[:, 2 * width + low : 2 * width + low + LANES]
        grad_mixed = mixture_s[:, low : low + LANES]
        grad_query = grad_keys = grad_values = 0.0
        for h in range(per):
            mine = (head == h).astype(BF)
            query_h, keys_h, grad_h = query * mine, keys * mine, grad_mixed * mine
            weights = softmax(dot_nt(query_h, keys) * factor)
            grad_values = grad_values + dot_tn(weights.astype(BF), grad_h)
            grad_weights = dot_nt(grad_h, values)
            inner = jnp.sum(grad_weights * weights, -1, keepdims=True)
            grad_scores = (weights * (grad_weights - inner)).astype(BF)
            grad_query = grad_query + dot_nn(grad_scores, keys_h)
            grad_keys = grad_keys + dot_tn(grad_scores, query_h)
        grad_packed_o[:, low : low + LANES] = (grad_query * factor).astype(BF)
        grad_packed_o[:, width + low : width + low + LANES] = (grad_keys * factor).astype(BF)
        grad_packed_o[:, 2 * width + low : 2 * width + low + LANES] = grad_values.astype(BF)
    grad_one = dot_nt(grad_packed_o[...], w_qkv[...])
    unit, inverse = normalize(image[...].astype(F32))
    gain_one = grad_one * unit
    grad_image_o[...] = (grad_middle + norm_backward(grad_one, unit, inverse, gains[0:1])).astype(BF)
    lane = lax.broadcasted_iota(jnp.int32, (image.shape[0], LANES), 1)
    tail = 0.0
    for at, gain in ((column, gain_one), (column + 1, gain_two)):
        ones = (lane == at).astype(BF)
        high = gain.astype(BF)
        tail = tail + dot_tn(high, ones) + dot_tn((gain - high.astype(F32)).astype(BF), ones)
    tail_o[...] = tail


def expert_kernel(own, experts, slots_in, grad_in, here, router, w_in, w_out, active_o, hidden_o, result_o, *rest):
    step = pl.program_id(0)
    if own:
        back_o, sent_o, tail_o, probs_s, result_s, back_s = rest
    width = slots_in.shape[-1]
    rows = slots_in[...].reshape(-1, width)

    @pl.when(step == 0)
    def _():
        logits = dot_nn(rows, router[...])
        lane = lax.broadcasted_iota(jnp.int32, logits.shape, 1)
        probs = softmax(jnp.where(lane < experts, logits, -1e30))
        gate = jnp.sum(probs * here[...], -1, keepdims=True)
        result_o[...] = (gate * grad_in[...].reshape(-1, width).astype(F32)).astype(BF)
        if own:
            probs_s[...] = probs
            result_s[...] = jnp.zeros_like(result_s)
            back_s[...] = jnp.zeros_like(back_s)

    hidden = dot_nn(rows, w_in[...])
    grad_active = dot_nt(result_o[...], w_out[...])
    cumulative = 0.5 + 0.5 * lax.erf(hidden * (0.5**0.5))
    active = (hidden * cumulative).astype(BF)
    slope = cumulative + hidden * jnp.exp(-0.5 * hidden * hidden) * 0.3989422804014327
    grad_hidden = (grad_active * slope).astype(BF)
    active_o[...] = active
    hidden_o[...] = grad_hidden
    if own:
        result_s[...] += dot_nn(active, w_out[...])
        back_s[...] += dot_nt(grad_hidden, w_in[...])

        @pl.when(step == pl.num_programs(0) - 1)
        def _():
            probs = probs_s[...]
            gate = jnp.sum(probs * here[...], -1, keepdims=True)
            result = result_s[...]
            grad_gate = jnp.sum(grad_in[...].reshape(-1, width).astype(F32) * result, -1, keepdims=True)
            grad_logit = (grad_gate * gate * (here[...] - probs)).astype(BF)
            back_o[...] = (back_s[...] + dot_nt(grad_logit, router[...])).astype(BF).reshape(back_o.shape)
            sent_o[...] = (gate * result).astype(BF).reshape(sent_o.shape)
            tail_o[...] = dot_tn(rows, grad_logit)


def total_kernel(terms, *refs):
    total = 0.0
    for left, right in zip(refs[:terms], refs[terms : 2 * terms]):
        total = total + dot_tn(left[...].reshape(-1, left.shape[-1]), right[...].reshape(-1, right.shape[-1]))
    refs[-1][...] = total


def dense_kernel(micro, *refs):
    ones, packs, mixes, lows, tails, out = (refs[i * micro : (i + 1) * micro] for i in (0, 1, 2, 3, 4, 6))
    tails = refs[4 * micro : 6 * micro]
    out = refs[-1]
    width = ones[0].shape[-1]
    for j in range(3):
        part = slice(j * width, (j + 1) * width)
        out[:, part] = sum(dot_tn(a[...], b[:, part]) for a, b in zip(ones, packs)).astype(BF)
    out[:, 3 * width : 4 * width] = sum(dot_tn(a[...], b[...]) for a, b in zip(mixes, lows)).astype(BF)
    out[:, 4 * width :] = sum(t[...] for t in tails).astype(BF)


def combine_kernel(middle, table, results, out):
    out[...] = (middle[...] + dot_tn(table[...], results[...].reshape(-1, middle.shape[-1]))).astype(BF)


def slot_tables(routes, experts, capacity):
    rows = routes.shape[1]
    ordering = jnp.concatenate([routes[:, :, 0], routes[:, :, 1]], 1)
    onehot = (ordering[:, :, None] == jnp.arange(experts, dtype=jnp.int32)).astype(BF)
    count = 2 * rows
    earlier = (jnp.arange(count)[:, None] > jnp.arange(count)[None, :]).astype(BF)
    before = jnp.einsum("ab,mbe->mae", earlier, onehot, preferred_element_type=F32)
    rank = jnp.sum(before * onehot, -1).astype(jnp.int32)
    target = jnp.where(rank < capacity, ordering * capacity + rank, -1)
    slots = jnp.arange(experts * capacity, dtype=jnp.int32)[None, :, None]
    first, second = target[:, None, :rows], target[:, None, rows:]
    return ((slots == first) | (slots == second)).astype(BF)


def exchange(blocks):
    return lax.all_to_all(blocks, "grp", split_axis=0, concat_axis=0, tiled=True)


def add_low(left, right):
    return (left.astype(F32) + right.astype(F32)).astype(BF)


def scatter_sums(sums, experts, replicas):
    bits = experts.bit_length() - 1
    place = lax.axis_index("grp")
    own_rep = lax.axis_index("rep")
    rows, columns = sums.shape[0] // experts, sums.shape[1] - LANES
    half = columns // 2
    sums = sums.reshape((2,) * bits + (rows, sums.shape[1]))

    def halve(array, bit, axis):
        mine = (place >> bit) & 1
        sent = lax.dynamic_index_in_dim(array, 1 - mine, axis, keepdims=False)
        kept = lax.dynamic_index_in_dim(array, mine, axis, keepdims=False)
        return add_low(kept, lax.ppermute(sent, "grp", [(g, g ^ (1 << bit)) for g in range(experts)]))

    swap = [(0, 1), (1, 0)]

    def halve_columns(array, shared):
        cut = (array.shape[-1] - shared) // 2
        parts = [array[..., :cut], array[..., cut : 2 * cut]]
        mine, other = (jnp.where(own_rep == 0, parts[i], parts[1 - i]) for i in (0, 1))
        if shared:
            mine, other = (jnp.concatenate([p, array[..., 2 * cut :]], -1) for p in (mine, other))
        return add_low(mine, lax.ppermute(other, "rep", swap))

    first = halve(sums, 0, bits - 1)
    left = jnp.concatenate([first[..., :half], first[..., columns:]], -1)
    right = first[..., half:columns]
    if replicas == 2:
        left = halve_columns(left, LANES)
    left = halve(left, 1, bits - 2)
    right = halve(right, 1, bits - 2)
    if replicas == 2:
        right = halve_columns(right, 0)
    for bit in range(2, bits):
        left = halve(left, bit, bits - 1 - bit)
        right = halve(right, bit, bits - 1 - bit)
    if replicas == 2:
        mine = jnp.concatenate([left[:, :-LANES], right], -1)
        other = lax.ppermute(mine, "rep", swap)
        low, high = (jnp.where(own_rep == i, mine, other) for i in (0, 1))
        cut = mine.shape[1] // 2
        pieces = [low[:, :cut], high[:, :cut], low[:, cut:], high[:, cut:], left[:, -LANES:]]
        return jnp.concatenate(pieces, 1).astype(F32)
    both = jnp.concatenate([left[:, :-LANES], right, left[:, -LANES:]], 1)
    return lax.psum(both, "rep").astype(F32)


def shards(images, attn_qkv, attn_proj, router, gain_attn, gain_moe, expert_in, expert_out, routes, cotangent):
    experts = lax.axis_size("grp")
    replicas = lax.axis_size("rep")
    mine = lax.axis_index("grp")
    micro, _, seq, width = images.shape
    capacity = max(2, 8 * seq * images.shape[1] // (3 * experts))
    slots = experts * capacity
    split = attn_qkv.shape[1]
    deep = expert_in.shape[2]
    here = (lax.broadcasted_iota(jnp.int32, (1, LANES), 1) == mine).astype(F32)

    tables = slot_tables(routes.reshape(micro, seq, 2), experts, capacity)

    small = jnp.concatenate([router, gain_attn[:, None], gain_moe[:, None]], 1)
    small = jnp.pad(small, ((0, 0), (0, LANES - small.shape[1])))
    full = lax.all_gather(jnp.concatenate([attn_qkv, attn_proj, small], 1), "grp", axis=0, tiled=True)
    gains = full[:, split + width + experts : split + width + experts + 2].T.astype(F32)
    w_qkv = (full, (width, split), lambda i: (0, 0))
    w_proj = (full, (width, width), lambda i: (0, split // width))
    w_router = (full, (width, LANES), lambda i: (0, (split + width) // LANES))

    packed_grads = call(
        gather_kernel,
        (micro,),
        [
            (tables, (None, slots, seq), lambda i: (i, 0, 0)),
            (cotangent, (None, None, seq, width), lambda i: (i, 0, 0, 0)),
        ],
        [((experts, micro, capacity, width), BF, (experts, None, capacity, width), lambda i: (0, i, 0, 0))],
        flops=2 * micro * slots * seq * width,
    )[0]
    grads_in = exchange(packed_grads.reshape(experts, micro * capacity, width)).reshape(packed_grads.shape)

    def slots_of(array, m):
        return (array, (experts, None, capacity, width), lambda i: (0, m, 0, 0))

    saved, slots_in = [], []
    for m in range(micro):
        one, packed, mixture, middle, sent = call(
            forward_kernel,
            (1,),
            [of_micro(images, m), of_micro(tables, m), w_qkv, w_proj, whole(gains)],
            [
                made((seq, width), BF),
                made((seq, split), BF),
                made((seq, width), BF),
                made((seq, width), F32),
                made((experts, capacity, width), BF),
            ],
            flops=6 * 10**9,
        )
        slots_in.append(exchange(sent))
        saved.append((one, packed, mixture, middle))

    block = 512
    swap = [(0, 1), (1, 0)]

    def expert_call(own, x, grads):
        ins = [
            whole(x),
            grads,
            whole(here),
            w_router,
            (expert_in, (None, width, block), lambda i: (0, 0, i)),
            (expert_out, (None, block, width), lambda i: (0, i, 0)),
        ]
        outs = [
            ((slots, deep), BF, (slots, block), lambda i: (0, i)),
            ((slots, deep), BF, (slots, block), lambda i: (0, i)),
            made((slots, width), BF),
        ]
        scratch = []
        if own:
            outs += [made((experts, capacity, width), BF)] * 2 + [made((width, LANES), F32)]
            scratch = [pltpu.VMEM((slots, LANES), F32)] + [pltpu.VMEM((slots, width), F32)] * 2
        return call(
            functools.partial(expert_kernel, own, experts),
            (deep // block,),
            ins,
            outs,
            scratch,
            flops=2 * slots * width * deep * (6 if own else 4),
        )

    others_grads = lax.ppermute(grads_in, "rep", swap) if replicas == 2 else None
    in_terms, out_terms, tails, backs, results = [], [], [], [], []
    for m in range(micro):
        x = slots_in[m]
        active, grad_hidden, grad_result, back, sent, tail = expert_call(True, x, slots_of(grads_in, m))
        backs.append(exchange(back))
        results.append(sent)
        tails.append(tail)
        in_terms.append((x.reshape(slots, width), grad_hidden))
        out_terms.append((active, grad_result))
        if replicas == 2:
            x = lax.ppermute(x, "rep", swap)
            active, grad_hidden, grad_result = expert_call(False, x, slots_of(others_grads, m))
            in_terms.append((x.reshape(slots, width), grad_hidden))
            out_terms.append((active, grad_result))
    results = exchange(jnp.concatenate(results, 1)).reshape(packed_grads.shape)

    one_rows, packed_rows, mix_rows, low_rows, input_grads = [], [], [], [], []
    for m in range(micro):
        one, packed, mixture, middle = saved[m]
        grad_image, grad_packed, low, tail = call(
            functools.partial(backward_kernel, experts),
            (1,),
            [
                of_micro(images, m),
                of_micro(cotangent, m),
                whole(middle),
                whole(packed),
                whole(backs[m]),
                of_micro(tables, m),
                w_qkv,
                w_proj,
                whole(gains),
            ],
            [made((seq, width), BF), made((seq, split), BF), made((seq, width), BF), made((width, LANES), F32)],
            [pltpu.VMEM((seq, width), BF)],
            flops=8 * 10**9,
        )
        input_grads.append(grad_image.reshape(images.shape[1:]))
        one_rows.append(one)
        packed_rows.append(grad_packed)
        mix_rows.append(mixture)
        low_rows.append(low)
        tails.append(tail)

    sums = call(
        functools.partial(dense_kernel, micro),
        (1,),
        [whole(a) for a in one_rows + packed_rows + mix_rows + low_rows + tails],
        [made(full.shape, BF)],
        flops=5 * 10**9,
    )[0]
    sums = scatter_sums(sums, experts, replicas)

    def total(terms, lead):
        left, right = zip(*terms)
        count = len(terms)
        if lead:
            lefts = [(a, (slots, block), lambda i: (0, i)) for a in left]
            rights = [whole(a) for a in right]
            out = ((1, deep, width), F32, (None, block, width), lambda i: (0, i, 0))
        else:
            lefts = [whole(a) for a in left]
            rights = [(a, (slots, block), lambda i: (0, i)) for a in right]
            out = ((1, width, deep), F32, (None, width, block), lambda i: (0, 0, i))
        grad = call(
            functools.partial(total_kernel, count),
            (deep // block,),
            lefts + rights,
            [out],
            flops=2 * count * slots * width * deep,
        )[0]
        return grad if replicas == 2 else lax.psum(grad.astype(BF), "rep").astype(F32)

    grad_in, grad_out = total(in_terms, False), total(out_terms, True)

    middles = [s[3] for s in saved]
    outputs = [
        call(
            combine_kernel,
            (1,),
            [whole(middles[m]), of_micro(tables, m), slots_of(results, m)],
            [made((seq, width), BF)],
            flops=10**9,
        )[0].reshape(images.shape[1:])
        for m in range(micro)
    ]
    return (
        jnp.stack(outputs),
        jnp.stack(input_grads),
        sums[:, :split],
        sums[:, split : split + width],
        sums[:, split + width : split + width + experts],
        sums[:, split + width + experts],
        sums[:, split + width + experts + 1],
        grad_in,
        grad_out,
    )


def solution(mesh):
    tokens = P(None, ("rep", "grp"), None, None)
    rows = P("grp", None)
    expert = P("grp", None, None)
    return jax.shard_map(
        shards,
        mesh=mesh,
        in_specs=(tokens, rows, rows, rows, P("grp"), P("grp"), expert, expert, tokens, tokens),
        out_specs=(tokens, tokens, rows, rows, rows, P("grp"), P("grp"), expert, expert),
        check_vma=False,
    )
```

```python
import functools

import jax
import jax.numpy as jnp
from jax import lax
from jax.experimental import pallas as pl
from jax.experimental.pallas import tpu as pltpu
from jax.sharding import PartitionSpec as P

HEADS = 12
EPSILON = 1e-06
BF = jnp.bfloat16
F32 = jnp.float32
LANES = 128
COST = 0.6
VMEM = 56 * 2**20


def dot_tn(left, right):
    return lax.dot_general(left, right, (((0,), (0,)), ((), ())), preferred_element_type=F32)


def dot_nt(left, right):
    return lax.dot_general(left, right, (((1,), (1,)), ((), ())), preferred_element_type=F32)


def dot_nn(left, right):
    return jnp.dot(left, right, preferred_element_type=F32)


def normalize(values):
    center = values - jnp.mean(values, -1, keepdims=True)
    inverse = lax.rsqrt(jnp.mean(center * center, -1, keepdims=True) + EPSILON)
    return center * inverse, inverse


def norm_backward(grad_rows, unit_rows, inverse, gain_row):
    scaled = grad_rows * gain_row
    inner = (
        scaled
        - jnp.mean(scaled, -1, keepdims=True)
        - unit_rows * jnp.mean(scaled * unit_rows, -1, keepdims=True)
    )
    return inner * inverse


def call(name, body, grid, ins, outs, scratch=(), flops=0, vmem=VMEM, through=(), into=(), after=()):
    buffers = [(i, array) for i, array in enumerate(into) if array is not None]
    kept = list(through) + [array for _, array in buffers] + list(after)
    count, made_count = len(ins), len(outs)
    aliases = {count + i: made_count + i for i in range(len(through))}
    for place, (i, _) in enumerate(buffers):
        aliases[count + len(through) + place] = i

    def inner(*refs):
        rest = refs[count + len(kept) :]
        body(*refs[:count], *rest[:made_count], *rest[made_count + len(through) :])

    anywhere = pl.BlockSpec(memory_space=pl.ANY)
    return pl.pallas_call(
        inner if kept else body,
        grid=grid,
        in_specs=[pl.BlockSpec(block, index) for _, block, index in ins] + [anywhere] * len(kept),
        out_specs=[pl.BlockSpec(block, index) for _, _, block, index in outs] + [anywhere] * len(through),
        out_shape=[jax.ShapeDtypeStruct(shape, dtype) for shape, dtype, _, _ in outs]
        + [jax.ShapeDtypeStruct(array.shape, array.dtype) for array in through],
        scratch_shapes=list(scratch),
        input_output_aliases=aliases,
        compiler_params=pltpu.CompilerParams(vmem_limit_bytes=vmem),
        cost_estimate=pl.CostEstimate(flops=int(flops * COST), bytes_accessed=0, transcendentals=0),
        name=name,
    )(*[array for array, _, _ in ins], *kept)


def whole(array):
    return (array, array.shape, lambda i: (0,) * array.ndim)


def made(shape, dtype):
    return (shape, dtype, shape, lambda i: (0,) * len(shape))


def of_micro(array, m):
    lead = array.ndim - 2
    return (array, (None,) * lead + array.shape[-2:], lambda i: (m,) + (0,) * (array.ndim - 1))


def head_mask(width):
    return lax.broadcasted_iota(jnp.int32, (1, LANES), 1) // (width // HEADS)


def softmax(scores):
    top = jnp.exp(scores - jnp.max(scores, -1, keepdims=True))
    return top * (1.0 / jnp.sum(top, -1, keepdims=True))


def hold_kernel(out):
    out[...] = jnp.zeros_like(out)


def hold(array, *waited):
    after = [corner(w) for w in waited if w is not None]
    if not after:
        return array
    return call("hold", hold_kernel, (1,), [], [made((8, LANES), F32)], through=[array], after=after)[1]


def gather_kernel(table, rows, out):
    out[...] = dot_nn(table[...], rows[...]).astype(BF).reshape(out.shape)


def forward_kernel(image, table, w_qkv, w_proj, gains, one_o, packed_o, mix_o, middle_o, slots_o):
    width = image.shape[1]
    states = image[...].astype(F32)
    unit, _ = normalize(states)
    one = (unit * gains[0:1]).astype(BF)
    one_o[...] = one
    packed_o[...] = dot_nn(one, w_qkv[...]).astype(BF)
    head = head_mask(width)
    per = LANES * HEADS // width
    factor = (width // HEADS) ** (-0.5)
    for low in range(0, width, LANES):
        query = packed_o[:, low : low + LANES]
        keys = packed_o[:, width + low : width + low + LANES]
        values = packed_o[:, 2 * width + low : 2 * width + low + LANES]
        mixed = 0.0
        for h in range(per):
            mine = (head == h).astype(BF)
            weights = softmax(dot_nt(query * mine, keys) * factor).astype(BF)
            mixed = mixed + dot_nn(weights, values * mine)
        mix_o[:, low : low + LANES] = mixed.astype(BF)
    middle = states + dot_nn(mix_o[...], w_proj[...])
    middle_o[...] = middle
    unit, _ = normalize(middle)
    two = (unit * gains[1:2]).astype(BF)
    slots_o[...] = dot_nn(table[...], two).astype(BF).reshape(slots_o.shape)


def backward_kernel(
    column, image, grad_y, middle, packed, backs, table, w_qkv, w_proj, gains, grad_image_o, grad_packed_o, low_o, tail_o, mixture_s
):
    width = image.shape[1]
    backs = backs[...]
    grad_two = dot_tn(table[...], backs.reshape(-1, width))
    unit, inverse = normalize(middle[...])
    gain_two = grad_two * unit
    grad_middle = grad_y[...].astype(F32) + norm_backward(grad_two, unit, inverse, gains[1:2])
    low_o[...] = grad_middle.astype(BF)
    mixture_s[...] = dot_nt(low_o[...], w_proj[...]).astype(BF)
    head = head_mask(width)
    per = LANES * HEADS // width
    factor = (width // HEADS) ** (-0.5)
    for low in range(0, width, LANES):
        query = packed[:, low : low + LANES]
        keys = packed[:, width + low : width + low + LANES]
        values = packed[:, 2 * width + low : 2 * width + low + LANES]
        grad_mixed = mixture_s[:, low : low + LANES]
        grad_query = grad_keys = grad_values = 0.0
        for h in range(per):
            mine = (head == h).astype(BF)
            query_h, keys_h, grad_h = query * mine, keys * mine, grad_mixed * mine
            weights = softmax(dot_nt(query_h, keys) * factor)
            grad_values = grad_values + dot_tn(weights.astype(BF), grad_h)
            grad_weights = dot_nt(grad_h, values)
            inner = jnp.sum(grad_weights * weights, -1, keepdims=True)
            grad_scores = (weights * (grad_weights - inner)).astype(BF)
            grad_query = grad_query + dot_nn(grad_scores, keys_h)
            grad_keys = grad_keys + dot_tn(grad_scores, query_h)
        grad_packed_o[:, low : low + LANES] = (grad_query * factor).astype(BF)
        grad_packed_o[:, width + low : width + low + LANES] = (grad_keys * factor).astype(BF)
        grad_packed_o[:, 2 * width + low : 2 * width + low + LANES] = grad_values.astype(BF)
    grad_one = dot_nt(grad_packed_o[...], w_qkv[...])
    unit, inverse = normalize(image[...].astype(F32))
    gain_one = grad_one * unit
    grad_image_o[...] = (grad_middle + norm_backward(grad_one, unit, inverse, gains[0:1])).astype(BF)
    lane = lax.broadcasted_iota(jnp.int32, (image.shape[0], LANES), 1)
    tail = 0.0
    for at, gain in ((column, gain_one), (column + 1, gain_two)):
        ones = (lane == at).astype(BF)
        high = gain.astype(BF)
        tail = tail + dot_tn(high, ones) + dot_tn((gain - high.astype(F32)).astype(BF), ones)
    tail_o[...] = tail


def expert_kernel(own, experts, slots_in, grad_in, here, router, w_in, w_out, active_o, hidden_o, result_o, rows_o, *rest):
    step = pl.program_id(0)
    if own:
        sent_o, back_o, tail_o, probs_s, result_s, back_s = rest
    width = slots_in.shape[-1]
    rows = slots_in[...].reshape(-1, width)

    @pl.when(step == 0)
    def _():
        rows_o[...] = rows
        logits = dot_nn(rows, router[...])
        lane = lax.broadcasted_iota(jnp.int32, logits.shape, 1)
        probs = softmax(jnp.where(lane < experts, logits, -1e30))
        gate = jnp.sum(probs * here[...], -1, keepdims=True)
        result_o[...] = (gate * grad_in[...].reshape(-1, width).astype(F32)).astype(BF)
        if own:
            probs_s[...] = probs
            result_s[...] = jnp.zeros_like(result_s)
            back_s[...] = jnp.zeros_like(back_s)

    hidden = dot_nn(rows, w_in[...])
    grad_active = dot_nt(result_o[...], w_out[...])
    cumulative = 0.5 + 0.5 * lax.erf(hidden * (0.5**0.5))
    active = (hidden * cumulative).astype(BF)
    slope = cumulative + hidden * jnp.exp(-0.5 * hidden * hidden) * 0.3989422804014327
    grad_hidden = (grad_active * slope).astype(BF)
    active_o[...] = active
    hidden_o[...] = grad_hidden
    if own:
        result_s[...] += dot_nn(active, w_out[...])
        back_s[...] += dot_nt(grad_hidden, w_in[...])

        @pl.when(step == pl.num_programs(0) - 1)
        def _():
            probs = probs_s[...]
            gate = jnp.sum(probs * here[...], -1, keepdims=True)
            result = result_s[...]
            grad_gate = jnp.sum(grad_in[...].reshape(-1, width).astype(F32) * result, -1, keepdims=True)
            grad_logit = (grad_gate * gate * (here[...] - probs)).astype(BF)
            back_o[...] = (back_s[...] + dot_nt(grad_logit, router[...])).astype(BF).reshape(back_o.shape)
            sent_o[...] = (gate * result).astype(BF).reshape(sent_o.shape)
            tail_o[...] = dot_tn(rows, grad_logit)


def total_kernel(left, right, out):
    out[...] = dot_tn(left[...].reshape(-1, left.shape[-1]), right[...].reshape(-1, right.shape[-1]))


def dense_kernel(micro, *refs):
    ones, packs, mixes, lows = (refs[i * micro : (i + 1) * micro] for i in range(4))
    tails, out = refs[4 * micro : 6 * micro], refs[-1]
    width = ones[0].shape[-1]
    for j in range(3):
        part = slice(j * width, (j + 1) * width)
        out[:, part] = sum(dot_tn(a[...], b[:, part]) for a, b in zip(ones, packs)).astype(BF)
    out[:, 3 * width : 4 * width] = sum(dot_tn(a[...], b[...]) for a, b in zip(mixes, lows)).astype(BF)
    out[:, 4 * width :] = sum(t[...] for t in tails).astype(BF)


def combine_kernel(micro, *refs):
    middles, (tables, results, out) = refs[:micro], refs[micro:]
    for m, middle in enumerate(middles):
        rows = results[:, m].reshape(-1, middle.shape[-1])
        out[m, 0] = (middle[...] + dot_tn(tables[m], rows)).astype(BF)


def slot_tables(routes, experts, capacity):
    rows = routes.shape[1]
    ordering = jnp.concatenate([routes[:, :, 0], routes[:, :, 1]], 1)
    onehot = (ordering[:, :, None] == jnp.arange(experts, dtype=jnp.int32)).astype(BF)
    count = 2 * rows
    earlier = (jnp.arange(count)[:, None] > jnp.arange(count)[None, :]).astype(BF)
    before = jnp.einsum("ab,mbe->mae", earlier, onehot, preferred_element_type=F32)
    rank = jnp.sum(before * onehot, -1).astype(jnp.int32)
    target = jnp.where(rank < capacity, ordering * capacity + rank, -1)
    slots = jnp.arange(experts * capacity, dtype=jnp.int32)[None, :, None]
    first, second = target[:, None, :rows], target[:, None, rows:]
    return ((slots == first) | (slots == second)).astype(BF)


def exchange(blocks):
    return lax.all_to_all(blocks, "grp", split_axis=0, concat_axis=0, tiled=True)


def add_low(left, right):
    return (left.astype(F32) + right.astype(F32)).astype(BF)


def corner(array):
    return array[(0,) * (array.ndim - 2)][:16, :LANES]


def scatter_sums(sums, experts, replicas, beside):
    bits = experts.bit_length() - 1
    place = lax.axis_index("grp")
    own_rep = lax.axis_index("rep")
    rows, columns = sums.shape[0] // experts, sums.shape[1] - LANES
    half = columns // 2
    swap = [(0, 1), (1, 0)]
    sums = sums.reshape((2,) * bits + (rows, sums.shape[1]))

    def halve(array, bit):
        mine, axis = (place >> bit) & 1, bits - 1 - bit
        sent = lax.dynamic_index_in_dim(array, 1 - mine, axis, keepdims=False)
        kept = lax.dynamic_index_in_dim(array, mine, axis, keepdims=False)
        came = lax.ppermute(sent, "grp", [(g, g ^ (1 << bit)) for g in range(experts)])
        return add_low(beside[bit](kept), came)

    sums = halve(sums, 0)
    if replicas == 2:
        parts = [sums[..., :half], sums[..., half:columns]]
        mine, other = (
            jnp.concatenate([jnp.where(own_rep == 0, parts[i], parts[1 - i]), sums[..., columns:]], -1)
            for i in (0, 1)
        )
        came = lax.ppermute(other, "rep", swap)
        sums = add_low(beside[bits](mine), came)
    for bit in range(1, bits):
        sums = halve(sums, bit)
    if replicas != 2:
        return lax.psum(sums, "rep").astype(F32)
    mine = sums[:, :half]
    other = lax.ppermute(mine, "rep", swap)
    low, high = (jnp.where(own_rep == i, mine, other) for i in (0, 1))
    return jnp.concatenate([low, high, sums[:, half:]], 1).astype(F32)


def shards(images, attn_qkv, attn_proj, router, gain_attn, gain_moe, expert_in, expert_out, routes, cotangent):
    experts = lax.axis_size("grp")
    replicas = lax.axis_size("rep")
    mine = lax.axis_index("grp")
    micro, _, seq, width = images.shape
    capacity = max(2, 8 * seq * images.shape[1] // (3 * experts))
    slots = experts * capacity
    split = attn_qkv.shape[1]
    deep = expert_in.shape[2]
    here = (lax.broadcasted_iota(jnp.int32, (1, LANES), 1) == mine).astype(F32)

    tables = slot_tables(routes.reshape(micro, seq, 2), experts, capacity)

    small = jnp.concatenate([router, gain_attn[:, None], gain_moe[:, None]], 1)
    small = jnp.pad(small, ((0, 0), (0, LANES - small.shape[1])))
    full = lax.all_gather(jnp.concatenate([attn_qkv, attn_proj, small], 1), "grp", axis=0, tiled=True)
    gains = full[:, split + width + experts : split + width + experts + 2].T.astype(F32)
    w_qkv = (full, (width, split), lambda i: (0, 0))
    w_proj = (full, (width, width), lambda i: (0, split // width))
    w_router = (full, (width, LANES), lambda i: (0, (split + width) // LANES))

    packed_grads = call(
        "pack",
        gather_kernel,
        (micro,),
        [
            (tables, (None, slots, seq), lambda i: (i, 0, 0)),
            (cotangent, (None, None, seq, width), lambda i: (i, 0, 0, 0)),
        ],
        [((experts, micro, capacity, width), BF, (experts, None, capacity, width), lambda i: (0, i, 0, 0))],
        flops=2 * micro * slots * seq * width,
    )[0]
    grads_in = exchange(packed_grads.reshape(experts, micro * capacity, width)).reshape(packed_grads.shape)

    def slots_of(array, m):
        return (array, (experts, None, capacity, width), lambda i: (0, m, 0, 0))

    saved, sents = [], []
    for m in range(micro):
        one, packed, mixture, middle, sent, *handed = call(
            "attend",
            forward_kernel,
            (1,),
            [of_micro(images, m), of_micro(tables, m), w_qkv, w_proj, whole(gains)],
            [
                made((seq, width), BF),
                made((seq, split), BF),
                made((seq, width), BF),
                made((seq, width), F32),
                made((experts, capacity, width), BF),
            ],
            flops=6 * 10**9,
            through=sents[1:],
        )
        sents[1:] = handed
        sents.append(sent)
        saved.append((one, packed, mixture, middle))

    block = 1024
    swap = [(0, 1), (1, 0)]
    sets = 2 * micro if replicas == 2 else micro
    stacks = [None] * 5

    def expert_call(own, m, x, grads, through):
        place = m if own else micro + m
        ins = [
            whole(x),
            grads,
            whole(here),
            w_router,
            (expert_in, (None, width, block), lambda i: (0, 0, i)),
            (expert_out, (None, block, width), lambda i: (0, i, 0)),
        ]
        outs = [
            ((sets, slots, deep), BF, (None, slots, block), lambda i: (place, 0, i)),
            ((sets, slots, deep), BF, (None, slots, block), lambda i: (place, 0, i)),
            ((sets, slots, width), BF, (None, slots, width), lambda i: (place, 0, 0)),
            ((sets, slots, width), BF, (None, slots, width), lambda i: (place, 0, 0)),
        ]
        scratch = []
        if own:
            outs += [
                (packed_grads.shape, BF, (experts, None, capacity, width), lambda i: (0, m, 0, 0)),
                made((experts, capacity, width), BF),
                made((width, LANES), F32),
            ]
            scratch = [pltpu.VMEM((slots, LANES), F32)] + [pltpu.VMEM((slots, width), F32)] * 2
        count = 5 if own else 4
        made_here = call(
            "expert_own" if own else "expert_other",
            functools.partial(expert_kernel, own, experts),
            (deep // block,),
            ins,
            outs,
            scratch,
            flops=2 * slots * width * deep * (6 if own else 4),
            through=through,
            into=stacks[:count],
        )
        stacks[:count] = made_here[:count]
        return made_here[count:]

    others_grads = lax.ppermute(grads_in, "rep", swap) if replicas == 2 else None
    tails, backs = [], []

    def other(m, x, through):
        return expert_call(False, m, x, slots_of(others_grads, m), through) if replicas == 2 else through

    others_in = []
    arrived = exchange(sents[0])
    for m in range(micro):
        x = arrived
        if m + 1 < micro:
            arrived = exchange(sents[m + 1])
        if replicas == 2:
            others_in.append(lax.ppermute(x, "rep", swap))
        through = sents[m + 2 : m + 3] + backs[-1:]
        back, tail, *handed = expert_call(True, m, x, slots_of(grads_in, m), through)
        if m + 2 < micro:
            sents[m + 2] = handed.pop(0)
        if handed:
            waited = [others_grads] + others_in[:1] if m == 1 else others_in[m - 1 : m]
            backs[-1] = exchange(hold(handed.pop(0), *waited))
        backs.append(back)
        tails.append(tail)
    others_in += [None] * (micro + 1)
    handed = other(0, others_in[0], [backs[-1]])
    backs[-1] = exchange(hold(handed[0], others_in[micro - 1]))

    one_rows, packed_rows, mix_rows, low_rows = [], [], [], []
    input_grads = None
    for m in range(micro):
        one, packed, mixture, middle = saved[m]
        early = m == micro - 2
        input_grads, grad_packed, low, tail, *handed = call(
            "attend_back",
            functools.partial(backward_kernel, experts),
            (1,),
            [
                of_micro(images, m),
                of_micro(cotangent, m),
                whole(middle),
                whole(packed),
                whole(backs[m]),
                of_micro(tables, m),
                w_qkv,
                w_proj,
                whole(gains),
            ],
            [
                (images.shape, BF, (None, None, seq, width), lambda i, m=m: (m, 0, 0, 0)),
                made((seq, split), BF),
                made((seq, width), BF),
                made((width, LANES), F32),
            ],
            [pltpu.VMEM((seq, width), BF)],
            flops=8 * 10**9,
            through=[stacks[4]] if early else [],
            into=[input_grads],
        )
        if early:
            stacks[4] = handed[0]
        one_rows.append(one)
        packed_rows.append(grad_packed)
        mix_rows.append(mixture)
        low_rows.append(low)
        tails.append(tail)
    results = exchange(stacks[4].reshape(experts, micro * capacity, width)).reshape(packed_grads.shape)

    sums = call(
        "dense",
        functools.partial(dense_kernel, micro),
        (1,),
        [whole(a) for a in one_rows + packed_rows + mix_rows + low_rows + tails],
        [made(full.shape, BF)],
        flops=5 * 10**9,
    )[0]

    def total(lead, part, parts, into, through):
        steps = deep // total_block // parts
        first = part * steps
        if lead:
            left = (stacks[0], (sets, slots, total_block), lambda i: (0, 0, first + i))
            right = whole(stacks[2])
            out = ((1, deep, width), F32, (None, total_block, width), lambda i: (0, first + i, 0))
        else:
            left = whole(stacks[3])
            right = (stacks[1], (sets, slots, total_block), lambda i: (0, 0, first + i))
            out = ((1, width, deep), F32, (None, width, total_block), lambda i: (0, 0, first + i))
        return call(
            "total_out" if lead else "total_in",
            total_kernel,
            (steps,),
            [left, right],
            [out],
            flops=2 * sets * slots * width * steps * total_block,
            through=through,
            into=[into],
        )

    total_block = 512
    middles = [s[3] for s in saved]
    made_in = made_out = outputs = None

    def beside_others(m):
        return lambda kept: (other(m, others_in[m], [kept]) or [kept])[0]

    def beside_total(lead, part=0, parts=1):
        def run(kept):
            nonlocal made_in, made_out
            if lead:
                made_out, kept = total(True, part, parts, made_out, [kept])
            else:
                made_in, kept = total(False, part, parts, made_in, [kept])
            return kept

        return run

    def beside_combine(kept):
        nonlocal outputs
        outputs, kept = call(
            "combine",
            functools.partial(combine_kernel, micro),
            (1,),
            [whole(a) for a in middles + [tables, results]],
            [made(images.shape, BF)],
            flops=micro * 10**9,
            through=[kept],
        )
        return kept

    def both(*runs):
        def run(kept):
            for r in runs:
                kept = r(kept)
            return kept

        return run

    bits = experts.bit_length() - 1
    plan = [lambda kept: kept] * (bits + 1)
    plan[0] = beside_others(1)
    plan[1] = beside_total(True, 0, 2)
    plan[2] = beside_combine
    plan[3] = beside_total(True, 1, 2)
    plan[bits] = both(*[beside_others(m) for m in range(2, micro)], beside_total(False))
    sums = scatter_sums(sums, experts, replicas, plan)
    if replicas != 2:
        plan[bits](sums)
    grad_in, grad_out = made_in, made_out
    if replicas != 2:
        grad_in, grad_out = (lax.psum(g.astype(BF), "rep").astype(F32) for g in (grad_in, grad_out))
    return (
        outputs,
        input_grads,
        sums[:, :split],
        sums[:, split : split + width],
        sums[:, split + width : split + width + experts],
        sums[:, split + width + experts],
        sums[:, split + width + experts + 1],
        grad_in,
        grad_out,
    )


def solution(mesh):
    tokens = P(None, ("rep", "grp"), None, None)
    rows = P("grp", None)
    expert = P("grp", None, None)
    return jax.shard_map(
        shards,
        mesh=mesh,
        in_specs=(tokens, rows, rows, rows, P("grp"), P("grp"), expert, expert, tokens, tokens),
        out_specs=(tokens, tokens, rows, rows, rows, P("grp"), P("grp"), expert, expert),
        check_vma=False,
    )
```

```python
import functools

import jax
import jax.numpy as jnp
from jax import lax
from jax.experimental import pallas as pl
from jax.experimental.pallas import tpu as pltpu
from jax.sharding import PartitionSpec as P

HEADS = 12
EPSILON = 1e-06
BF = jnp.bfloat16
F32 = jnp.float32
LANES = 128
COST = 0.6
WAIT_FOR = ()


def dot_tn(left, right):
    return lax.dot_general(left, right, (((0,), (0,)), ((), ())), preferred_element_type=F32)


def dot_nt(left, right):
    return lax.dot_general(left, right, (((1,), (1,)), ((), ())), preferred_element_type=F32)


def dot_nn(left, right):
    return jnp.dot(left, right, preferred_element_type=F32)


def normalize(values):
    center = values - jnp.mean(values, -1, keepdims=True)
    inverse = lax.rsqrt(jnp.mean(center * center, -1, keepdims=True) + EPSILON)
    return center * inverse, inverse


def norm_backward(grad_rows, unit_rows, inverse, gain_row):
    scaled = grad_rows * gain_row
    inner = (
        scaled
        - jnp.mean(scaled, -1, keepdims=True)
        - unit_rows * jnp.mean(scaled * unit_rows, -1, keepdims=True)
    )
    return inner * inverse


def call(name, body, grid, ins, outs, scratch=(), flops=0, vmem=56, through=(), into=(), after=()):
    buffers = [(i, array) for i, array in enumerate(into) if array is not None]
    kept = list(through) + [array for _, array in buffers] + list(after)
    count, made_count = len(ins), len(outs)
    aliases = {count + i: made_count + i for i in range(len(through))}
    for place, (i, _) in enumerate(buffers):
        aliases[count + len(through) + place] = i

    def inner(*refs):
        rest = refs[count + len(kept) :]
        body(*refs[:count], *rest[:made_count], *rest[made_count + len(through) :])

    anywhere = pl.BlockSpec(memory_space=pltpu.HBM)
    return pl.pallas_call(
        inner if kept else body,
        grid=grid,
        in_specs=[pl.BlockSpec(block, index) for _, block, index in ins] + [anywhere] * len(kept),
        out_specs=[pl.BlockSpec(block, index) for _, _, block, index in outs] + [anywhere] * len(through),
        out_shape=[jax.ShapeDtypeStruct(shape, dtype) for shape, dtype, _, _ in outs]
        + [jax.ShapeDtypeStruct(array.shape, array.dtype) for array in through],
        scratch_shapes=list(scratch),
        input_output_aliases=aliases,
        compiler_params=pltpu.CompilerParams(vmem_limit_bytes=vmem * 2**20),
        cost_estimate=pl.CostEstimate(flops=int(flops * COST), bytes_accessed=0, transcendentals=0),
        name=name,
    )(*[array for array, _, _ in ins], *kept)


def whole(array):
    return (array, array.shape, lambda i: (0,) * array.ndim)


def made(shape, dtype):
    return (shape, dtype, shape, lambda i: (0,) * len(shape))


def of_micro(array, m):
    lead = array.ndim - 2
    return (array, (None,) * lead + array.shape[-2:], lambda i: (m,) + (0,) * (array.ndim - 1))


def head_mask(width):
    return lax.broadcasted_iota(jnp.int32, (1, LANES), 1) // (width // HEADS)


def softmax(scores):
    top = jnp.exp(scores - jnp.max(scores, -1, keepdims=True))
    return top * (1.0 / jnp.sum(top, -1, keepdims=True))


def hold_kernel(out):
    out[...] = jnp.zeros_like(out)


def hold(array, *waited):
    after = [corner(w) for w in waited if w is not None]
    if not after:
        return array
    return call("hold", hold_kernel, (1,), [], [made((8, LANES), F32)], through=[array], after=after)[1]


def gather_kernel(table, rows, out):
    out[...] = dot_nn(table[...], rows[...]).astype(BF).reshape(out.shape)


def forward_kernel(image, table, grad_y, w_qkv, w_proj, gains, one_o, packed_o, mix_o, middle_o, slots_o):
    width = image.shape[1]
    states = image[...].astype(F32)
    unit, _ = normalize(states)
    one = (unit * gains[0:1]).astype(BF)
    one_o[...] = one
    packed_o[...] = dot_nn(one, w_qkv[...]).astype(BF)
    head = head_mask(width)
    per = LANES * HEADS // width
    factor = (width // HEADS) ** (-0.5)
    for low in range(0, width, LANES):
        query = packed_o[:, low : low + LANES]
        keys = packed_o[:, width + low : width + low + LANES]
        values = packed_o[:, 2 * width + low : 2 * width + low + LANES]
        mixed = 0.0
        for h in range(per):
            mine = (head == h).astype(BF)
            weights = softmax(dot_nt(query * mine, keys) * factor).astype(BF)
            mixed = mixed + dot_nn(weights, values * mine)
        mix_o[:, low : low + LANES] = mixed.astype(BF)
    middle = states + dot_nn(mix_o[...], w_proj[...])
    middle_o[...] = middle
    unit, _ = normalize(middle)
    two = (unit * gains[1:2]).astype(BF)
    block = slots_o.shape[:1] + slots_o.shape[2:]
    for at, rows in enumerate((two, grad_y[...])[: slots_o.shape[1]]):
        slots_o[:, at] = dot_nn(table[...], rows).astype(BF).reshape(block)


def assemble_kernel(place, *refs):
    rows = refs[0].shape[0]
    for r, piece in enumerate(refs[:-1]):
        refs[-1][pl.ds(pl.multiple_of((place[0] ^ r) * rows, 16), rows), :] = piece[...]


def backward_kernel(
    column, image, grad_y, middle, packed, backs, table, w_qkv, w_proj, gains, grad_image_o, grad_packed_o, low_o, tail_o, mixture_s
):
    width = image.shape[1]
    backs = backs[...]
    grad_two = dot_tn(table[...], backs.reshape(-1, width))
    unit, inverse = normalize(middle[...])
    gain_two = grad_two * unit
    grad_middle = grad_y[...].astype(F32) + norm_backward(grad_two, unit, inverse, gains[1:2])
    low_o[...] = grad_middle.astype(BF)
    mixture_s[...] = dot_nt(low_o[...], w_proj[...]).astype(BF)
    head = head_mask(width)
    per = LANES * HEADS // width
    factor = (width // HEADS) ** (-0.5)
    for low in range(0, width, LANES):
        query = packed[:, low : low + LANES]
        keys = packed[:, width + low : width + low + LANES]
        values = packed[:, 2 * width + low : 2 * width + low + LANES]
        grad_mixed = mixture_s[:, low : low + LANES]
        grad_query = grad_keys = grad_values = 0.0
        for h in range(per):
            mine = (head == h).astype(BF)
            query_h, keys_h, grad_h = query * mine, keys * mine, grad_mixed * mine
            weights = softmax(dot_nt(query_h, keys) * factor)
            grad_values = grad_values + dot_tn(weights.astype(BF), grad_h)
            grad_weights = dot_nt(grad_h, values)
            inner = jnp.sum(grad_weights * weights, -1, keepdims=True)
            grad_scores = (weights * (grad_weights - inner)).astype(BF)
            grad_query = grad_query + dot_nn(grad_scores, keys_h)
            grad_keys = grad_keys + dot_tn(grad_scores, query_h)
        grad_packed_o[:, low : low + LANES] = (grad_query * factor).astype(BF)
        grad_packed_o[:, width + low : width + low + LANES] = (grad_keys * factor).astype(BF)
        grad_packed_o[:, 2 * width + low : 2 * width + low + LANES] = grad_values.astype(BF)
    grad_one = dot_nt(grad_packed_o[...], w_qkv[...])
    unit, inverse = normalize(image[...].astype(F32))
    gain_one = grad_one * unit
    grad_image_o[...] = (grad_middle + norm_backward(grad_one, unit, inverse, gains[0:1])).astype(BF)
    lane = lax.broadcasted_iota(jnp.int32, (image.shape[0], LANES), 1)
    tail = 0.0
    for at, gain in ((column, gain_one), (column + 1, gain_two)):
        ones = (lane == at).astype(BF)
        high = gain.astype(BF)
        tail = tail + dot_tn(high, ones) + dot_tn((gain - high.astype(F32)).astype(BF), ones)
    tail_o[...] = tail


def expert_kernel(own, experts, slots_in, grad_in, here, router, w_in, w_out, active_o, hidden_o, result_o, rows_o, *rest):
    step = pl.program_id(0)
    if own:
        sent_o, back_o, tail_o, probs_s, result_s, back_s = rest
    width = slots_in.shape[-1]
    rows = slots_in[...].reshape(-1, width)

    @pl.when(step == 0)
    def _():
        rows_o[...] = rows
        logits = dot_nn(rows, router[...])
        lane = lax.broadcasted_iota(jnp.int32, logits.shape, 1)
        probs = softmax(jnp.where(lane < experts, logits, -1e30))
        gate = jnp.sum(probs * here[...], -1, keepdims=True)
        result_o[...] = (gate * grad_in[...].reshape(-1, width).astype(F32)).astype(BF)
        if own:
            probs_s[...] = probs
            result_s[...] = jnp.zeros_like(result_s)
            back_s[...] = jnp.zeros_like(back_s)

    hidden = dot_nn(rows, w_in[...])
    grad_active = dot_nt(result_o[...], w_out[...])
    cumulative = 0.5 + 0.5 * lax.erf(hidden * (0.5**0.5))
    active = (hidden * cumulative).astype(BF)
    slope = cumulative + hidden * jnp.exp(-0.5 * hidden * hidden) * 0.3989422804014327
    grad_hidden = (grad_active * slope).astype(BF)
    active_o[...] = active
    hidden_o[...] = grad_hidden
    if own:
        result_s[...] += dot_nn(active, w_out[...])
        back_s[...] += dot_nt(grad_hidden, w_in[...])

        @pl.when(step == pl.num_programs(0) - 1)
        def _():
            probs = probs_s[...]
            gate = jnp.sum(probs * here[...], -1, keepdims=True)
            result = result_s[...]
            grad_gate = jnp.sum(grad_in[...].reshape(-1, width).astype(F32) * result, -1, keepdims=True)
            grad_logit = (grad_gate * gate * (here[...] - probs)).astype(BF)
            back_o[...] = (back_s[...] + dot_nt(grad_logit, router[...])).astype(BF).reshape(back_o.shape)
            sent_o[...] = (gate * result).astype(BF).reshape(sent_o.shape)
            tail_o[...] = dot_tn(rows, grad_logit)


def total_kernel(left, right, *refs):
    total = dot_tn(left[...].reshape(-1, left.shape[-1]), right[...].reshape(-1, right.shape[-1]))
    refs[-1][...] = total if len(refs) == 1 else refs[0][...] + total


def dense_kernel(micro, *refs):
    ones, packs, mixes, lows = (refs[i * micro : (i + 1) * micro] for i in range(4))
    tails, out = refs[4 * micro : 6 * micro], refs[-1]
    width = ones[0].shape[-1]
    for j in range(3):
        part = slice(j * width, (j + 1) * width)
        out[:, part] = sum(dot_tn(a[...], b[:, part]) for a, b in zip(ones, packs)).astype(BF)
    out[:, 3 * width : 4 * width] = sum(dot_tn(a[...], b[...]) for a, b in zip(mixes, lows)).astype(BF)
    out[:, 4 * width :] = sum(t[...] for t in tails).astype(BF)


def combine_kernel(micro, *refs):
    middles, (tables, results, out) = refs[:micro], refs[micro:]
    for m, middle in enumerate(middles):
        rows = results[:, m].reshape(-1, middle.shape[-1])
        out[m, 0] = (middle[...] + dot_tn(tables[m], rows)).astype(BF)


def slot_tables(routes, experts, capacity):
    rows = routes.shape[1]
    ordering = jnp.concatenate([routes[:, :, 0], routes[:, :, 1]], 1)
    onehot = (ordering[:, :, None] == jnp.arange(experts, dtype=jnp.int32)).astype(BF)
    count = 2 * rows
    earlier = (jnp.arange(count)[:, None] > jnp.arange(count)[None, :]).astype(BF)
    before = jnp.einsum("ab,mbe->mae", earlier, onehot, preferred_element_type=F32)
    rank = jnp.sum(before * onehot, -1).astype(jnp.int32)
    target = jnp.where(rank < capacity, ordering * capacity + rank, -1)
    slots = jnp.arange(experts * capacity, dtype=jnp.int32)[None, :, None]
    first, second = target[:, None, :rows], target[:, None, rows:]
    return ((slots == first) | (slots == second)).astype(BF)


def exchange(blocks):
    merged = blocks.reshape(blocks.shape[0], -1, blocks.shape[-1])
    return lax.all_to_all(merged, "grp", split_axis=0, concat_axis=0, tiled=True).reshape(blocks.shape)


def add_low(left, right):
    return (left.astype(F32) + right.astype(F32)).astype(BF)


def corner(array):
    return array[(0,) * (array.ndim - 2)][:16, :LANES]


def scatter_sums(sums, experts, replicas, beside):
    bits = experts.bit_length() - 1
    place = lax.axis_index("grp")
    own_rep = lax.axis_index("rep")
    rows, columns = sums.shape[0] // experts, sums.shape[1] - LANES
    half = columns // 2
    swap = [(0, 1), (1, 0)]
    sums = sums.reshape((2,) * bits + (rows, sums.shape[1]))

    def halve(array, bit, run=lambda kept: kept):
        mine, axis = (place >> bit) & 1, bits - 1 - bit
        sent = lax.dynamic_index_in_dim(array, 1 - mine, axis, keepdims=False)
        kept = lax.dynamic_index_in_dim(array, mine, axis, keepdims=False)
        came = lax.ppermute(sent, "grp", [(g, g ^ (1 << bit)) for g in range(experts)])
        return add_low(run(kept), came)

    def halve_columns(array, shared, run=lambda kept: kept):
        if replicas != 2:
            return run(array)
        cut = (array.shape[-1] - shared) // 2
        parts = [array[..., :cut], array[..., cut : 2 * cut]]
        mine, other = (jnp.where(own_rep == 0, parts[i], parts[1 - i]) for i in (0, 1))
        if shared:
            mine, other = (jnp.concatenate([p, array[..., 2 * cut :]], -1) for p in (mine, other))
        return add_low(run(mine), lax.ppermute(other, "rep", swap))

    sums = halve(sums, 0, beside[0])
    left = jnp.concatenate([sums[..., :half], sums[..., columns:]], -1)
    right = sums[..., half:columns]
    left, right = halve_columns(left, LANES, beside[1]), halve(right, 1)
    left, right = halve(left, 1, beside[2]), halve_columns(right, 0)
    cut = right.shape[-1]
    sums = jnp.concatenate([left[..., :cut], right, left[..., cut:]], -1)
    for bit in range(2, bits):
        sums = halve(sums, bit, beside[min(bit + 1, 4)] if bit < 4 else lambda kept: kept)
    if replicas != 2:
        return lax.psum(sums, "rep").astype(F32)
    mine = sums[:, : 2 * cut]
    other = lax.ppermute(mine, "rep", swap)
    low, high = (jnp.where(own_rep == i, mine, other) for i in (0, 1))
    pieces = [low[:, :cut], high[:, :cut], low[:, cut:], high[:, cut:], sums[:, 2 * cut :]]
    return jnp.concatenate(pieces, 1).astype(F32)


def gather_rows(piece, experts):
    if piece.shape[0] % 16 or experts & (experts - 1):
        return lax.all_gather(piece, "grp", axis=0, tiled=True), []

    def send(array, k):
        return lax.ppermute(array, "grp", [(g, g ^ k) for g in range(experts)])

    pieces = {0: piece}
    for k in range(4, experts, 4):
        pieces[k] = send(piece, k)
    for bit in (2, 1):
        for k in list(pieces):
            pieces[k ^ bit] = send(pieces[k], bit)
    high = [pieces[k] for k in WAIT_FOR]
    rows, columns = piece.shape
    place = lax.axis_index("grp").astype(jnp.int32).reshape(1)
    whole_piece = pl.BlockSpec((rows, columns), lambda i, p: (0, 0))
    full = pl.pallas_call(
        assemble_kernel,
        grid_spec=pltpu.PrefetchScalarGridSpec(
            num_scalar_prefetch=1,
            grid=(1,),
            in_specs=[whole_piece] * experts,
            out_specs=pl.BlockSpec((experts * rows, columns), lambda i, p: (0, 0)),
        ),
        out_shape=jax.ShapeDtypeStruct((experts * rows, columns), piece.dtype),
        compiler_params=pltpu.CompilerParams(vmem_limit_bytes=24 * 2**20),
        name="assemble",
    )(place, *[pieces[r] for r in range(experts)])
    return full, high


def shards(images, attn_qkv, attn_proj, router, gain_attn, gain_moe, expert_in, expert_out, routes, cotangent):
    experts = lax.axis_size("grp")
    replicas = lax.axis_size("rep")
    mine = lax.axis_index("grp")
    micro, _, seq, width = images.shape
    capacity = max(2, 8 * seq * images.shape[1] // (3 * experts))
    slots = experts * capacity
    split = attn_qkv.shape[1]
    deep = expert_in.shape[2]
    here = (lax.broadcasted_iota(jnp.int32, (1, LANES), 1) == mine).astype(F32)

    tables = slot_tables(routes.reshape(micro, seq, 2), experts, capacity)

    small = jnp.concatenate([router, gain_attn[:, None], gain_moe[:, None]], 1)
    small = jnp.pad(small, ((0, 0), (0, LANES - small.shape[1])))
    full, first_pieces = gather_rows(jnp.concatenate([attn_qkv, attn_proj, small], 1), experts)
    gains = full[:, split + width + experts : split + width + experts + 2].T.astype(F32)
    w_qkv = (full, (width, split), lambda i: (0, 0))
    w_proj = (full, (width, width), lambda i: (0, split // width))
    w_router = (full, (width, LANES), lambda i: (0, (split + width) // LANES))

    one_block = (experts, 1, capacity, width)
    first_grads = call(
        "pack",
        gather_kernel,
        (1,),
        [of_micro(tables, 0), of_micro(cotangent, 0)],
        [made(one_block, BF)],
        flops=2 * slots * seq * width,
    )[0]
    first_grads = exchange(hold(first_grads, *first_pieces))

    saved, sents = [], []
    for m in range(micro):
        one, packed, mixture, middle, sent, *handed = call(
            "attend",
            forward_kernel,
            (1,),
            [
                of_micro(images, m),
                of_micro(tables, m),
                of_micro(cotangent, m),
                w_qkv,
                w_proj,
                whole(gains),
            ],
            [
                made((seq, width), BF),
                made((seq, split), BF),
                made((seq, width), BF),
                made((seq, width), F32),
                made((experts, min(2, m + 1), capacity, width), BF),
            ],
            flops=6 * 10**9,
            through=sents[1:],
        )
        sents[1:] = handed
        sents.append(sent)
        saved.append((one, packed, mixture, middle))

    block = 1024
    swap = [(0, 1), (1, 0)]
    order = [(True, 0), (False, 0), (True, 1), (True, 2), (False, 1), (False, 2)]
    if replicas != 2:
        order = [pair for pair in order if pair[0]]
    sets, groups = len(order), replicas if replicas == 2 else 1
    stacks = [None] * 6

    def part_of(array, at):
        return (array, (experts, None, capacity, width), lambda i: (0, at, 0, 0))

    def expert_call(own, m, arrays, through):
        place = order.index((own, m))
        ins = [
            part_of(*arrays[0]),
            part_of(*arrays[1]),
            whole(here),
            w_router,
            (expert_in, (None, width, block), lambda i: (0, 0, i)),
            (expert_out, (None, block, width), lambda i: (0, i, 0)),
        ]
        outs = [
            ((sets, slots, deep), BF, (None, slots, block), lambda i: (place, 0, i)),
            ((sets, slots, deep), BF, (None, slots, block), lambda i: (place, 0, i)),
            ((sets, slots, width), BF, (None, slots, width), lambda i: (place, 0, 0)),
            ((sets, slots, width), BF, (None, slots, width), lambda i: (place, 0, 0)),
        ]
        scratch = []
        if own:
            last = m == micro - 1
            outs += [
                ((experts, micro, capacity, width), BF, (experts, None, capacity, width), lambda i: (0, m, 0, 0)),
                (one_block, BF, (experts, None, capacity, width), lambda i: (0, 0, 0, 0))
                if last
                else ((experts, micro - 1, capacity, width), BF, (experts, None, capacity, width), lambda i: (0, m, 0, 0)),
                made((width, LANES), F32),
            ]
            scratch = [pltpu.VMEM((slots, LANES), F32)] + [pltpu.VMEM((slots, width), F32)] * 2
        count = (5 if last else 6) if own else 4
        made_here = call(
            "expert_own" if own else "expert_other",
            functools.partial(expert_kernel, own, experts),
            (deep // block,),
            ins,
            outs,
            scratch,
            flops=2 * slots * width * deep * (6 if own else 4),
            vmem=56,
            through=through,
            into=stacks[:count],
        )
        stacks[:count] = made_here[:count]
        return made_here[count:]

    def total(lead, early, before, into, through, part=0, parts=1):
        steps = deep // total_block // parts
        first = part * steps
        half = sets // groups
        at = 0 if early else groups - 1
        if lead:
            left = (stacks[0], (half, slots, total_block), lambda i: (at, 0, first + i))
            right = (stacks[2], (half, slots, width), lambda i: (at, 0, 0))
            out = ((1, deep, width), F32, (None, total_block, width), lambda i: (0, first + i, 0))
        else:
            left = (stacks[3], (half, slots, width), lambda i: (at, 0, 0))
            right = (stacks[1], (half, slots, total_block), lambda i: (at, 0, first + i))
            out = ((1, width, deep), F32, (None, width, total_block), lambda i: (0, 0, first + i))
        return call(
            "total_out" if lead else "total_in",
            total_kernel,
            (steps,),
            [left, right] + ([] if before is None else [(before,) + out[2:]]),
            [out],
            flops=2 * half * slots * width * steps * total_block,
            vmem=56,
            through=through,
            into=[into],
        )

    total_block = 512

    def swapped(array):
        return lax.ppermute(array, "rep", swap) if replicas == 2 else None


    def other(m, through):
        return expert_call(False, m, theirs[m], through) if replicas == 2 else through

    def waited(m):
        return [array for array, _ in theirs[m]] if replicas == 2 else []

    arrived = exchange(sents[0])
    ours = [((arrived, 0), (first_grads, 0))]
    theirs = [((swapped(arrived), 0), (swapped(first_grads), 0))]
    tails = []
    for m in range(1, micro):
        arrived = exchange(hold(sents[m], *[theirs[0][1][0]][: 2 - m]))
        tail, *handed = expert_call(True, m - 1, ours[m - 1], sents[m + 1 : m + 2] if m > 1 else [])
        tails.append(tail)
        if m == 1:
            handed = other(0, sents[2:3])
        sents[m + 1 : m + 2] = handed
        came = arrived.reshape(sents[1].shape)
        ours.append(((came, 0), (came, 1)))
        came = swapped(came)
        theirs.append(((came, 0), (came, 1)))
    early_in = early_out = None
    if groups == 2:
        early_in, stacks[5] = total(False, True, None, None, [stacks[5]])
    backs = exchange(hold(stacks[5], *waited(1)[:1]))
    last_back, tail = expert_call(True, micro - 1, ours[-1], [])
    tails.append(tail)
    [last_back] = other(1, [last_back])
    if groups == 2:
        early_out, last_back = total(True, True, None, None, [last_back])
    last_back = exchange(hold(last_back, *waited(micro - 1)[:1]))

    one_rows, packed_rows, mix_rows, low_rows = [], [], [], []
    input_grads = None
    for m in range(micro):
        one, packed, mixture, middle = saved[m]
        early = m == micro - 2
        input_grads, grad_packed, low, tail, *handed = call(
            "attend_back",
            functools.partial(backward_kernel, experts),
            (1,),
            [
                of_micro(images, m),
                of_micro(cotangent, m),
                whole(middle),
                whole(packed),
                part_of(last_back, 0) if m == micro - 1 else part_of(backs, m),
                of_micro(tables, m),
                w_qkv,
                w_proj,
                whole(gains),
            ],
            [
                (images.shape, BF, (None, None, seq, width), lambda i, m=m: (m, 0, 0, 0)),
                made((seq, split), BF),
                made((seq, width), BF),
                made((width, LANES), F32),
            ],
            [pltpu.VMEM((seq, width), BF)],
            flops=8 * 10**9,
            through=[stacks[4]] if early else [],
            into=[input_grads],
        )
        if early:
            stacks[4] = handed[0]
        one_rows.append(one)
        packed_rows.append(grad_packed)
        mix_rows.append(mixture)
        low_rows.append(low)
        tails.append(tail)
    results = exchange(stacks[4])

    sums = call(
        "dense",
        functools.partial(dense_kernel, micro),
        (1,),
        [whole(a) for a in one_rows + packed_rows + mix_rows + low_rows + tails],
        [made(full.shape, BF)],
        vmem=24,
            flops=5 * 10**9,
    )[0]

    middles = [s[3] for s in saved]
    made_in = made_out = outputs = None

    def beside_others(m):
        return lambda kept: other(m, [kept])[0]

    def beside_total(lead, part=0, parts=1):
        def run(kept):
            nonlocal made_in, made_out
            if lead:
                made_out, kept = total(True, False, early_out, made_out, [kept], part, parts)
            else:
                made_in, kept = total(False, False, early_in, made_in, [kept], part, parts)
            return kept

        return run

    def beside_combine(kept):
        nonlocal outputs
        outputs, kept = call(
            "combine",
            functools.partial(combine_kernel, micro),
            (1,),
            [whole(a) for a in middles + [tables, results]],
            [made(images.shape, BF)],
            flops=micro * 10**9,
            through=[kept],
        )
        return kept

    def both(*runs):
        def run(kept):
            for r in runs:
                kept = r(kept)
            return kept

        return run

    sums = scatter_sums(
        sums,
        experts,
        replicas,
        [
            beside_others(2),
            beside_total(False),
            beside_total(True, 0, 2),
            beside_total(True, 1, 2),
            beside_combine,
        ],
    )
    grad_in, grad_out = made_in, made_out
    if replicas != 2:
        grad_in, grad_out = (lax.psum(g.astype(BF), "rep").astype(F32) for g in (grad_in, grad_out))
    return (
        outputs,
        input_grads,
        sums[:, :split],
        sums[:, split : split + width],
        sums[:, split + width : split + width + experts],
        sums[:, split + width + experts],
        sums[:, split + width + experts + 1],
        grad_in,
        grad_out,
    )


def solution(mesh):
    tokens = P(None, ("rep", "grp"), None, None)
    rows = P("grp", None)
    expert = P("grp", None, None)
    return jax.shard_map(
        shards,
        mesh=mesh,
        in_specs=(tokens, rows, rows, rows, P("grp"), P("grp"), expert, expert, tokens, tokens),
        out_specs=(tokens, tokens, rows, rows, rows, P("grp"), P("grp"), expert, expert),
        check_vma=False,
    )
```

```python
import functools

import jax
import jax.numpy as jnp
from jax import lax
from jax.experimental import pallas as pl
from jax.experimental.pallas import tpu as pltpu
from jax.sharding import PartitionSpec as P

HEADS = 12
EPSILON = 1e-06
BF = jnp.bfloat16
F32 = jnp.float32
LANES = 128
COST = 0.6


def dot_tn(left, right):
    return lax.dot_general(left, right, (((0,), (0,)), ((), ())), preferred_element_type=F32)


def dot_nt(left, right):
    return lax.dot_general(left, right, (((1,), (1,)), ((), ())), preferred_element_type=F32)


def dot_nn(left, right):
    return jnp.dot(left, right, preferred_element_type=F32)


def normalize(values):
    center = values - jnp.mean(values, -1, keepdims=True)
    inverse = lax.rsqrt(jnp.mean(center * center, -1, keepdims=True) + EPSILON)
    return center * inverse, inverse


def norm_backward(grad_rows, unit_rows, inverse, gain_row):
    scaled = grad_rows * gain_row
    inner = (
        scaled
        - jnp.mean(scaled, -1, keepdims=True)
        - unit_rows * jnp.mean(scaled * unit_rows, -1, keepdims=True)
    )
    return inner * inverse


def call(name, body, grid, ins, outs, scratch=(), flops=0, vmem=56, through=(), into=(), after=()):
    buffers = [(i, array) for i, array in enumerate(into) if array is not None]
    kept = list(through) + [array for _, array in buffers] + list(after)
    count, made_count = len(ins), len(outs)
    aliases = {count + i: made_count + i for i in range(len(through))}
    for place, (i, _) in enumerate(buffers):
        aliases[count + len(through) + place] = i

    def inner(*refs):
        rest = refs[count + len(kept) :]
        body(*refs[:count], *rest[:made_count], *rest[made_count + len(through) :])

    anywhere = pl.BlockSpec(memory_space=pltpu.HBM)
    return pl.pallas_call(
        inner if kept else body,
        grid=grid,
        in_specs=[
            pl.BlockSpec(memory_space=pltpu.SMEM) if block is None else pl.BlockSpec(block, index)
            for _, block, index in ins
        ]
        + [anywhere] * len(kept),
        out_specs=[pl.BlockSpec(block, index) for _, _, block, index in outs] + [anywhere] * len(through),
        out_shape=[jax.ShapeDtypeStruct(shape, dtype) for shape, dtype, _, _ in outs]
        + [jax.ShapeDtypeStruct(array.shape, array.dtype) for array in through],
        scratch_shapes=list(scratch),
        input_output_aliases=aliases,
        compiler_params=pltpu.CompilerParams(vmem_limit_bytes=vmem * 2**20),
        cost_estimate=pl.CostEstimate(flops=int(flops * COST), bytes_accessed=0, transcendentals=0),
        name=name,
    )(*[array for array, _, _ in ins], *kept)


def whole(array):
    return (array, array.shape, lambda i: (0,) * array.ndim)


def made(shape, dtype):
    return (shape, dtype, shape, lambda i: (0,) * len(shape))


def of_micro(array, m):
    lead = array.ndim - 2
    return (array, (None,) * lead + array.shape[-2:], lambda i: (m,) + (0,) * (array.ndim - 1))


def head_mask(width):
    return lax.broadcasted_iota(jnp.int32, (1, LANES), 1) // (width // HEADS)


def softmax(scores):
    top = jnp.exp(scores - jnp.max(scores, -1, keepdims=True))
    return top * (1.0 / jnp.sum(top, -1, keepdims=True))


def hold_kernel(out):
    out[...] = jnp.zeros_like(out)


def hold(array, *waited):
    if not waited:
        return array
    after = [corner(w) for w in waited]
    return call("hold", hold_kernel, (1,), [], [made((8, LANES), F32)], through=[array], after=after)[1]


def gather_kernel(table, rows, out):
    out[...] = dot_nn(table[...], rows[...]).astype(BF).reshape(out.shape)


def gain_rows(small, experts):
    return small[...].astype(F32).T[experts : experts + 2]


def forward_kernel(split, experts, image, table, grad_y, *refs):
    w_qkv, w_proj, small, *outs = refs
    one_o, packed_o, mix_o, middle_o, slots_o = outs
    gains = gain_rows(small, experts)
    width = image.shape[1]
    states = image[...].astype(F32)
    unit, _ = normalize(states)
    one = (unit * gains[0:1]).astype(BF)
    one_o[...] = one
    packed_o[...] = dot_nn(one, w_qkv[...]).astype(BF)
    head = head_mask(width)
    per = LANES * HEADS // width
    factor = (width // HEADS) ** (-0.5)
    for low in range(0, width, LANES):
        query = packed_o[:, low : low + LANES]
        keys = packed_o[:, width + low : width + low + LANES]
        values = packed_o[:, 2 * width + low : 2 * width + low + LANES]
        mixed = 0.0
        for h in range(per):
            mine = (head == h).astype(BF)
            weights = softmax(dot_nt(query * mine, keys) * factor).astype(BF)
            mixed = mixed + dot_nn(weights, values * mine)
        mix_o[:, low : low + LANES] = mixed.astype(BF)
    middle = states + dot_nn(mix_o[...], w_proj[...])
    middle_o[...] = middle
    unit, _ = normalize(middle)
    two = (unit * gains[1:2]).astype(BF)
    block = slots_o.shape[:1] + slots_o.shape[2:]
    for at, rows in enumerate((two, grad_y[...])[: slots_o.shape[1]]):
        slots_o[:, at] = dot_nn(table[...], rows).astype(BF).reshape(block)


def assemble_kernel(differ, place, *refs):
    *pieces, full = refs
    rows = pieces[0].shape[0]
    for piece, (first, other) in zip(pieces, differ):
        at = place[0] ^ jnp.where(place[1] == 0, first, other)
        full[pl.ds(pl.multiple_of(at * rows, 16), rows), :] = piece[...]


def backward_kernel(
    column, last, image, grad_y, middle, packed, backs, table, w_qkv, w_proj, small, tail_in, *refs
):
    if last:
        place, ones, mixes, packs, lows, grad_image_o, kept_o, sent_o = refs[:8]
        mixture_s, grad_packed_o, low_o, sums = refs[8:]
    else:
        grad_image_o, grad_packed_o, low_o, tail_o, mixture_s = refs
    width = image.shape[1]
    backs = backs[...]
    gains = gain_rows(small, column)
    grad_two = dot_tn(table[...], backs.reshape(-1, width))
    unit, inverse = normalize(middle[...])
    gain_two = grad_two * unit
    grad_middle = grad_y[...].astype(F32) + norm_backward(grad_two, unit, inverse, gains[1:2])
    low_o[...] = grad_middle.astype(BF)
    mixture_s[...] = dot_nt(low_o[...], w_proj[...]).astype(BF)
    head = head_mask(width)
    per = LANES * HEADS // width
    factor = (width // HEADS) ** (-0.5)
    for low in range(0, width, LANES):
        query = packed[:, low : low + LANES]
        keys = packed[:, width + low : width + low + LANES]
        values = packed[:, 2 * width + low : 2 * width + low + LANES]
        grad_mixed = mixture_s[:, low : low + LANES]
        grad_query = grad_keys = grad_values = 0.0
        for h in range(per):
            mine = (head == h).astype(BF)
            query_h, keys_h, grad_h = query * mine, keys * mine, grad_mixed * mine
            weights = softmax(dot_nt(query_h, keys) * factor)
            grad_values = grad_values + dot_tn(weights.astype(BF), grad_h)
            grad_weights = dot_nt(grad_h, values)
            inner = jnp.sum(grad_weights * weights, -1, keepdims=True)
            grad_scores = (weights * (grad_weights - inner)).astype(BF)
            grad_query = grad_query + dot_nn(grad_scores, keys_h)
            grad_keys = grad_keys + dot_tn(grad_scores, query_h)
        grad_packed_o[:, low : low + LANES] = (grad_query * factor).astype(BF)
        grad_packed_o[:, width + low : width + low + LANES] = (grad_keys * factor).astype(BF)
        grad_packed_o[:, 2 * width + low : 2 * width + low + LANES] = grad_values.astype(BF)
    grad_one = dot_nt(grad_packed_o[...], w_qkv[...])
    unit, inverse = normalize(image[...].astype(F32))
    gain_one = grad_one * unit
    grad_image_o[...] = (grad_middle + norm_backward(grad_one, unit, inverse, gains[0:1])).astype(BF)
    lane = lax.broadcasted_iota(jnp.int32, (image.shape[0], LANES), 1)
    tail = 0.0
    for at, gain in ((column, gain_one), (column + 1, gain_two)):
        column_of = (lane == at).astype(BF)
        high = gain.astype(BF)
        tail = tail + dot_tn(high, column_of) + dot_tn((gain - high.astype(F32)).astype(BF), column_of)
    if last:
        sums[:, 4 * width :] = (tail_in[...] + tail).astype(sums.dtype)
        dense_sums(place, (ones, mixes), (packs, lows), (grad_packed_o, low_o), sums, kept_o, sent_o)
    else:
        first = pl.program_id(0) == 0

        @pl.when(first)
        def _():
            tail_o[...] = tail_in[...] + tail

        @pl.when(jnp.logical_not(first))
        def _():
            tail_o[...] += tail


def expert_kernel(own, experts, slots_in, grad_in, here, router, w_in, w_out, *refs):
    tail_in, *refs = refs if own == "later" else (None, *refs)
    active_o, hidden_o, result_o, rows_o, *rest = refs
    step = pl.program_id(0)
    if own:
        sent_o, back_o, tail_o, probs_s, result_s, back_s = rest
    width = slots_in.shape[-1]
    rows = slots_in[...].reshape(-1, width)

    @pl.when(step == 0)
    def _():
        rows_o[...] = rows
        logits = dot_nn(rows, router[...])
        lane = lax.broadcasted_iota(jnp.int32, logits.shape, 1)
        probs = softmax(jnp.where(lane < experts, logits, -1e30))
        gate = jnp.sum(probs * here[...], -1, keepdims=True)
        result_o[...] = (gate * grad_in[...].reshape(-1, width).astype(F32)).astype(BF)
        if own:
            probs_s[...] = probs
            result_s[...] = jnp.zeros_like(result_s)
            back_s[...] = jnp.zeros_like(back_s)

    hidden = dot_nn(rows, w_in[...])
    grad_active = dot_nt(result_o[...], w_out[...])
    cumulative = 0.5 + 0.5 * lax.erf(hidden * (0.5**0.5))
    active = (hidden * cumulative).astype(BF)
    slope = cumulative + hidden * jnp.exp(-0.5 * hidden * hidden) * 0.3989422804014327
    grad_hidden = (grad_active * slope).astype(BF)
    active_o[...] = active
    hidden_o[...] = grad_hidden
    if own:
        result_s[...] += dot_nn(active, w_out[...])
        back_s[...] += dot_nt(grad_hidden, w_in[...])

        @pl.when(step == pl.num_programs(0) - 1)
        def _():
            probs = probs_s[...]
            gate = jnp.sum(probs * here[...], -1, keepdims=True)
            result = result_s[...]
            grad_gate = jnp.sum(grad_in[...].reshape(-1, width).astype(F32) * result, -1, keepdims=True)
            grad_logit = (grad_gate * gate * (here[...] - probs)).astype(BF)
            back_o[...] = (back_s[...] + dot_nt(grad_logit, router[...])).astype(BF).reshape(back_o.shape)
            sent_o[...] = (gate * result).astype(BF).reshape(sent_o.shape)
            tail = dot_tn(rows, grad_logit)
            tail_o[...] = tail if tail_in is None else tail_in[...] + tail


def total_kernel(left, right, *refs):
    total = dot_tn(left[...].reshape(-1, left.shape[-1]), right[...].reshape(-1, right.shape[-1]))
    refs[-1][...] = total if len(refs) == 1 else refs[0][...] + total


def dense_sums(place, lefts, rights, last, sums, kept_o, sent_o):
    width = lefts[0].shape[-1]

    def total(which, part):
        left, right = lefts[which], rights[which]
        result = dot_tn(left[left.shape[0] - 1], last[which][:, part])
        for i in range(right.shape[0]):
            result = result + dot_tn(left[i], right[i, :, part])
        return result.astype(sums.dtype)

    for j in range(3):
        part = slice(j * width, (j + 1) * width)
        sums[:, part] = total(0, part)
    sums[:, 3 * width : 4 * width] = total(1, slice(None))
    half, rows = kept_o.shape[:2]
    bit = place[0] & 1
    for j in range(half):
        for out, at in ((kept_o, 2 * j + bit), (sent_o, 2 * j + 1 - bit)):
            out[j] = sums[pl.ds(pl.multiple_of(at * rows, rows), rows), :].astype(BF)


def combine_kernel(middle, tables, results, out):
    for m in range(middle.shape[0]):
        rows = results[:, m].reshape(-1, middle.shape[-1])
        out[m, 0] = (middle[m] + dot_tn(tables[m], rows)).astype(BF)


def slot_tables(routes, experts, capacity):
    rows = routes.shape[1]
    ordering = jnp.concatenate([routes[:, :, 0], routes[:, :, 1]], 1)
    onehot = (ordering[:, :, None] == jnp.arange(experts, dtype=jnp.int32)).astype(BF)
    count = 2 * rows
    earlier = (jnp.arange(count)[:, None] > jnp.arange(count)[None, :]).astype(BF)
    before = jnp.einsum("ab,mbe->mae", earlier, onehot, preferred_element_type=F32)
    rank = jnp.sum(before * onehot, -1).astype(jnp.int32)
    target = jnp.where(rank < capacity, ordering * capacity + rank, -1)
    slots = jnp.arange(experts * capacity, dtype=jnp.int32)[None, :, None]
    first, second = target[:, None, :rows], target[:, None, rows:]
    return ((slots == first) | (slots == second)).astype(BF)


def exchange(blocks):
    merged = blocks.reshape(blocks.shape[0], -1, blocks.shape[-1])
    return lax.all_to_all(merged, "grp", split_axis=0, concat_axis=0, tiled=True).reshape(blocks.shape)


def add_low(left, right):
    return (left.astype(F32) + right.astype(F32)).astype(BF)


def corner(array):
    return array[(0,) * (array.ndim - 2)][:16, :LANES]


def scatter_sums(kept, sent, experts, replicas, beside):
    bits = experts.bit_length() - 1
    place = lax.axis_index("grp")
    own_rep = lax.axis_index("rep")
    rows, columns = kept.shape[1], kept.shape[2] - LANES
    half = columns // 2
    swap = [(0, 1), (1, 0)]

    def send(array, bit):
        return lax.ppermute(array, "grp", [(g, g ^ (1 << bit)) for g in range(experts)])

    def halve(array, bit, run=lambda kept: kept):
        mine, axis = (place >> bit) & 1, bits - 1 - bit
        sent = lax.dynamic_index_in_dim(array, 1 - mine, axis, keepdims=False)
        kept = lax.dynamic_index_in_dim(array, mine, axis, keepdims=False)
        return add_low(run(kept), send(sent, bit))

    def halve_columns(array, shared, run=lambda kept: kept):
        if replicas != 2:
            return run(array)
        cut = (array.shape[-1] - shared) // 2
        parts = [array[..., :cut], array[..., cut : 2 * cut]]
        mine, other = (jnp.where(own_rep == 0, parts[i], parts[1 - i]) for i in (0, 1))
        if shared:
            mine, other = (jnp.concatenate([p, array[..., 2 * cut :]], -1) for p in (mine, other))
        return add_low(run(mine), lax.ppermute(other, "rep", swap))

    sums = add_low(beside[0](kept), send(sent, 0))
    sums = sums.reshape((2,) * (bits - 1) + sums.shape[1:])
    left = jnp.concatenate([sums[..., :half], sums[..., columns:]], -1)
    right = sums[..., half:columns]
    left, right = halve_columns(left, LANES, beside[1]), halve(right, 1)
    left, right = halve(left, 1, beside[2]), halve_columns(right, 0)
    cut = right.shape[-1]
    sums = jnp.concatenate([left[..., :cut], right, left[..., cut:]], -1)
    for bit in range(2, bits):
        sums = halve(sums, bit, beside[min(bit + 1, 4)] if bit < 4 else lambda kept: kept)
    if replicas != 2:
        return lax.psum(sums, "rep").astype(F32)
    mine = sums[:, : 2 * cut]
    other = lax.ppermute(mine, "rep", swap)
    low, high = (jnp.where(own_rep == i, mine, other) for i in (0, 1))
    pieces = [low[:, :cut], high[:, :cut], low[:, cut:], high[:, cut:], sums[:, 2 * cut :]]
    return jnp.concatenate(pieces, 1).astype(F32)


def gather_pieces(piece, experts):
    second = lax.axis_index("rep")
    both = ("rep", "grp")

    def send(array, first, other):
        pairs = [(r * experts + g, r * experts + (g ^ k)) for r, k in enumerate((first, other)) for g in range(experts)]
        return lax.ppermute(array, both, pairs)

    def swap(array):
        return lax.ppermute(array, "rep", [(0, 1), (1, 0)])

    near, far = send(piece, 4, 4), send(piece, 8, 12)
    mixed = send(jnp.where(second == 0, piece, near), 2, 2)
    mixed_far = send(far, 2, 2)
    found = [(piece, 0, 0), (near, 4, 4), (far, 8, 12), (swap(far), 12, 8)]
    found += [(mixed, 2, 6), (swap(mixed), 6, 2), (mixed_far, 10, 14), (swap(mixed_far), 14, 10)]
    found += [(send(array, 1, 1), first ^ 1, other ^ 1) for array, first, other in found]
    return [array for array, _, _ in found], [(first, other) for _, first, other in found]


def shards(images, attn_qkv, attn_proj, router, gain_attn, gain_moe, expert_in, expert_out, routes, cotangent):
    experts = lax.axis_size("grp")
    replicas = lax.axis_size("rep")
    mine = lax.axis_index("grp")
    micro, _, seq, width = images.shape
    capacity = max(2, 8 * seq * images.shape[1] // (3 * experts))
    slots = experts * capacity
    split = attn_qkv.shape[1]
    deep = expert_in.shape[2]
    here = (lax.broadcasted_iota(jnp.int32, (1, LANES), 1) == mine).astype(F32)

    tables = slot_tables(routes.reshape(micro, seq, 2), experts, capacity)

    small = jnp.concatenate([router, gain_attn[:, None], gain_moe[:, None]], 1)
    small = jnp.pad(small, ((0, 0), (0, LANES - small.shape[1])))
    piece = jnp.concatenate([attn_qkv, attn_proj, small], 1)
    full_shape = (width, piece.shape[1])
    direct = experts == 16 and replicas == 2 and piece.shape[0] % 16 == 0
    place = (jnp.stack([mine, lax.axis_index("rep")]).astype(jnp.int32), None, None)
    if direct:
        pieces, differ = gather_pieces(piece, experts)
        [full] = call(
            "assemble",
            functools.partial(assemble_kernel, differ),
            (1,),
            [place] + [whole(p) for p in pieces],
            [made(full_shape, BF)],
            flops=12 * 10**9,
        )
    else:
        full = lax.all_gather(piece, "grp", axis=0, tiled=True)

    w_qkv = (full, (width, split), lambda i: (0, 0))
    w_proj = (full, (width, width), lambda i: (0, split // width))
    w_router = (full, (width, LANES), lambda i: (0, (split + width) // LANES))

    one_block = (experts, 1, capacity, width)
    first_grads = call(
        "pack",
        gather_kernel,
        (1,),
        [of_micro(tables, 0), of_micro(cotangent, 0)],
        [made(one_block, BF)],
        flops=2 * slots * seq * width,
    )[0]
    first_grads = exchange(first_grads)

    saved, sents = [None] * 4, []
    for m in range(micro):
        outs = [
            ((micro,) + shape, dtype, (None,) + shape, lambda i, m=m: (m, 0, 0))
            for shape, dtype in (((seq, width), BF), ((seq, split), BF), ((seq, width), BF), ((seq, width), F32))
        ]
        outs.append(made((experts, min(2, m + 1), capacity, width), BF))
        made_here = call(
            "attend",
            functools.partial(forward_kernel, split, experts),
            (1,),
            [of_micro(images, m), of_micro(tables, m), of_micro(cotangent, m)]
            + [w_qkv, w_proj, w_router],
            outs,
            flops=6 * 10**9,
            through=sents[1:],
            into=saved,
        )
        saved, sents[1:] = made_here[:4], made_here[5:]
        sents.append(made_here[4])

    block = 1024
    swap = [(0, 1), (1, 0)]
    order = [(True, 0), (False, 0), (True, 1), (True, 2), (False, 1), (False, 2)]
    if replicas != 2:
        order = [pair for pair in order if pair[0]]
    sets, groups = len(order), replicas if replicas == 2 else 1
    stacks = [None] * 6

    def part_of(array, at):
        return (array, (experts, None, capacity, width), lambda i: (0, at, 0, 0))

    def expert_call(own, m, arrays, through, after=()):
        place = order.index((own, m))
        ins = [
            part_of(*arrays[0]),
            part_of(*arrays[1]),
            whole(here),
            w_router,
            (expert_in, (None, width, block), lambda i: (0, 0, i)),
            (expert_out, (None, block, width), lambda i: (0, i, 0)),
        ]
        if own and tails:
            ins.append(whole(tails[-1]))
        outs = [
            ((sets, slots, deep), BF, (None, slots, block), lambda i: (place, 0, i)),
            ((sets, slots, deep), BF, (None, slots, block), lambda i: (place, 0, i)),
            ((sets, slots, width), BF, (None, slots, width), lambda i: (place, 0, 0)),
            ((sets, slots, width), BF, (None, slots, width), lambda i: (place, 0, 0)),
        ]
        scratch = []
        if own:
            last = m == micro - 1
            outs += [
                ((experts, micro, capacity, width), BF, (experts, None, capacity, width), lambda i: (0, m, 0, 0)),
                (one_block, BF, (experts, None, capacity, width), lambda i: (0, 0, 0, 0))
                if last
                else ((experts, micro - 1, capacity, width), BF, (experts, None, capacity, width), lambda i: (0, m, 0, 0)),
                made((width, LANES), F32),
            ]
            scratch = [pltpu.VMEM((slots, LANES), F32)] + [pltpu.VMEM((slots, width), F32)] * 2
        count = (5 if last else 6) if own else 4
        made_here = call(
            "expert_own" if own else "expert_other",
            functools.partial(expert_kernel, "later" if own and tails else own, experts),
            (deep // block,),
            ins,
            outs,
            scratch,
            flops=2 * slots * width * deep * (6 if own else 4),
            vmem=56,
            through=through,
            into=stacks[:count],
            after=[corner(a) for a in after],
        )
        stacks[:count] = made_here[:count]
        return made_here[count:]

    def total(lead, early, before, into, through, part=0, parts=1):
        steps = deep // total_block // parts
        first = part * steps
        half = sets // groups if early or before is not None else sets
        at = 0 if early or half == sets else groups - 1
        if lead:
            left = (stacks[0], (half, slots, total_block), lambda i: (at, 0, first + i))
            right = (stacks[2], (half, slots, width), lambda i: (at, 0, 0))
            out = ((1, deep, width), F32, (None, total_block, width), lambda i: (0, first + i, 0))
        else:
            left = (stacks[3], (half, slots, width), lambda i: (at, 0, 0))
            right = (stacks[1], (half, slots, total_block), lambda i: (at, 0, first + i))
            out = ((1, width, deep), F32, (None, width, total_block), lambda i: (0, 0, first + i))
        return call(
            "total_out" if lead else "total_in",
            total_kernel,
            (steps,),
            [left, right] + ([] if before is None else [(before,) + out[2:]]),
            [out],
            flops=2 * half * slots * width * steps * total_block,
            vmem=56,
            through=through,
            into=[into],
        )

    total_block = 512

    def swapped(array):
        return lax.ppermute(array, "rep", swap) if replicas == 2 else None


    def other(m, through):
        return expert_call(False, m, theirs[m], through) if replicas == 2 else through

    def waited(m):
        return [array for array, _ in theirs[m]] if replicas == 2 else []

    arrived = exchange(sents[0])
    ours = [((arrived, 0), (first_grads, 0))]
    theirs = [((swapped(arrived), 0), (swapped(first_grads), 0))]
    tails = []
    for m in range(1, micro):
        arrived = exchange(hold(sents[m], *waited(0)[1:]) if m == 1 else sents[m])
        tail, *handed = expert_call(True, m - 1, ours[m - 1], sents[m + 1 : m + 2] if m > 1 else [])
        tails.append(tail)
        if m == 1:
            handed = other(0, sents[2:3])
        sents[m + 1 : m + 2] = handed
        came = arrived.reshape(sents[1].shape)
        ours.append(((came, 0), (came, 1)))
        came = swapped(came)
        theirs.append(((came, 0), (came, 1)))
    early_in = None
    if groups == 2:
        early_in, stacks[5] = total(False, True, None, None, [stacks[5]])
    backs = exchange(stacks[5])
    last_back, tail = expert_call(True, micro - 1, ours[-1], [], waited(1)[:1])
    tails.append(tail)
    [last_back] = other(1, [last_back])
    last_back = exchange(last_back)

    one_all, packed_all, mix_all, middle_all = saved
    half_shape = (experts // 2, width // experts, full_shape[1])

    def backward_call(last, backs, tail, into, extra=(), through=(), after=()):
        start, count = (micro - 1, 1) if last else (0, micro - 1)

        def of(array):
            lead = array.ndim - 2
            return (
                array,
                (None,) * lead + array.shape[-2:],
                lambda i: (start + i,) + (0,) * (array.ndim - 1),
            )

        def each(shape, dtype):
            return ((count,) + shape, dtype, (None,) + shape, lambda i: (i,) + (0,) * len(shape))

        outs = [(images.shape, BF, (None, None, seq, width), lambda i: (start + i, 0, 0, 0))]
        scratch = [pltpu.VMEM((seq, width), BF)]
        if last:
            outs += [made(half_shape, BF)] * 2
            scratch += [pltpu.VMEM((seq, split), BF), pltpu.VMEM((seq, width), BF)]
            scratch += [pltpu.VMEM(full_shape, BF if (width // experts) % 16 == 0 else F32)]
        else:
            outs += [each((seq, split), BF), each((seq, width), BF), made((width, LANES), F32)]
        return call(
            "attend_back",
            functools.partial(backward_kernel, experts, last),
            (count,),
            [of(images), of(cotangent), of(middle_all), of(packed_all)]
            + [(backs, (experts, None, capacity, width), lambda i: (0, i, 0, 0)), of(tables), w_qkv, w_proj, w_router]
            + [whole(tail)]
            + list(extra),
            outs,
            scratch,
            flops=8 * 10**9 * count,
            through=through,
            into=[into],
            after=[corner(a) for a in after],
        )

    input_grads, grads_packed, lows, tail, stacks[4] = backward_call(
        False, backs, tails[-1], None, through=[stacks[4]], after=waited(micro - 1)[:1]
    )
    extra = [place] + [whole(a) for a in (one_all, mix_all, grads_packed, lows)]
    input_grads, kept, sent = backward_call(True, last_back, tail, input_grads, extra)
    results = exchange(stacks[4])

    made_in = made_out = outputs = None

    def beside_others(m):
        return lambda kept: other(m, [kept])[0]

    def beside_total(lead, part=0, parts=1):
        def run(kept):
            nonlocal made_in, made_out
            if lead:
                made_out, kept = total(True, False, None, made_out, [kept], part, parts)
            else:
                made_in, kept = total(False, False, early_in, made_in, [kept], part, parts)
            return kept

        return run

    def beside_combine(kept):
        nonlocal outputs
        outputs, kept = call(
            "combine",
            combine_kernel,
            (1,),
            [whole(a) for a in (middle_all, tables, results)],
            [made(images.shape, BF)],
            flops=micro * 10**9,
            through=[kept],
        )
        return kept

    def both(*runs):
        def run(kept):
            for r in runs:
                kept = r(kept)
            return kept

        return run

    sums = scatter_sums(
        kept,
        sent,
        experts,
        replicas,
        [
            beside_others(2),
            beside_total(False),
            beside_total(True, 0, 2),
            beside_total(True, 1, 2),
            beside_combine,
        ],
    )
    grad_in, grad_out = made_in, made_out
    if replicas != 2:
        grad_in, grad_out = (lax.psum(g.astype(BF), "rep").astype(F32) for g in (grad_in, grad_out))
    return (
        outputs,
        input_grads,
        sums[:, :split],
        sums[:, split : split + width],
        sums[:, split + width : split + width + experts],
        sums[:, split + width + experts],
        sums[:, split + width + experts + 1],
        grad_in,
        grad_out,
    )


def solution(mesh):
    tokens = P(None, ("rep", "grp"), None, None)
    rows = P("grp", None)
    expert = P("grp", None, None)
    return jax.shard_map(
        shards,
        mesh=mesh,
        in_specs=(tokens, rows, rows, rows, P("grp"), P("grp"), expert, expert, tokens, tokens),
        out_specs=(tokens, tokens, rows, rows, rows, P("grp"), P("grp"), expert, expert),
        check_vma=False,
    )
```

```python
import functools

import jax
import jax.numpy as jnp
from jax import lax
from jax.experimental import pallas as pl
from jax.experimental.pallas import tpu as pltpu
from jax.sharding import PartitionSpec as P

HEADS = 12
EPSILON = 1e-06
BF = jnp.bfloat16
F32 = jnp.float32
LANES = 128
COST = 0.6


def dot_tn(left, right):
    return lax.dot_general(left, right, (((0,), (0,)), ((), ())), preferred_element_type=F32)


def dot_nt(left, right):
    return lax.dot_general(left, right, (((1,), (1,)), ((), ())), preferred_element_type=F32)


def dot_nn(left, right):
    return jnp.dot(left, right, preferred_element_type=F32)


def normalize(values):
    center = values - jnp.mean(values, -1, keepdims=True)
    inverse = lax.rsqrt(jnp.mean(center * center, -1, keepdims=True) + EPSILON)
    return center * inverse, inverse


def norm_backward(grad_rows, unit_rows, inverse, gain_row):
    scaled = grad_rows * gain_row
    inner = (
        scaled
        - jnp.mean(scaled, -1, keepdims=True)
        - unit_rows * jnp.mean(scaled * unit_rows, -1, keepdims=True)
    )
    return inner * inverse


def call(name, body, grid, ins, outs, scratch=(), flops=0, vmem=56, through=(), into=(), after=()):
    buffers = [(i, array) for i, array in enumerate(into) if array is not None]
    kept = list(through) + [array for _, array in buffers] + list(after)
    count, made_count = len(ins), len(outs)
    aliases = {count + i: made_count + i for i in range(len(through))}
    for place, (i, _) in enumerate(buffers):
        aliases[count + len(through) + place] = i

    def inner(*refs):
        rest = refs[count + len(kept) :]
        body(*refs[:count], *rest[:made_count], *rest[made_count + len(through) :])

    anywhere = pl.BlockSpec(memory_space=pltpu.HBM)
    return pl.pallas_call(
        inner if kept else body,
        grid=grid,
        in_specs=[
            pl.BlockSpec(memory_space=index) if block is None else pl.BlockSpec(block, index)
            for _, block, index in ins
        ]
        + [anywhere] * len(kept),
        out_specs=[pl.BlockSpec(block, index) for _, _, block, index in outs] + [anywhere] * len(through),
        out_shape=[jax.ShapeDtypeStruct(shape, dtype) for shape, dtype, _, _ in outs]
        + [jax.ShapeDtypeStruct(array.shape, array.dtype) for array in through],
        scratch_shapes=list(scratch),
        input_output_aliases=aliases,
        compiler_params=pltpu.CompilerParams(vmem_limit_bytes=vmem * 2**20),
        cost_estimate=pl.CostEstimate(flops=int(flops * COST), bytes_accessed=0, transcendentals=0),
        name=name,
    )(*[array for array, _, _ in ins], *kept)


def whole(array):
    return (array, array.shape, lambda i: (0,) * array.ndim)


def made(shape, dtype):
    return (shape, dtype, shape, lambda i: (0,) * len(shape))


def of_micro(array, m):
    lead = array.ndim - 2
    return (array, (None,) * lead + array.shape[-2:], lambda i: (m,) + (0,) * (array.ndim - 1))


def head_mask(width):
    return lax.broadcasted_iota(jnp.int32, (1, LANES), 1) // (width // HEADS)


def softmax(scores):
    top = jnp.exp(scores - jnp.max(scores, -1, keepdims=True))
    return top * (1.0 / jnp.sum(top, -1, keepdims=True))


def hold_kernel(out):
    out[...] = jnp.zeros_like(out)


def hold(array, *waited):
    if not waited:
        return array
    after = [corner(w) for w in waited]
    return call("hold", hold_kernel, (1,), [], [made((8, LANES), F32)], through=[array], after=after)[1]


def join_kernel(qkv, proj, router, gain_one, gain_two, out):
    rows = qkv.shape[0]
    out[:, : qkv.shape[1]] = qkv[...]
    end = qkv.shape[1] + proj.shape[1]
    out[:, qkv.shape[1] : end] = proj[...]
    parts = [router[...].astype(F32), gain_one[...].astype(F32), gain_two[...].astype(F32)]
    parts.append(jnp.zeros((LANES - router.shape[0] - 2, rows), F32))
    out[:, end:] = jnp.concatenate(parts, 0).T.astype(BF)


def gather_kernel(table, rows, out):
    out[...] = dot_nn(table[...], rows[...]).astype(BF).reshape(out.shape)


def gain_rows(small, experts):
    return small[...].astype(F32).T[experts : experts + 2]


def forward_kernel(split, experts, image, table, grad_y, *refs):
    w_qkv, w_proj, small, *outs = refs
    one_o, packed_o, mix_o, middle_o, slots_o = outs
    gains = gain_rows(small, experts)
    width = image.shape[1]
    states = image[...].astype(F32)
    unit, _ = normalize(states)
    one = (unit * gains[0:1]).astype(BF)
    one_o[...] = one
    packed_o[...] = dot_nn(one, w_qkv[...]).astype(BF)
    head = head_mask(width)
    per = LANES * HEADS // width
    factor = (width // HEADS) ** (-0.5)
    for low in range(0, width, LANES):
        query = packed_o[:, low : low + LANES]
        keys = packed_o[:, width + low : width + low + LANES]
        values = packed_o[:, 2 * width + low : 2 * width + low + LANES]
        mixed = 0.0
        for h in range(per):
            mine = (head == h).astype(BF)
            weights = softmax(dot_nt(query * mine, keys) * factor).astype(BF)
            mixed = mixed + dot_nn(weights, values * mine)
        mix_o[:, low : low + LANES] = mixed.astype(BF)
    middle = states + dot_nn(mix_o[...], w_proj[...])
    middle_o[...] = middle
    unit, _ = normalize(middle)
    two = (unit * gains[1:2]).astype(BF)
    block = slots_o.shape[:1] + slots_o.shape[2:]
    for at, rows in enumerate((two, grad_y[...])[: slots_o.shape[1]]):
        slots_o[:, at] = dot_nn(table[...], rows).astype(BF).reshape(block)


def assemble_kernel(differ, place, *refs):
    *pieces, full = refs
    rows = pieces[0].shape[0]
    for piece, (first, other) in zip(pieces, differ):
        at = place[0] ^ jnp.where(place[1] == 0, first, other)
        full[pl.ds(pl.multiple_of(at * rows, 16), rows), :] = piece[...]


def backward_kernel(
    column, last, image, grad_y, middle, packed, backs, table, w_proj, small, tail_in, w_all, *refs
):
    if last:
        place, *late, grad_image_o, kept_o, sent_o = refs[:8]
        mixture_s, grad_packed_o, low_o, sums, w_qkv, *held, arrived = refs[8:]
    else:
        grad_image_o, grad_packed_o, low_o, tail_o, mixture_s, w_qkv, arrived = refs
        late, held = [], []
    first = pl.program_id(0) == 0
    fetches = [pltpu.make_async_copy(w_all.at[:, : w_qkv.shape[1]], w_qkv, arrived.at[0])]
    fetches += [pltpu.make_async_copy(a, b, arrived.at[1 + i]) for i, (a, b) in enumerate(zip(late, held))]

    @pl.when(first)
    def _():
        for fetch in fetches:
            fetch.start()

    width = image.shape[1]
    backs = backs[...]
    gains = gain_rows(small, column)
    grad_two = dot_tn(table[...], backs.reshape(-1, width))
    unit, inverse = normalize(middle[...])
    gain_two = grad_two * unit
    grad_middle = grad_y[...].astype(F32) + norm_backward(grad_two, unit, inverse, gains[1:2])
    low_o[...] = grad_middle.astype(BF)
    mixture_s[...] = dot_nt(low_o[...], w_proj[...]).astype(BF)
    head = head_mask(width)
    per = LANES * HEADS // width
    factor = (width // HEADS) ** (-0.5)
    for low in range(0, width, LANES):
        query = packed[:, low : low + LANES]
        keys = packed[:, width + low : width + low + LANES]
        values = packed[:, 2 * width + low : 2 * width + low + LANES]
        grad_mixed = mixture_s[:, low : low + LANES]
        grad_query = grad_keys = grad_values = 0.0
        for h in range(per):
            mine = (head == h).astype(BF)
            query_h, keys_h, grad_h = query * mine, keys * mine, grad_mixed * mine
            weights = softmax(dot_nt(query_h, keys) * factor)
            grad_values = grad_values + dot_tn(weights.astype(BF), grad_h)
            grad_weights = dot_nt(grad_h, values)
            inner = jnp.sum(grad_weights * weights, -1, keepdims=True)
            grad_scores = (weights * (grad_weights - inner)).astype(BF)
            grad_query = grad_query + dot_nn(grad_scores, keys_h)
            grad_keys = grad_keys + dot_tn(grad_scores, query_h)
        grad_packed_o[:, low : low + LANES] = (grad_query * factor).astype(BF)
        grad_packed_o[:, width + low : width + low + LANES] = (grad_keys * factor).astype(BF)
        grad_packed_o[:, 2 * width + low : 2 * width + low + LANES] = grad_values.astype(BF)

    @pl.when(first)
    def _():
        fetches[0].wait()

    grad_one = dot_nt(grad_packed_o[...], w_qkv[...])
    unit, inverse = normalize(image[...].astype(F32))
    gain_one = grad_one * unit
    grad_image_o[...] = (grad_middle + norm_backward(grad_one, unit, inverse, gains[0:1])).astype(BF)
    lane = lax.broadcasted_iota(jnp.int32, (image.shape[0], LANES), 1)
    tail = 0.0
    for at, gain in ((column, gain_one), (column + 1, gain_two)):
        column_of = (lane == at).astype(BF)
        high = gain.astype(BF)
        tail = tail + dot_tn(high, column_of) + dot_tn((gain - high.astype(F32)).astype(BF), column_of)
    if last:
        sums[:, 4 * width :] = (tail_in[...] + tail).astype(sums.dtype)
        for fetch in fetches[1:]:
            fetch.wait()
        ones, mixes, packs, lows = held
        dense_sums(place, (ones, mixes), (packs, lows), (grad_packed_o, low_o), sums, kept_o, sent_o)
    else:

        @pl.when(first)
        def _():
            tail_o[...] = tail_in[...] + tail

        @pl.when(jnp.logical_not(first))
        def _():
            tail_o[...] += tail


def expert_kernel(own, experts, slots_in, grad_in, here, router, w_in, w_out, *refs):
    tail_in, *refs = refs if own == "later" else (None, *refs)
    active_o, hidden_o, result_o, rows_o, *rest = refs
    step = pl.program_id(0)
    if own:
        sent_o, back_o, tail_o, probs_s, result_s, back_s = rest
    width = slots_in.shape[-1]
    rows = slots_in[...].reshape(-1, width)

    @pl.when(step == 0)
    def _():
        rows_o[...] = rows
        logits = dot_nn(rows, router[...])
        lane = lax.broadcasted_iota(jnp.int32, logits.shape, 1)
        probs = softmax(jnp.where(lane < experts, logits, -1e30))
        gate = jnp.sum(probs * here[...], -1, keepdims=True)
        result_o[...] = (gate * grad_in[...].reshape(-1, width).astype(F32)).astype(BF)
        if own:
            probs_s[...] = probs
            result_s[...] = jnp.zeros_like(result_s)
            back_s[...] = jnp.zeros_like(back_s)

    hidden = dot_nn(rows, w_in[...])
    grad_active = dot_nt(result_o[...], w_out[...])
    cumulative = 0.5 + 0.5 * lax.erf(hidden * (0.5**0.5))
    active = (hidden * cumulative).astype(BF)
    slope = cumulative + hidden * jnp.exp(-0.5 * hidden * hidden) * 0.3989422804014327
    grad_hidden = (grad_active * slope).astype(BF)
    active_o[...] = active
    hidden_o[...] = grad_hidden
    if own:
        result_s[...] += dot_nn(active, w_out[...])
        back_s[...] += dot_nt(grad_hidden, w_in[...])

        @pl.when(step == pl.num_programs(0) - 1)
        def _():
            probs = probs_s[...]
            gate = jnp.sum(probs * here[...], -1, keepdims=True)
            result = result_s[...]
            grad_gate = jnp.sum(grad_in[...].reshape(-1, width).astype(F32) * result, -1, keepdims=True)
            grad_logit = (grad_gate * gate * (here[...] - probs)).astype(BF)
            back_o[...] = (back_s[...] + dot_nt(grad_logit, router[...])).astype(BF).reshape(back_o.shape)
            sent_o[...] = (gate * result).astype(BF).reshape(sent_o.shape)
            tail = dot_tn(rows, grad_logit)
            tail_o[...] = tail if tail_in is None else tail_in[...] + tail


def total_kernel(left, right, *refs):
    total = dot_tn(left[...].reshape(-1, left.shape[-1]), right[...].reshape(-1, right.shape[-1]))
    refs[-1][...] = total if len(refs) == 1 else refs[0][...] + total


def dense_sums(place, lefts, rights, last, sums, kept_o, sent_o):
    width = lefts[0].shape[-1]

    def total(which, part):
        left, right = lefts[which], rights[which]
        result = dot_tn(left[left.shape[0] - 1], last[which][:, part])
        for i in range(right.shape[0]):
            result = result + dot_tn(left[i], right[i, :, part])
        return result.astype(sums.dtype)

    for j in range(3):
        part = slice(j * width, (j + 1) * width)
        sums[:, part] = total(0, part)
    sums[:, 3 * width : 4 * width] = total(1, slice(None))
    half, rows = kept_o.shape[:2]
    bit = place[0] & 1
    for j in range(half):
        for out, at in ((kept_o, 2 * j + bit), (sent_o, 2 * j + 1 - bit)):
            out[j] = sums[pl.ds(pl.multiple_of(at * rows, rows), rows), :].astype(BF)


def combine_kernel(middle, tables, results, out):
    for m in range(middle.shape[0]):
        rows = results[:, m].reshape(-1, middle.shape[-1])
        out[m, 0] = (middle[m] + dot_tn(tables[m], rows)).astype(BF)


def finish_kernel(experts, place, mine, other, qkv_o, proj_o, router_o, one_o, two_o):
    cut = other.shape[1] // 2
    split = qkv_o.shape[1]
    first = place[1] == 0
    for k in range(4):
        part = slice(k // 2 * cut, (k // 2 + 1) * cut)
        both = (mine[:, part], other[:, part])
        columns = jnp.where(first, both[k % 2], both[1 - k % 2]).astype(F32)
        at = k * cut
        if at < split:
            qkv_o[:, at : at + cut] = columns
        else:
            proj_o[:, at - split : at - split + cut] = columns
    tail = mine[:, 2 * cut :].astype(F32)
    rows = tail.T
    router_o[...] = rows[:experts]
    one_o[...] = rows[experts : experts + 1]
    two_o[...] = rows[experts + 1 : experts + 2]


def slot_tables(routes, experts, capacity):
    rows = routes.shape[1]
    ordering = jnp.concatenate([routes[:, :, 0], routes[:, :, 1]], 1)
    onehot = (ordering[:, :, None] == jnp.arange(experts, dtype=jnp.int32)).astype(BF)
    count = 2 * rows
    earlier = (jnp.arange(count)[:, None] > jnp.arange(count)[None, :]).astype(BF)
    before = jnp.einsum("ab,mbe->mae", earlier, onehot, preferred_element_type=F32)
    rank = jnp.sum(before * onehot, -1).astype(jnp.int32)
    target = jnp.where(rank < capacity, ordering * capacity + rank, -1)
    slots = jnp.arange(experts * capacity, dtype=jnp.int32)[None, :, None]
    first, second = target[:, None, :rows], target[:, None, rows:]
    return ((slots == first) | (slots == second)).astype(BF)


def exchange(blocks):
    merged = blocks.reshape(blocks.shape[0], -1, blocks.shape[-1])
    return lax.all_to_all(merged, "grp", split_axis=0, concat_axis=0, tiled=True).reshape(blocks.shape)


def add_low(left, right):
    return (left.astype(F32) + right.astype(F32)).astype(BF)


def corner(array):
    return array[(0,) * (array.ndim - 2)][:16, :LANES]


def scatter_sums(kept, sent, experts, replicas, beside):
    bits = experts.bit_length() - 1
    place = lax.axis_index("grp")
    own_rep = lax.axis_index("rep")
    rows, columns = kept.shape[1], kept.shape[2] - LANES
    half = columns // 2
    swap = [(0, 1), (1, 0)]

    def send(array, bit):
        return lax.ppermute(array, "grp", [(g, g ^ (1 << bit)) for g in range(experts)])

    def halve(array, bit, run=lambda kept: kept):
        mine, axis = (place >> bit) & 1, bits - 1 - bit
        sent = lax.dynamic_index_in_dim(array, 1 - mine, axis, keepdims=False)
        kept = lax.dynamic_index_in_dim(array, mine, axis, keepdims=False)
        return add_low(run(kept), send(sent, bit))

    def halve_columns(array, shared, run=lambda kept: kept):
        if replicas != 2:
            return run(array)
        cut = (array.shape[-1] - shared) // 2
        parts = [array[..., :cut], array[..., cut : 2 * cut]]
        mine, other = (jnp.where(own_rep == 0, parts[i], parts[1 - i]) for i in (0, 1))
        if shared:
            mine, other = (jnp.concatenate([p, array[..., 2 * cut :]], -1) for p in (mine, other))
        return add_low(run(mine), lax.ppermute(other, "rep", swap))

    sums = add_low(beside[0](kept), send(sent, 0))
    sums = sums.reshape((2,) * (bits - 1) + sums.shape[1:])
    left = jnp.concatenate([sums[..., :half], sums[..., columns:]], -1)
    right = sums[..., half:columns]
    left, right = halve_columns(left, LANES, beside[1]), halve(right, 1)
    left, right = halve(left, 1, beside[2]), halve_columns(right, 0)
    cut = right.shape[-1]
    sums = jnp.concatenate([left[..., :cut], right, left[..., cut:]], -1)
    for bit in range(2, bits):
        sums = halve(sums, bit, beside[min(bit + 1, 4)] if bit < 4 else lambda kept: kept)
    if replicas != 2:
        beside[5](sums)
        return lax.psum(sums, "rep").astype(F32), None
    return beside[5](sums), lax.ppermute(sums[:, : 2 * cut], "rep", swap)


def gather_pieces(piece, experts):
    second = lax.axis_index("rep")
    both = ("rep", "grp")

    def send(array, first, other):
        pairs = [(r * experts + g, r * experts + (g ^ k)) for r, k in enumerate((first, other)) for g in range(experts)]
        return lax.ppermute(array, both, pairs)

    def swap(array):
        return lax.ppermute(array, "rep", [(0, 1), (1, 0)])

    near, far = send(piece, 4, 4), send(piece, 8, 12)
    mixed = send(jnp.where(second == 0, piece, near), 2, 2)
    mixed_far = send(far, 2, 2)
    found = [(piece, 0, 0), (near, 4, 4), (far, 8, 12), (swap(far), 12, 8)]
    found += [(mixed, 2, 6), (swap(mixed), 6, 2), (mixed_far, 10, 14), (swap(mixed_far), 14, 10)]
    found += [(send(array, 1, 1), first ^ 1, other ^ 1) for array, first, other in found]
    return [array for array, _, _ in found], [(first, other) for _, first, other in found]


def shards(images, attn_qkv, attn_proj, router, gain_attn, gain_moe, expert_in, expert_out, routes, cotangent):
    experts = lax.axis_size("grp")
    replicas = lax.axis_size("rep")
    mine = lax.axis_index("grp")
    micro, _, seq, width = images.shape
    capacity = max(2, 8 * seq * images.shape[1] // (3 * experts))
    slots = experts * capacity
    split = attn_qkv.shape[1]
    deep = expert_in.shape[2]
    here = (lax.broadcasted_iota(jnp.int32, (1, LANES), 1) == mine).astype(F32)

    tables = slot_tables(routes.reshape(micro, seq, 2), experts, capacity)

    shard = attn_qkv.shape[0]
    [piece] = call(
        "join",
        join_kernel,
        (1,),
        [whole(a) for a in (attn_qkv, attn_proj, router.T, gain_attn.reshape(1, shard), gain_moe.reshape(1, shard))],
        [made((shard, split + width + LANES), BF)],
    )
    full_shape = (width, piece.shape[1])
    direct = experts == 16 and replicas == 2 and piece.shape[0] % 16 == 0
    place = (jnp.stack([mine, lax.axis_index("rep")]).astype(jnp.int32), None, pltpu.SMEM)
    if direct:
        pieces, differ = gather_pieces(piece, experts)
        [full] = call(
            "assemble",
            functools.partial(assemble_kernel, differ),
            (1,),
            [place] + [whole(p) for p in pieces],
            [made(full_shape, BF)],
            flops=12 * 10**9,
        )
    else:
        full = lax.all_gather(piece, "grp", axis=0, tiled=True)

    w_qkv = (full, (width, split), lambda i: (0, 0))
    w_proj = (full, (width, width), lambda i: (0, split // width))
    w_router = (full, (width, LANES), lambda i: (0, (split + width) // LANES))

    one_block = (experts, 1, capacity, width)
    first_grads = call(
        "pack",
        gather_kernel,
        (1,),
        [of_micro(tables, 0), of_micro(cotangent, 0)],
        [made(one_block, BF)],
        flops=2 * slots * seq * width,
    )[0]
    first_grads = exchange(first_grads)

    saved, sents = [None] * 4, []
    for m in range(micro):
        outs = [
            ((micro,) + shape, dtype, (None,) + shape, lambda i, m=m: (m, 0, 0))
            for shape, dtype in (((seq, width), BF), ((seq, split), BF), ((seq, width), BF), ((seq, width), F32))
        ]
        outs.append(made((experts, min(2, m + 1), capacity, width), BF))
        made_here = call(
            "attend",
            functools.partial(forward_kernel, split, experts),
            (1,),
            [of_micro(images, m), of_micro(tables, m), of_micro(cotangent, m)]
            + [w_qkv, w_proj, w_router],
            outs,
            flops=6 * 10**9,
            through=sents[1:],
            into=saved,
        )
        saved, sents[1:] = made_here[:4], made_here[5:]
        sents.append(made_here[4])

    block = 1024
    swap = [(0, 1), (1, 0)]
    order = [(True, 0), (False, 0), (True, 1), (True, 2), (False, 1), (False, 2)]
    if replicas != 2:
        order = [pair for pair in order if pair[0]]
    sets, groups = len(order), replicas if replicas == 2 else 1
    stacks = [None] * 6

    def part_of(array, at):
        return (array, (experts, None, capacity, width), lambda i: (0, at, 0, 0))

    def expert_call(own, m, arrays, through, after=()):
        place = order.index((own, m))
        ins = [
            part_of(*arrays[0]),
            part_of(*arrays[1]),
            whole(here),
            w_router,
            (expert_in, (None, width, block), lambda i: (0, 0, i)),
            (expert_out, (None, block, width), lambda i: (0, i, 0)),
        ]
        if own and tails:
            ins.append(whole(tails[-1]))
        outs = [
            ((sets, slots, deep), BF, (None, slots, block), lambda i: (place, 0, i)),
            ((sets, slots, deep), BF, (None, slots, block), lambda i: (place, 0, i)),
            ((sets, slots, width), BF, (None, slots, width), lambda i: (place, 0, 0)),
            ((sets, slots, width), BF, (None, slots, width), lambda i: (place, 0, 0)),
        ]
        scratch = []
        if own:
            last = m == micro - 1
            outs += [
                ((experts, micro, capacity, width), BF, (experts, None, capacity, width), lambda i: (0, m, 0, 0)),
                (one_block, BF, (experts, None, capacity, width), lambda i: (0, 0, 0, 0))
                if last
                else ((experts, micro - 1, capacity, width), BF, (experts, None, capacity, width), lambda i: (0, m, 0, 0)),
                made((width, LANES), F32),
            ]
            scratch = [pltpu.VMEM((slots, LANES), F32)] + [pltpu.VMEM((slots, width), F32)] * 2
        count = (5 if last else 6) if own else 4
        made_here = call(
            "expert_own" if own else "expert_other",
            functools.partial(expert_kernel, "later" if own and tails else own, experts),
            (deep // block,),
            ins,
            outs,
            scratch,
            flops=2 * slots * width * deep * (6 if own else 4),
            vmem=56,
            through=through,
            into=stacks[:count],
            after=[corner(a) for a in after],
        )
        stacks[:count] = made_here[:count]
        return made_here[count:]

    def total(lead, early, before, into, through, part=0, parts=1):
        steps = deep // total_block // parts
        first = part * steps
        half = sets // groups if early or before is not None else sets
        at = 0 if early or half == sets else groups - 1
        if lead:
            left = (stacks[0], (half, slots, total_block), lambda i: (at, 0, first + i))
            right = (stacks[2], (half, slots, width), lambda i: (at, 0, 0))
            out = ((1, deep, width), F32, (None, total_block, width), lambda i: (0, first + i, 0))
        else:
            left = (stacks[3], (half, slots, width), lambda i: (at, 0, 0))
            right = (stacks[1], (half, slots, total_block), lambda i: (at, 0, first + i))
            out = ((1, width, deep), F32, (None, width, total_block), lambda i: (0, 0, first + i))
        return call(
            "total_out" if lead else "total_in",
            total_kernel,
            (steps,),
            [left, right] + ([] if before is None else [(before,) + out[2:]]),
            [out],
            flops=2 * half * slots * width * steps * total_block,
            vmem=56,
            through=through,
            into=[into],
        )

    total_block = 512

    def swapped(array):
        return lax.ppermute(array, "rep", swap) if replicas == 2 else None


    def other(m, through):
        return expert_call(False, m, theirs[m], through) if replicas == 2 else through

    def waited(m):
        return [array for array, _ in theirs[m]] if replicas == 2 else []

    arrived = exchange(sents[0])
    ours = [((arrived, 0), (first_grads, 0))]
    theirs = [((swapped(arrived), 0), (swapped(first_grads), 0))]
    tails = []
    for m in range(1, micro):
        arrived = exchange(hold(sents[m], *waited(0)[1:]) if m == 1 else sents[m])
        tail, *handed = expert_call(True, m - 1, ours[m - 1], sents[m + 1 : m + 2] if m > 1 else [])
        tails.append(tail)
        if m == 1:
            handed = other(0, sents[2:3])
        sents[m + 1 : m + 2] = handed
        came = arrived.reshape(sents[1].shape)
        ours.append(((came, 0), (came, 1)))
        came = swapped(came)
        theirs.append(((came, 0), (came, 1)))
    early_in = None
    if groups == 2:
        early_in, stacks[5] = total(False, True, None, None, [stacks[5]])
    backs = exchange(stacks[5])
    last_back, tail = expert_call(True, micro - 1, ours[-1], [], waited(1)[:1])
    tails.append(tail)
    [last_back] = other(1, [last_back])
    last_back = exchange(last_back)

    one_all, packed_all, mix_all, middle_all = saved
    half_shape = (experts // 2, width // experts, full_shape[1])

    def backward_call(last, backs, tail, into, late=(), through=(), after=()):
        start, count = (micro - 1, 1) if last else (0, micro - 1)

        def of(array):
            lead = array.ndim - 2
            return (
                array,
                (None,) * lead + array.shape[-2:],
                lambda i: (start + i,) + (0,) * (array.ndim - 1),
            )

        def each(shape, dtype):
            return ((count,) + shape, dtype, (None,) + shape, lambda i: (i,) + (0,) * len(shape))

        outs = [(images.shape, BF, (None, None, seq, width), lambda i: (start + i, 0, 0, 0))]
        scratch = [pltpu.VMEM((seq, width), BF)]
        if last:
            outs += [made(half_shape, BF)] * 2
            scratch += [pltpu.VMEM((seq, split), BF), pltpu.VMEM((seq, width), BF)]
            scratch += [pltpu.VMEM(full_shape, BF if (width // experts) % 16 == 0 else F32)]
        else:
            outs += [each((seq, split), BF), each((seq, width), BF), made((width, LANES), F32)]
        held = [pltpu.VMEM((width, split), BF)] + [pltpu.VMEM(a.shape, a.dtype) for a in late]
        scratch += held + [pltpu.SemaphoreType.DMA((len(held),))]
        return call(
            "attend_back",
            functools.partial(backward_kernel, experts, last),
            (count,),
            [of(images), of(cotangent), of(middle_all), of(packed_all)]
            + [(backs, (experts, None, capacity, width), lambda i: (0, i, 0, 0)), of(tables), w_proj, w_router]
            + [whole(tail), (full, None, pl.ANY)]
            + ([place] if last else [])
            + [(a, None, pl.ANY) for a in late],
            outs,
            scratch,
            flops=8 * 10**9 * count,
            through=through,
            into=[into],
            after=[corner(a) for a in after],
        )

    input_grads, grads_packed, lows, tail, stacks[4] = backward_call(
        False, backs, tails[-1], None, through=[stacks[4]], after=waited(micro - 1)[:1]
    )
    input_grads, kept, sent = backward_call(
        True, last_back, tail, input_grads, (one_all, mix_all, grads_packed, lows)
    )
    results = exchange(stacks[4])

    made_in = made_out = outputs = None

    def beside_others(m):
        return lambda kept: other(m, [kept])[0]

    def beside_total(lead, part=0, parts=1):
        def run(kept):
            nonlocal made_in, made_out
            if lead:
                made_out, kept = total(True, False, None, made_out, [kept], part, parts)
            else:
                made_in, kept = total(False, False, early_in, made_in, [kept], part, parts)
            return kept

        return run

    def beside_combine(kept):
        nonlocal outputs
        outputs, kept = call(
            "combine",
            combine_kernel,
            (1,),
            [whole(a) for a in (middle_all, tables, results)],
            [made(images.shape, BF)],
            flops=micro * 10**9,
            through=[kept],
        )
        return kept

    def both(*runs):
        def run(kept):
            for r in runs:
                kept = r(kept)
            return kept

        return run

    sums, other_sums = scatter_sums(
        kept,
        sent,
        experts,
        replicas,
        [
            beside_others(2),
            beside_total(False),
            beside_total(True, 0, 3),
            beside_total(True, 1, 3),
            beside_total(True, 2, 3),
            beside_combine,
        ],
    )
    grad_in, grad_out = made_in, made_out
    if replicas != 2:
        grad_in, grad_out = (lax.psum(g.astype(BF), "rep").astype(F32) for g in (grad_in, grad_out))
    if other_sums is None:
        end = split + width
        dense_grads = (
            sums[:, :split],
            sums[:, split:end],
            sums[:, end : end + experts],
            sums[:, end + experts],
            sums[:, end + experts + 1],
        )
    else:
        rows = sums.shape[0]
        *dense_grads, one_gain, two_gain = call(
            "finish",
            functools.partial(finish_kernel, experts),
            (1,),
            [place, whole(sums), whole(other_sums)],
            [made(shape, F32) for shape in ((rows, split), (rows, width), (experts, rows), (1, rows), (1, rows))],
        )
        dense_grads[2] = dense_grads[2].T
        dense_grads += [one_gain.reshape(rows), two_gain.reshape(rows)]
    return (outputs, input_grads, *dense_grads, grad_in, grad_out)


def solution(mesh):
    tokens = P(None, ("rep", "grp"), None, None)
    rows = P("grp", None)
    expert = P("grp", None, None)
    return jax.shard_map(
        shards,
        mesh=mesh,
        in_specs=(tokens, rows, rows, rows, P("grp"), P("grp"), expert, expert, tokens, tokens),
        out_specs=(tokens, tokens, rows, rows, rows, P("grp"), P("grp"), expert, expert),
        check_vma=False,
    )
```

```python
import functools

import jax
import jax.numpy as jnp
from jax import lax
from jax.experimental import pallas as pl
from jax.experimental.pallas import tpu as pltpu
from jax.sharding import PartitionSpec as P

HEADS = 12
EPSILON = 1e-06
BF = jnp.bfloat16
F32 = jnp.float32
LANES = 128
COST = 0.6


def dot_tn(left, right):
    return lax.dot_general(left, right, (((0,), (0,)), ((), ())), preferred_element_type=F32)


def dot_nt(left, right):
    return lax.dot_general(left, right, (((1,), (1,)), ((), ())), preferred_element_type=F32)


def dot_nn(left, right):
    return jnp.dot(left, right, preferred_element_type=F32)


def normalize(values):
    center = values - jnp.mean(values, -1, keepdims=True)
    inverse = lax.rsqrt(jnp.mean(center * center, -1, keepdims=True) + EPSILON)
    return center * inverse, inverse


def norm_backward(grad_rows, unit_rows, inverse, gain_row):
    scaled = grad_rows * gain_row
    inner = (
        scaled
        - jnp.mean(scaled, -1, keepdims=True)
        - unit_rows * jnp.mean(scaled * unit_rows, -1, keepdims=True)
    )
    return inner * inverse


def call(name, body, grid, ins, outs, scratch=(), flops=0, vmem=56, through=(), into=(), after=()):
    buffers = [(i, array) for i, array in enumerate(into) if array is not None]
    kept = list(through) + [array for _, array in buffers] + list(after)
    count, made_count = len(ins), len(outs)
    aliases = {count + i: made_count + i for i in range(len(through))}
    for place, (i, _) in enumerate(buffers):
        aliases[count + len(through) + place] = i

    def inner(*refs):
        rest = refs[count + len(kept) :]
        body(*refs[:count], *rest[:made_count], *rest[made_count + len(through) :])

    anywhere = pl.BlockSpec(memory_space=pltpu.HBM)
    return pl.pallas_call(
        inner if kept else body,
        grid=grid,
        in_specs=[
            pl.BlockSpec(memory_space=index) if block is None else pl.BlockSpec(block, index)
            for _, block, index in ins
        ]
        + [anywhere] * len(kept),
        out_specs=[pl.BlockSpec(block, index) for _, _, block, index in outs] + [anywhere] * len(through),
        out_shape=[jax.ShapeDtypeStruct(shape, dtype) for shape, dtype, _, _ in outs]
        + [jax.ShapeDtypeStruct(array.shape, array.dtype) for array in through],
        scratch_shapes=list(scratch),
        input_output_aliases=aliases,
        compiler_params=pltpu.CompilerParams(vmem_limit_bytes=vmem * 2**20),
        cost_estimate=pl.CostEstimate(flops=int(flops * COST), bytes_accessed=0, transcendentals=0),
        name=name,
    )(*[array for array, _, _ in ins], *kept)


def whole(array):
    return (array, array.shape, lambda i: (0,) * array.ndim)


def made(shape, dtype):
    return (shape, dtype, shape, lambda i: (0,) * len(shape))


def of_micro(array, m):
    lead = array.ndim - 2
    return (array, (None,) * lead + array.shape[-2:], lambda i: (m,) + (0,) * (array.ndim - 1))


def head_mask(width):
    return lax.broadcasted_iota(jnp.int32, (1, LANES), 1) // (width // HEADS)


def softmax(scores):
    top = jnp.exp(scores - jnp.max(scores, -1, keepdims=True))
    return top * (1.0 / jnp.sum(top, -1, keepdims=True))


def hold_kernel(out):
    out[...] = jnp.zeros_like(out)


def hold(array, *waited):
    if not waited:
        return array
    after = [corner(w) for w in waited]
    return call("hold", hold_kernel, (1,), [], [made((8, LANES), F32)], through=[array], after=after)[1]


def join_kernel(qkv, proj, router, gain_one, gain_two, out):
    rows = qkv.shape[0]
    out[:, : qkv.shape[1]] = qkv[...]
    end = qkv.shape[1] + proj.shape[1]
    out[:, qkv.shape[1] : end] = proj[...]
    parts = [router[...].astype(F32), gain_one[...].astype(F32), gain_two[...].astype(F32)]
    parts.append(jnp.zeros((LANES - router.shape[0] - 2, rows), F32))
    out[:, end:] = jnp.concatenate(parts, 0).T.astype(BF)


def gather_kernel(table, rows, out):
    out[...] = dot_nn(table[...], rows[...]).astype(BF).reshape(out.shape)


def gain_rows(small, experts):
    return small[...].astype(F32).T[experts : experts + 2]


def forward_kernel(split, experts, image, table, grad_y, *refs):
    w_qkv, w_proj, small, *outs = refs
    one_o, packed_o, mix_o, middle_o, slots_o = outs
    gains = gain_rows(small, experts)
    width = image.shape[1]
    states = image[...].astype(F32)
    unit, _ = normalize(states)
    one = (unit * gains[0:1]).astype(BF)
    one_o[...] = one
    packed_o[...] = dot_nn(one, w_qkv[...]).astype(BF)
    head = head_mask(width)
    per = LANES * HEADS // width
    factor = (width // HEADS) ** (-0.5)
    for low in range(0, width, LANES):
        query = packed_o[:, low : low + LANES]
        keys = packed_o[:, width + low : width + low + LANES]
        values = packed_o[:, 2 * width + low : 2 * width + low + LANES]
        mixed = 0.0
        for h in range(per):
            mine = (head == h).astype(BF)
            weights = softmax(dot_nt(query * mine, keys) * factor).astype(BF)
            mixed = mixed + dot_nn(weights, values * mine)
        mix_o[:, low : low + LANES] = mixed.astype(BF)
    middle = states + dot_nn(mix_o[...], w_proj[...])
    middle_o[...] = middle
    unit, _ = normalize(middle)
    two = (unit * gains[1:2]).astype(BF)
    block = slots_o.shape[:1] + slots_o.shape[2:]
    for at, rows in enumerate((two, grad_y[...])[: slots_o.shape[1]]):
        slots_o[:, at] = dot_nn(table[...], rows).astype(BF).reshape(block)


def assemble_kernel(differ, place, *refs):
    *pieces, full = refs
    rows = pieces[0].shape[0]
    for piece, (first, other) in zip(pieces, differ):
        at = place[0] ^ jnp.where(place[1] == 0, first, other)
        full[pl.ds(pl.multiple_of(at * rows, 16), rows), :] = piece[...]


def backward_kernel(
    column, last, image, grad_y, middle, packed, backs, table, w_proj, small, tail_in, w_all, *refs
):
    if last:
        place, *late, grad_image_o, kept_o, sent_o = refs[:8]
        mixture_s, grad_packed_o, low_o, sums, w_qkv, *held, arrived = refs[8:]
    else:
        grad_image_o, grad_packed_o, low_o, tail_o, mixture_s, w_qkv, arrived = refs
        late, held = [], []
    first = pl.program_id(0) == 0
    fetches = [pltpu.make_async_copy(w_all.at[:, : w_qkv.shape[1]], w_qkv, arrived.at[0])]
    fetches += [pltpu.make_async_copy(a, b, arrived.at[1 + i]) for i, (a, b) in enumerate(zip(late, held))]

    @pl.when(first)
    def _():
        for fetch in fetches:
            fetch.start()

    width = image.shape[1]
    backs = backs[...]
    gains = gain_rows(small, column)
    grad_two = dot_tn(table[...], backs.reshape(-1, width))
    unit, inverse = normalize(middle[...])
    gain_two = grad_two * unit
    grad_middle = grad_y[...].astype(F32) + norm_backward(grad_two, unit, inverse, gains[1:2])
    low_o[...] = grad_middle.astype(BF)
    mixture_s[...] = dot_nt(low_o[...], w_proj[...]).astype(BF)
    head = head_mask(width)
    per = LANES * HEADS // width
    factor = (width // HEADS) ** (-0.5)
    for low in range(0, width, LANES):
        query = packed[:, low : low + LANES]
        keys = packed[:, width + low : width + low + LANES]
        values = packed[:, 2 * width + low : 2 * width + low + LANES]
        grad_mixed = mixture_s[:, low : low + LANES]
        grad_query = grad_keys = grad_values = 0.0
        for h in range(per):
            mine = (head == h).astype(BF)
            query_h, keys_h, grad_h = query * mine, keys * mine, grad_mixed * mine
            weights = softmax(dot_nt(query_h, keys) * factor)
            grad_values = grad_values + dot_tn(weights.astype(BF), grad_h)
            grad_weights = dot_nt(grad_h, values)
            inner = jnp.sum(grad_weights * weights, -1, keepdims=True)
            grad_scores = (weights * (grad_weights - inner)).astype(BF)
            grad_query = grad_query + dot_nn(grad_scores, keys_h)
            grad_keys = grad_keys + dot_tn(grad_scores, query_h)
        grad_packed_o[:, low : low + LANES] = (grad_query * factor).astype(BF)
        grad_packed_o[:, width + low : width + low + LANES] = (grad_keys * factor).astype(BF)
        grad_packed_o[:, 2 * width + low : 2 * width + low + LANES] = grad_values.astype(BF)

    @pl.when(first)
    def _():
        fetches[0].wait()

    grad_one = dot_nt(grad_packed_o[...], w_qkv[...])
    unit, inverse = normalize(image[...].astype(F32))
    gain_one = grad_one * unit
    grad_image_o[...] = (grad_middle + norm_backward(grad_one, unit, inverse, gains[0:1])).astype(BF)
    lane = lax.broadcasted_iota(jnp.int32, (image.shape[0], LANES), 1)
    tail = 0.0
    for at, gain in ((column, gain_one), (column + 1, gain_two)):
        column_of = (lane == at).astype(BF)
        high = gain.astype(BF)
        tail = tail + dot_tn(high, column_of) + dot_tn((gain - high.astype(F32)).astype(BF), column_of)
    if last:
        sums[:, 4 * width :] = (tail_in[...] + tail).astype(sums.dtype)
        for fetch in fetches[1:]:
            fetch.wait()
        ones, mixes, packs, lows = held
        dense_sums(place, (ones, mixes), (packs, lows), (grad_packed_o, low_o), sums, kept_o, sent_o)
    else:

        @pl.when(first)
        def _():
            tail_o[...] = tail_in[...] + tail

        @pl.when(jnp.logical_not(first))
        def _():
            tail_o[...] += tail


def expert_kernel(own, experts, slots_in, grad_in, here, router, w_in, w_out, *refs):
    tail_in, *refs = refs if own == "later" else (None, *refs)
    active_o, hidden_o, result_o, rows_o, *rest = refs
    step = pl.program_id(0)
    if own:
        sent_o, back_o, tail_o, probs_s, result_s, back_s = rest
    width = slots_in.shape[-1]
    rows = slots_in[...].reshape(-1, width)

    @pl.when(step == 0)
    def _():
        rows_o[...] = rows
        logits = dot_nn(rows, router[...])
        lane = lax.broadcasted_iota(jnp.int32, logits.shape, 1)
        probs = softmax(jnp.where(lane < experts, logits, -1e30))
        gate = jnp.sum(probs * here[...], -1, keepdims=True)
        result_o[...] = (gate * grad_in[...].reshape(-1, width).astype(F32)).astype(BF)
        if own:
            probs_s[...] = probs
            result_s[...] = jnp.zeros_like(result_s)
            back_s[...] = jnp.zeros_like(back_s)

    hidden = dot_nn(rows, w_in[...])
    grad_active = dot_nt(result_o[...], w_out[...])
    cumulative = 0.5 + 0.5 * lax.erf(hidden * (0.5**0.5))
    active = (hidden * cumulative).astype(BF)
    slope = cumulative + hidden * jnp.exp(-0.5 * hidden * hidden) * 0.3989422804014327
    grad_hidden = (grad_active * slope).astype(BF)
    active_o[...] = active
    hidden_o[...] = grad_hidden
    if own:
        result_s[...] += dot_nn(active, w_out[...])
        back_s[...] += dot_nt(grad_hidden, w_in[...])

        @pl.when(step == pl.num_programs(0) - 1)
        def _():
            probs = probs_s[...]
            gate = jnp.sum(probs * here[...], -1, keepdims=True)
            result = result_s[...]
            grad_gate = jnp.sum(grad_in[...].reshape(-1, width).astype(F32) * result, -1, keepdims=True)
            grad_logit = (grad_gate * gate * (here[...] - probs)).astype(BF)
            back_o[...] = (back_s[...] + dot_nt(grad_logit, router[...])).astype(BF).reshape(back_o.shape)
            sent_o[...] = (gate * result).astype(BF).reshape(sent_o.shape)
            tail = dot_tn(rows, grad_logit)
            tail_o[...] = tail if tail_in is None else tail_in[...] + tail


def total_kernel(left, right, *refs):
    total = dot_tn(left[...].reshape(-1, left.shape[-1]), right[...].reshape(-1, right.shape[-1]))
    refs[-1][...] = total if len(refs) == 1 else refs[0][...] + total


def dense_sums(place, lefts, rights, last, sums, kept_o, sent_o):
    width = lefts[0].shape[-1]

    def total(which, part):
        left, right = lefts[which], rights[which]
        result = dot_tn(left[left.shape[0] - 1], last[which][:, part])
        for i in range(right.shape[0]):
            result = result + dot_tn(left[i], right[i, :, part])
        return result.astype(sums.dtype)

    for j in range(3):
        part = slice(j * width, (j + 1) * width)
        sums[:, part] = total(0, part)
    sums[:, 3 * width : 4 * width] = total(1, slice(None))
    half, rows = kept_o.shape[:2]
    bit = place[0] & 1
    for j in range(half):
        for out, at in ((kept_o, 2 * j + bit), (sent_o, 2 * j + 1 - bit)):
            out[j] = sums[pl.ds(pl.multiple_of(at * rows, rows), rows), :].astype(BF)


def combine_kernel(middle, tables, results, out):
    for m in range(middle.shape[0]):
        rows = results[:, m].reshape(-1, middle.shape[-1])
        out[m, 0] = (middle[m] + dot_tn(tables[m], rows)).astype(BF)


def finish_kernel(experts, place, mine, other, qkv_o, proj_o, router_o, one_o, two_o):
    cut = other.shape[1] // 2
    split = qkv_o.shape[1]
    first = place[1] == 0
    for k in range(4):
        part = slice(k // 2 * cut, (k // 2 + 1) * cut)
        both = (mine[:, part], other[:, part])
        columns = jnp.where(first, both[k % 2], both[1 - k % 2]).astype(F32)
        at = k * cut
        if at < split:
            qkv_o[:, at : at + cut] = columns
        else:
            proj_o[:, at - split : at - split + cut] = columns
    tail = mine[:, 2 * cut :].astype(F32)
    rows = tail.T
    router_o[...] = rows[:experts]
    one_o[...] = rows[experts : experts + 1]
    two_o[...] = rows[experts + 1 : experts + 2]


def slot_tables(routes, experts, capacity):
    rows = routes.shape[1]
    ordering = jnp.concatenate([routes[:, :, 0], routes[:, :, 1]], 1)
    onehot = (ordering[:, :, None] == jnp.arange(experts, dtype=jnp.int32)).astype(BF)
    count = 2 * rows
    earlier = (jnp.arange(count)[:, None] > jnp.arange(count)[None, :]).astype(BF)
    before = jnp.einsum("ab,mbe->mae", earlier, onehot, preferred_element_type=F32)
    rank = jnp.sum(before * onehot, -1).astype(jnp.int32)
    target = jnp.where(rank < capacity, ordering * capacity + rank, -1)
    slots = jnp.arange(experts * capacity, dtype=jnp.int32)[None, :, None]
    first, second = target[:, None, :rows], target[:, None, rows:]
    return ((slots == first) | (slots == second)).astype(BF)


def exchange(blocks):
    merged = blocks.reshape(blocks.shape[0], -1, blocks.shape[-1])
    return lax.all_to_all(merged, "grp", split_axis=0, concat_axis=0, tiled=True).reshape(blocks.shape)


def add_low(left, right):
    return (left.astype(F32) + right.astype(F32)).astype(BF)


def corner(array):
    return array[(0,) * (array.ndim - 2)][:16, :LANES]


def scatter_sums(kept, sent, experts, replicas, beside):
    bits = experts.bit_length() - 1
    place = lax.axis_index("grp")
    own_rep = lax.axis_index("rep")
    rows, columns = kept.shape[1], kept.shape[2] - LANES
    half = columns // 2
    swap = [(0, 1), (1, 0)]

    def send(array, bit):
        return lax.ppermute(array, "grp", [(g, g ^ (1 << bit)) for g in range(experts)])

    def halve(array, bit, run=lambda kept: kept):
        mine, axis = (place >> bit) & 1, bits - 1 - bit
        sent = lax.dynamic_index_in_dim(array, 1 - mine, axis, keepdims=False)
        kept = lax.dynamic_index_in_dim(array, mine, axis, keepdims=False)
        return add_low(run(kept), send(sent, bit))

    def halve_columns(array, shared, run=lambda kept: kept):
        if replicas != 2:
            return run(array)
        cut = (array.shape[-1] - shared) // 2
        parts = [array[..., :cut], array[..., cut : 2 * cut]]
        mine, other = (jnp.where(own_rep == 0, parts[i], parts[1 - i]) for i in (0, 1))
        if shared:
            mine, other = (jnp.concatenate([p, array[..., 2 * cut :]], -1) for p in (mine, other))
        return add_low(run(mine), lax.ppermute(other, "rep", swap))

    sums = add_low(beside[0](kept), send(sent, 0))
    sums = sums.reshape((2,) * (bits - 1) + sums.shape[1:])
    left = jnp.concatenate([sums[..., :half], sums[..., columns:]], -1)
    right = sums[..., half:columns]
    left, right = halve_columns(left, LANES, beside[1]), halve(right, 1)
    left, right = halve(left, 1, beside[2]), halve_columns(right, 0)
    cut = right.shape[-1]
    sums = jnp.concatenate([left[..., :cut], right, left[..., cut:]], -1)
    for bit in range(2, bits):
        sums = halve(sums, bit, beside[min(bit + 1, 4)] if bit < 4 else lambda kept: kept)
    if replicas != 2:
        beside[5](sums)
        return lax.psum(sums, "rep").astype(F32), None
    return beside[5](sums), lax.ppermute(sums[:, : 2 * cut], "rep", swap)


def pick_kernel(place, first, other, out):
    out[...] = jnp.where(place[1] == 0, first[...], other[...])


def gather_pieces(piece, experts, place, after):
    both = ("rep", "grp")

    def send(array, first, other):
        pairs = [(r * experts + g, r * experts + (g ^ k)) for r, k in enumerate((first, other)) for g in range(experts)]
        return lax.ppermute(array, both, pairs)

    def swap(array):
        return lax.ppermute(array, "rep", [(0, 1), (1, 0)])

    near, far = send(piece, 4, 4), send(piece, 8, 12)
    [mixed] = call(
        "pick",
        pick_kernel,
        (1,),
        [place, whole(piece), whole(near)],
        [made(piece.shape, piece.dtype)],
        after=[after],
    )
    mixed = send(mixed, 2, 2)
    mixed_far = send(far, 2, 2)
    found = [(piece, 0, 0), (near, 4, 4), (far, 8, 12), (swap(far), 12, 8)]
    found += [(mixed, 2, 6), (swap(mixed), 6, 2), (mixed_far, 10, 14), (swap(mixed_far), 14, 10)]
    found += [(send(array, 1, 1), first ^ 1, other ^ 1) for array, first, other in found]
    return [array for array, _, _ in found], [(first, other) for _, first, other in found]


def shards(images, attn_qkv, attn_proj, router, gain_attn, gain_moe, expert_in, expert_out, routes, cotangent):
    experts = lax.axis_size("grp")
    replicas = lax.axis_size("rep")
    mine = lax.axis_index("grp")
    micro, _, seq, width = images.shape
    capacity = max(2, 8 * seq * images.shape[1] // (3 * experts))
    slots = experts * capacity
    split = attn_qkv.shape[1]
    deep = expert_in.shape[2]
    here = (lax.broadcasted_iota(jnp.int32, (1, LANES), 1) == mine).astype(F32)

    tables = slot_tables(routes.reshape(micro, seq, 2), experts, capacity)

    one_block = (experts, 1, capacity, width)
    first_grads = call(
        "pack",
        gather_kernel,
        (1,),
        [of_micro(tables, 0), of_micro(cotangent, 0)],
        [made(one_block, BF)],
        flops=2 * slots * seq * width,
    )[0]
    shard = attn_qkv.shape[0]
    [piece] = call(
        "join",
        join_kernel,
        (1,),
        [whole(a) for a in (attn_qkv, attn_proj, router.T, gain_attn.reshape(1, shard), gain_moe.reshape(1, shard))],
        [made((shard, split + width + LANES), BF)],
    )
    full_shape = (width, piece.shape[1])
    direct = experts == 16 and replicas == 2 and piece.shape[0] % 16 == 0
    place = (jnp.stack([mine, lax.axis_index("rep")]).astype(jnp.int32), None, pltpu.SMEM)
    if direct:
        pieces, differ = gather_pieces(piece, experts, place, first_grads)
        [full] = call(
            "assemble",
            functools.partial(assemble_kernel, differ),
            (1,),
            [place] + [whole(p) for p in pieces],
            [made(full_shape, BF)],
            flops=12 * 10**9,
        )
    else:
        full = lax.all_gather(piece, "grp", axis=0, tiled=True)

    w_qkv = (full, (width, split), lambda i: (0, 0))
    w_proj = (full, (width, width), lambda i: (0, split // width))
    w_router = (full, (width, LANES), lambda i: (0, (split + width) // LANES))

    first_grads = exchange(first_grads)

    saved, sents = [None] * 4, []
    for m in range(micro):
        outs = [
            ((micro,) + shape, dtype, (None,) + shape, lambda i, m=m: (m, 0, 0))
            for shape, dtype in (((seq, width), BF), ((seq, split), BF), ((seq, width), BF), ((seq, width), F32))
        ]
        outs.append(made((experts, min(2, m + 1), capacity, width), BF))
        made_here = call(
            "attend",
            functools.partial(forward_kernel, split, experts),
            (1,),
            [of_micro(images, m), of_micro(tables, m), of_micro(cotangent, m)]
            + [w_qkv, w_proj, w_router],
            outs,
            flops=6 * 10**9,
            through=sents[1:],
            into=saved,
        )
        saved, sents[1:] = made_here[:4], made_here[5:]
        sents.append(made_here[4])

    block = 1024
    swap = [(0, 1), (1, 0)]
    order = [(True, 0), (False, 0), (True, 1), (True, 2), (False, 1), (False, 2)]
    if replicas != 2:
        order = [pair for pair in order if pair[0]]
    sets, groups = len(order), replicas if replicas == 2 else 1
    stacks = [None] * 6

    def part_of(array, at):
        return (array, (experts, None, capacity, width), lambda i: (0, at, 0, 0))

    def expert_call(own, m, arrays, through, after=()):
        place = order.index((own, m))
        ins = [
            part_of(*arrays[0]),
            part_of(*arrays[1]),
            whole(here),
            w_router,
            (expert_in, (None, width, block), lambda i: (0, 0, i)),
            (expert_out, (None, block, width), lambda i: (0, i, 0)),
        ]
        if own and tails:
            ins.append(whole(tails[-1]))
        outs = [
            ((sets, slots, deep), BF, (None, slots, block), lambda i: (place, 0, i)),
            ((sets, slots, deep), BF, (None, slots, block), lambda i: (place, 0, i)),
            ((sets, slots, width), BF, (None, slots, width), lambda i: (place, 0, 0)),
            ((sets, slots, width), BF, (None, slots, width), lambda i: (place, 0, 0)),
        ]
        scratch = []
        if own:
            last = m == micro - 1
            outs += [
                ((experts, micro, capacity, width), BF, (experts, None, capacity, width), lambda i: (0, m, 0, 0)),
                (one_block, BF, (experts, None, capacity, width), lambda i: (0, 0, 0, 0))
                if last
                else ((experts, micro - 1, capacity, width), BF, (experts, None, capacity, width), lambda i: (0, m, 0, 0)),
                made((width, LANES), F32),
            ]
            scratch = [pltpu.VMEM((slots, LANES), F32)] + [pltpu.VMEM((slots, width), F32)] * 2
        count = (5 if last else 6) if own else 4
        made_here = call(
            "expert_own" if own else "expert_other",
            functools.partial(expert_kernel, "later" if own and tails else own, experts),
            (deep // block,),
            ins,
            outs,
            scratch,
            flops=2 * slots * width * deep * (6 if own else 4),
            vmem=56,
            through=through,
            into=stacks[:count],
            after=[corner(a) for a in after],
        )
        stacks[:count] = made_here[:count]
        return made_here[count:]

    def total(lead, early, before, into, through, part=0, parts=1):
        steps = deep // total_block // parts
        first = part * steps
        half = sets // groups if early or before is not None else sets
        at = 0 if early or half == sets else groups - 1
        if lead:
            left = (stacks[0], (half, slots, total_block), lambda i: (at, 0, first + i))
            right = (stacks[2], (half, slots, width), lambda i: (at, 0, 0))
            out = ((1, deep, width), F32, (None, total_block, width), lambda i: (0, first + i, 0))
        else:
            left = (stacks[3], (half, slots, width), lambda i: (at, 0, 0))
            right = (stacks[1], (half, slots, total_block), lambda i: (at, 0, first + i))
            out = ((1, width, deep), F32, (None, width, total_block), lambda i: (0, 0, first + i))
        return call(
            "total_out" if lead else "total_in",
            total_kernel,
            (steps,),
            [left, right] + ([] if before is None else [(before,) + out[2:]]),
            [out],
            flops=2 * half * slots * width * steps * total_block,
            vmem=56,
            through=through,
            into=[into],
        )

    total_block = 512

    def swapped(array):
        return lax.ppermute(array, "rep", swap) if replicas == 2 else None


    def other(m, through):
        return expert_call(False, m, theirs[m], through) if replicas == 2 else through

    def waited(m):
        return [array for array, _ in theirs[m]] if replicas == 2 else []

    arrived = exchange(sents[0])
    ours = [((arrived, 0), (first_grads, 0))]
    theirs = [((swapped(arrived), 0), (swapped(first_grads), 0))]
    tails = []
    for m in range(1, micro):
        arrived = exchange(hold(sents[m], *waited(0)[1:]) if m == 1 else sents[m])
        tail, *handed = expert_call(True, m - 1, ours[m - 1], sents[m + 1 : m + 2] if m > 1 else [])
        tails.append(tail)
        if m == 1:
            handed = other(0, sents[2:3])
        sents[m + 1 : m + 2] = handed
        came = arrived.reshape(sents[1].shape)
        ours.append(((came, 0), (came, 1)))
        came = swapped(came)
        theirs.append(((came, 0), (came, 1)))
    early_in = None
    if groups == 2:
        early_in, stacks[5] = total(False, True, None, None, [stacks[5]])
    backs = exchange(stacks[5])
    last_back, tail = expert_call(True, micro - 1, ours[-1], [], waited(1)[:1])
    tails.append(tail)
    [last_back] = other(1, [last_back])
    last_back = exchange(last_back)

    one_all, packed_all, mix_all, middle_all = saved
    half_shape = (experts // 2, width // experts, full_shape[1])

    def backward_call(last, backs, tail, into, late=(), through=(), after=()):
        start, count = (micro - 1, 1) if last else (0, micro - 1)

        def of(array):
            lead = array.ndim - 2
            return (
                array,
                (None,) * lead + array.shape[-2:],
                lambda i: (start + i,) + (0,) * (array.ndim - 1),
            )

        def each(shape, dtype):
            return ((count,) + shape, dtype, (None,) + shape, lambda i: (i,) + (0,) * len(shape))

        outs = [(images.shape, BF, (None, None, seq, width), lambda i: (start + i, 0, 0, 0))]
        scratch = [pltpu.VMEM((seq, width), BF)]
        if last:
            outs += [made(half_shape, BF)] * 2
            scratch += [pltpu.VMEM((seq, split), BF), pltpu.VMEM((seq, width), BF)]
            scratch += [pltpu.VMEM(full_shape, BF if (width // experts) % 16 == 0 else F32)]
        else:
            outs += [each((seq, split), BF), each((seq, width), BF), made((width, LANES), F32)]
        held = [pltpu.VMEM((width, split), BF)] + [pltpu.VMEM(a.shape, a.dtype) for a in late]
        scratch += held + [pltpu.SemaphoreType.DMA((len(held),))]
        return call(
            "attend_back",
            functools.partial(backward_kernel, experts, last),
            (count,),
            [of(images), of(cotangent), of(middle_all), of(packed_all)]
            + [(backs, (experts, None, capacity, width), lambda i: (0, i, 0, 0)), of(tables), w_proj, w_router]
            + [whole(tail), (full, None, pl.ANY)]
            + ([place] if last else [])
            + [(a, None, pl.ANY) for a in late],
            outs,
            scratch,
            flops=8 * 10**9 * count,
            through=through,
            into=[into],
            after=[corner(a) for a in after],
        )

    input_grads, grads_packed, lows, tail, stacks[4] = backward_call(
        False, backs, tails[-1], None, through=[stacks[4]], after=waited(micro - 1)[:1]
    )
    input_grads, kept, sent = backward_call(
        True, last_back, tail, input_grads, (one_all, mix_all, grads_packed, lows)
    )
    results = exchange(stacks[4])

    made_in = made_out = outputs = None

    def beside_others(m):
        return lambda kept: other(m, [kept])[0]

    def beside_total(lead, part=0, parts=1):
        def run(kept):
            nonlocal made_in, made_out
            if lead:
                made_out, kept = total(True, False, None, made_out, [kept], part, parts)
            else:
                made_in, kept = total(False, False, early_in, made_in, [kept], part, parts)
            return kept

        return run

    def beside_combine(kept):
        nonlocal outputs
        outputs, kept = call(
            "combine",
            combine_kernel,
            (1,),
            [whole(a) for a in (middle_all, tables, results)],
            [made(images.shape, BF)],
            flops=micro * 10**9,
            through=[kept],
        )
        return kept

    def both(*runs):
        def run(kept):
            for r in runs:
                kept = r(kept)
            return kept

        return run

    sums, other_sums = scatter_sums(
        kept,
        sent,
        experts,
        replicas,
        [
            beside_others(2),
            beside_total(False),
            beside_total(True, 0, 3),
            beside_total(True, 1, 3),
            beside_total(True, 2, 3),
            beside_combine,
        ],
    )
    grad_in, grad_out = made_in, made_out
    if replicas != 2:
        grad_in, grad_out = (lax.psum(g.astype(BF), "rep").astype(F32) for g in (grad_in, grad_out))
    if other_sums is None:
        end = split + width
        dense_grads = (
            sums[:, :split],
            sums[:, split:end],
            sums[:, end : end + experts],
            sums[:, end + experts],
            sums[:, end + experts + 1],
        )
    else:
        rows = sums.shape[0]
        *dense_grads, one_gain, two_gain = call(
            "finish",
            functools.partial(finish_kernel, experts),
            (1,),
            [place, whole(sums), whole(other_sums)],
            [made(shape, F32) for shape in ((rows, split), (rows, width), (experts, rows), (1, rows), (1, rows))],
        )
        dense_grads[2] = dense_grads[2].T
        dense_grads += [one_gain.reshape(rows), two_gain.reshape(rows)]
    return (outputs, input_grads, *dense_grads, grad_in, grad_out)


def solution(mesh):
    tokens = P(None, ("rep", "grp"), None, None)
    rows = P("grp", None)
    expert = P("grp", None, None)
    return jax.shard_map(
        shards,
        mesh=mesh,
        in_specs=(tokens, rows, rows, rows, P("grp"), P("grp"), expert, expert, tokens, tokens),
        out_specs=(tokens, tokens, rows, rows, rows, P("grp"), P("grp"), expert, expert),
        check_vma=False,
    )
```

```python
import functools

import jax
import jax.numpy as jnp
from jax import lax
from jax.experimental import pallas as pl
from jax.experimental.pallas import tpu as pltpu
from jax.sharding import PartitionSpec as P

HEADS = 12
EPSILON = 1e-06
BF = jnp.bfloat16
F32 = jnp.float32
LANES = 128
COST = 0.6
FIRST = 18


def dot_tn(left, right):
    return lax.dot_general(left, right, (((0,), (0,)), ((), ())), preferred_element_type=F32)


def dot_nt(left, right):
    return lax.dot_general(left, right, (((1,), (1,)), ((), ())), preferred_element_type=F32)


def dot_nn(left, right):
    return jnp.dot(left, right, preferred_element_type=F32)


def normalize(values):
    center = values - jnp.mean(values, -1, keepdims=True)
    inverse = lax.rsqrt(jnp.mean(center * center, -1, keepdims=True) + EPSILON)
    return center * inverse, inverse


def norm_backward(grad_rows, unit_rows, inverse, gain_row):
    scaled = grad_rows * gain_row
    inner = (
        scaled
        - jnp.mean(scaled, -1, keepdims=True)
        - unit_rows * jnp.mean(scaled * unit_rows, -1, keepdims=True)
    )
    return inner * inverse


def call(name, body, grid, ins, outs, scratch=(), flops=0, vmem=56, through=(), into=(), after=()):
    buffers = [(i, array) for i, array in enumerate(into) if array is not None]
    kept = list(through) + [array for _, array in buffers] + list(after)
    count, made_count = len(ins), len(outs)
    aliases = {count + i: made_count + i for i in range(len(through))}
    for place, (i, _) in enumerate(buffers):
        aliases[count + len(through) + place] = i

    def inner(*refs):
        rest = refs[count + len(kept) :]
        body(*refs[:count], *rest[:made_count], *rest[made_count + len(through) :])

    anywhere = pl.BlockSpec(memory_space=pltpu.HBM)
    return pl.pallas_call(
        inner if kept else body,
        grid=grid,
        in_specs=[
            pl.BlockSpec(memory_space=index) if block is None else pl.BlockSpec(block, index)
            for _, block, index in ins
        ]
        + [anywhere] * len(kept),
        out_specs=[pl.BlockSpec(block, index) for _, _, block, index in outs] + [anywhere] * len(through),
        out_shape=[jax.ShapeDtypeStruct(shape, dtype) for shape, dtype, _, _ in outs]
        + [jax.ShapeDtypeStruct(array.shape, array.dtype) for array in through],
        scratch_shapes=list(scratch),
        input_output_aliases=aliases,
        compiler_params=pltpu.CompilerParams(vmem_limit_bytes=vmem * 2**20),
        cost_estimate=pl.CostEstimate(flops=int(flops * COST), bytes_accessed=0, transcendentals=0),
        name=name,
    )(*[array for array, _, _ in ins], *kept)


def whole(array):
    return (array, array.shape, lambda i: (0,) * array.ndim)


def made(shape, dtype):
    return (shape, dtype, shape, lambda i: (0,) * len(shape))


def of_micro(array, m):
    lead = array.ndim - 2
    return (array, (None,) * lead + array.shape[-2:], lambda i: (m,) + (0,) * (array.ndim - 1))


def head_mask(width):
    return lax.broadcasted_iota(jnp.int32, (1, LANES), 1) // (width // HEADS)


def softmax(scores):
    top = jnp.exp(scores - jnp.max(scores, -1, keepdims=True))
    return top * (1.0 / jnp.sum(top, -1, keepdims=True))


def hold_kernel(out):
    out[...] = jnp.zeros_like(out)


def hold(array, *waited):
    if not waited:
        return array
    after = [corner(w) for w in waited]
    return call("hold", hold_kernel, (1,), [], [made((8, LANES), F32)], through=[array], after=after)[1]


def join_kernel(qkv, proj, router, gain_one, gain_two, out):
    rows = qkv.shape[0]
    out[:, : qkv.shape[1]] = qkv[...]
    end = qkv.shape[1] + proj.shape[1]
    out[:, qkv.shape[1] : end] = proj[...]
    parts = [router[...].astype(F32), gain_one[...].astype(F32), gain_two[...].astype(F32)]
    parts.append(jnp.zeros((LANES - router.shape[0] - 2, rows), F32))
    out[:, end:] = jnp.concatenate(parts, 0).T.astype(BF)


def gather_kernel(table, rows, out):
    out[...] = dot_nn(table[...], rows[...]).astype(BF).reshape(out.shape)


def gain_rows(small, experts):
    return small[...].astype(F32).T[experts : experts + 2]


def assemble(differ, place, pieces, full):
    rows = pieces[0].shape[0]
    for piece, (first, other) in zip(pieces, differ):
        at = place[0] ^ jnp.where(place[1] == 0, first, other)
        full[pl.ds(pl.multiple_of(at * rows, 16), rows), :] = piece[...]


def forward_kernel(split, experts, differ, image, table, grad_y, *refs):
    if differ is None:
        w_qkv, w_proj, small, *outs = refs
    else:
        place, *pieces = refs[: 1 + len(differ)]
        *outs, full = refs[1 + len(differ) :]
        assemble(differ, place, pieces, full)
        end = split + image.shape[1]
        w_qkv, w_proj, small = full.at[:, :split], full.at[:, split:end], full.at[:, end:]
    one_o, packed_o, mix_o, middle_o, slots_o = outs
    gains = gain_rows(small, experts)
    width = image.shape[1]
    states = image[...].astype(F32)
    unit, _ = normalize(states)
    one = (unit * gains[0:1]).astype(BF)
    one_o[...] = one
    packed_o[...] = dot_nn(one, w_qkv[...]).astype(BF)
    head = head_mask(width)
    per = LANES * HEADS // width
    factor = (width // HEADS) ** (-0.5)
    for low in range(0, width, LANES):
        query = packed_o[:, low : low + LANES]
        keys = packed_o[:, width + low : width + low + LANES]
        values = packed_o[:, 2 * width + low : 2 * width + low + LANES]
        mixed = 0.0
        for h in range(per):
            mine = (head == h).astype(BF)
            weights = softmax(dot_nt(query * mine, keys) * factor).astype(BF)
            mixed = mixed + dot_nn(weights, values * mine)
        mix_o[:, low : low + LANES] = mixed.astype(BF)
    middle = states + dot_nn(mix_o[...], w_proj[...])
    middle_o[...] = middle
    unit, _ = normalize(middle)
    two = (unit * gains[1:2]).astype(BF)
    block = slots_o.shape[:1] + slots_o.shape[2:]
    for at, rows in enumerate((two, grad_y[...])[: slots_o.shape[1]]):
        slots_o[:, at] = dot_nn(table[...], rows).astype(BF).reshape(block)


def backward_kernel(
    column, last, image, grad_y, middle, packed, backs, table, w_proj, small, tail_in, w_all, *refs
):
    if last:
        place, *late, grad_image_o, kept_o, sent_o = refs[:8]
        mixture_s, grad_packed_o, low_o, sums, w_qkv, *held, arrived = refs[8:]
    else:
        grad_image_o, grad_packed_o, low_o, tail_o, mixture_s, w_qkv, arrived = refs
        late, held = [], []
    first = pl.program_id(0) == 0
    fetches = [pltpu.make_async_copy(w_all.at[:, : w_qkv.shape[1]], w_qkv, arrived.at[0])]
    fetches += [pltpu.make_async_copy(a, b, arrived.at[1 + i]) for i, (a, b) in enumerate(zip(late, held))]

    @pl.when(first)
    def _():
        for fetch in fetches:
            fetch.start()

    width = image.shape[1]
    backs = backs[...]
    gains = gain_rows(small, column)
    grad_two = dot_tn(table[...], backs.reshape(-1, width))
    unit, inverse = normalize(middle[...])
    gain_two = grad_two * unit
    grad_middle = grad_y[...].astype(F32) + norm_backward(grad_two, unit, inverse, gains[1:2])
    low_o[...] = grad_middle.astype(BF)
    mixture_s[...] = dot_nt(low_o[...], w_proj[...]).astype(BF)
    head = head_mask(width)
    per = LANES * HEADS // width
    factor = (width // HEADS) ** (-0.5)
    for low in range(0, width, LANES):
        query = packed[:, low : low + LANES]
        keys = packed[:, width + low : width + low + LANES]
        values = packed[:, 2 * width + low : 2 * width + low + LANES]
        grad_mixed = mixture_s[:, low : low + LANES]
        grad_query = grad_keys = grad_values = 0.0
        for h in range(per):
            mine = (head == h).astype(BF)
            query_h, keys_h, grad_h = query * mine, keys * mine, grad_mixed * mine
            weights = softmax(dot_nt(query_h, keys) * factor)
            grad_values = grad_values + dot_tn(weights.astype(BF), grad_h)
            grad_weights = dot_nt(grad_h, values)
            inner = jnp.sum(grad_weights * weights, -1, keepdims=True)
            grad_scores = (weights * (grad_weights - inner)).astype(BF)
            grad_query = grad_query + dot_nn(grad_scores, keys_h)
            grad_keys = grad_keys + dot_tn(grad_scores, query_h)
        grad_packed_o[:, low : low + LANES] = (grad_query * factor).astype(BF)
        grad_packed_o[:, width + low : width + low + LANES] = (grad_keys * factor).astype(BF)
        grad_packed_o[:, 2 * width + low : 2 * width + low + LANES] = grad_values.astype(BF)

    @pl.when(first)
    def _():
        fetches[0].wait()

    grad_one = dot_nt(grad_packed_o[...], w_qkv[...])
    unit, inverse = normalize(image[...].astype(F32))
    gain_one = grad_one * unit
    grad_image_o[...] = (grad_middle + norm_backward(grad_one, unit, inverse, gains[0:1])).astype(BF)
    lane = lax.broadcasted_iota(jnp.int32, (image.shape[0], LANES), 1)
    tail = 0.0
    for at, gain in ((column, gain_one), (column + 1, gain_two)):
        column_of = (lane == at).astype(BF)
        high = gain.astype(BF)
        tail = tail + dot_tn(high, column_of) + dot_tn((gain - high.astype(F32)).astype(BF), column_of)
    if last:
        sums[:, 4 * width :] = (tail_in[...] + tail).astype(sums.dtype)
        for fetch in fetches[1:]:
            fetch.wait()
        ones, mixes, packs, lows = held
        dense_sums(place, (ones, mixes), (packs, lows), (grad_packed_o, low_o), sums, kept_o, sent_o)
    else:

        @pl.when(first)
        def _():
            tail_o[...] = tail_in[...] + tail

        @pl.when(jnp.logical_not(first))
        def _():
            tail_o[...] += tail


def expert_kernel(own, experts, slots_in, grad_in, here, router, w_in, w_out, *refs):
    tail_in, *refs = refs if own == "later" else (None, *refs)
    active_o, hidden_o, result_o, rows_o, *rest = refs
    step = pl.program_id(0)
    if own:
        sent_o, back_o, tail_o, probs_s, result_s, back_s = rest
    width = slots_in.shape[-1]
    rows = slots_in[...].reshape(-1, width)

    @pl.when(step == 0)
    def _():
        rows_o[...] = rows
        logits = dot_nn(rows, router[...])
        lane = lax.broadcasted_iota(jnp.int32, logits.shape, 1)
        probs = softmax(jnp.where(lane < experts, logits, -1e30))
        gate = jnp.sum(probs * here[...], -1, keepdims=True)
        result_o[...] = (gate * grad_in[...].reshape(-1, width).astype(F32)).astype(BF)
        if own:
            probs_s[...] = probs
            result_s[...] = jnp.zeros_like(result_s)
            back_s[...] = jnp.zeros_like(back_s)

    hidden = dot_nn(rows, w_in[...])
    grad_active = dot_nt(result_o[...], w_out[...])
    cumulative = 0.5 + 0.5 * lax.erf(hidden * (0.5**0.5))
    active = (hidden * cumulative).astype(BF)
    slope = cumulative + hidden * jnp.exp(-0.5 * hidden * hidden) * 0.3989422804014327
    grad_hidden = (grad_active * slope).astype(BF)
    active_o[...] = active
    hidden_o[...] = grad_hidden
    if own:
        result_s[...] += dot_nn(active, w_out[...])
        back_s[...] += dot_nt(grad_hidden, w_in[...])

        @pl.when(step == pl.num_programs(0) - 1)
        def _():
            probs = probs_s[...]
            gate = jnp.sum(probs * here[...], -1, keepdims=True)
            result = result_s[...]
            grad_gate = jnp.sum(grad_in[...].reshape(-1, width).astype(F32) * result, -1, keepdims=True)
            grad_logit = (grad_gate * gate * (here[...] - probs)).astype(BF)
            back_o[...] = (back_s[...] + dot_nt(grad_logit, router[...])).astype(BF).reshape(back_o.shape)
            sent_o[...] = (gate * result).astype(BF).reshape(sent_o.shape)
            tail = dot_tn(rows, grad_logit)
            tail_o[...] = tail if tail_in is None else tail_in[...] + tail


def total_kernel(left, right, *refs):
    total = dot_tn(left[...].reshape(-1, left.shape[-1]), right[...].reshape(-1, right.shape[-1]))
    refs[-1][...] = total if len(refs) == 1 else refs[0][...] + total


def dense_sums(place, lefts, rights, last, sums, kept_o, sent_o):
    width = lefts[0].shape[-1]

    def total(which, part):
        left, right = lefts[which], rights[which]
        result = dot_tn(left[left.shape[0] - 1], last[which][:, part])
        for i in range(right.shape[0]):
            result = result + dot_tn(left[i], right[i, :, part])
        return result.astype(sums.dtype)

    for j in range(3):
        part = slice(j * width, (j + 1) * width)
        sums[:, part] = total(0, part)
    sums[:, 3 * width : 4 * width] = total(1, slice(None))
    half, rows = kept_o.shape[:2]
    bit = place[0] & 1
    for j in range(half):
        for out, at in ((kept_o, 2 * j + bit), (sent_o, 2 * j + 1 - bit)):
            out[j] = sums[pl.ds(pl.multiple_of(at * rows, rows), rows), :].astype(BF)


def combine_kernel(middle, tables, results, out):
    for m in range(middle.shape[0]):
        rows = results[:, m].reshape(-1, middle.shape[-1])
        out[m, 0] = (middle[m] + dot_tn(tables[m], rows)).astype(BF)


def finish_kernel(experts, place, mine, other, qkv_o, proj_o, router_o, one_o, two_o):
    cut = other.shape[1] // 2
    split = qkv_o.shape[1]
    first = place[1] == 0
    for k in range(4):
        part = slice(k // 2 * cut, (k // 2 + 1) * cut)
        both = (mine[:, part], other[:, part])
        columns = jnp.where(first, both[k % 2], both[1 - k % 2]).astype(F32)
        at = k * cut
        if at < split:
            qkv_o[:, at : at + cut] = columns
        else:
            proj_o[:, at - split : at - split + cut] = columns
    tail = mine[:, 2 * cut :].astype(F32)
    rows = tail.T
    router_o[...] = rows[:experts]
    one_o[...] = rows[experts : experts + 1]
    two_o[...] = rows[experts + 1 : experts + 2]


def slot_tables(routes, experts, capacity):
    rows = routes.shape[1]
    ordering = jnp.concatenate([routes[:, :, 0], routes[:, :, 1]], 1)
    onehot = (ordering[:, :, None] == jnp.arange(experts, dtype=jnp.int32)).astype(BF)
    count = 2 * rows
    earlier = (jnp.arange(count)[:, None] > jnp.arange(count)[None, :]).astype(BF)
    before = jnp.einsum("ab,mbe->mae", earlier, onehot, preferred_element_type=F32)
    rank = jnp.sum(before * onehot, -1).astype(jnp.int32)
    target = jnp.where(rank < capacity, ordering * capacity + rank, -1)
    slots = jnp.arange(experts * capacity, dtype=jnp.int32)[None, :, None]
    first, second = target[:, None, :rows], target[:, None, rows:]
    return ((slots == first) | (slots == second)).astype(BF)


def exchange(blocks):
    merged = blocks.reshape(blocks.shape[0], -1, blocks.shape[-1])
    return lax.all_to_all(merged, "grp", split_axis=0, concat_axis=0, tiled=True).reshape(blocks.shape)


def add_low(left, right):
    return (left.astype(F32) + right.astype(F32)).astype(BF)


def corner(array):
    return array[(0,) * (array.ndim - 2)][:16, :LANES]


def scatter_sums(kept, sent, experts, replicas, beside):
    bits = experts.bit_length() - 1
    place = lax.axis_index("grp")
    own_rep = lax.axis_index("rep")
    rows, columns = kept.shape[1], kept.shape[2] - LANES
    half = columns // 2
    swap = [(0, 1), (1, 0)]

    def send(array, bit):
        return lax.ppermute(array, "grp", [(g, g ^ (1 << bit)) for g in range(experts)])

    def halve(array, bit, run=lambda kept: kept):
        mine, axis = (place >> bit) & 1, bits - 1 - bit
        sent = lax.dynamic_index_in_dim(array, 1 - mine, axis, keepdims=False)
        kept = lax.dynamic_index_in_dim(array, mine, axis, keepdims=False)
        return add_low(run(kept), send(sent, bit))

    def halve_columns(array, shared, run=lambda kept: kept):
        if replicas != 2:
            return run(array)
        cut = (array.shape[-1] - shared) // 2
        parts = [array[..., :cut], array[..., cut : 2 * cut]]
        mine, other = (jnp.where(own_rep == 0, parts[i], parts[1 - i]) for i in (0, 1))
        if shared:
            mine, other = (jnp.concatenate([p, array[..., 2 * cut :]], -1) for p in (mine, other))
        return add_low(run(mine), lax.ppermute(other, "rep", swap))

    sums = add_low(beside[0](kept), send(sent, 0))
    sums = sums.reshape((2,) * (bits - 1) + sums.shape[1:])
    left = jnp.concatenate([sums[..., :half], sums[..., columns:]], -1)
    right = sums[..., half:columns]
    left, right = halve_columns(left, LANES, beside[1]), halve(right, 1)
    left, right = halve(left, 1, beside[2]), halve_columns(right, 0)
    cut = right.shape[-1]
    sums = jnp.concatenate([left[..., :cut], right, left[..., cut:]], -1)
    for bit in range(2, bits):
        sums = halve(sums, bit, beside[min(bit + 1, 4)] if bit < 4 else lambda kept: kept)
    if replicas != 2:
        beside[5](sums)
        return lax.psum(sums, "rep").astype(F32), None
    return beside[5](sums), lax.ppermute(sums[:, : 2 * cut], "rep", swap)


def pick_kernel(place, first, other, out):
    out[...] = jnp.where(place[1] == 0, first[...], other[...])


def gather_pieces(piece, experts, place, after):
    both = ("rep", "grp")

    def send(array, first, other):
        pairs = [(r * experts + g, r * experts + (g ^ k)) for r, k in enumerate((first, other)) for g in range(experts)]
        return lax.ppermute(array, both, pairs)

    def swap(array):
        return lax.ppermute(array, "rep", [(0, 1), (1, 0)])

    near, far = send(piece, 4, 4), send(piece, 8, 12)
    [mixed] = call(
        "pick",
        pick_kernel,
        (1,),
        [place, whole(piece), whole(near)],
        [made(piece.shape, piece.dtype)],
        after=[after],
    )
    mixed = send(mixed, 2, 2)
    mixed_far = send(far, 2, 2)
    found = [(piece, 0, 0), (near, 4, 4), (far, 8, 12), (swap(far), 12, 8)]
    found += [(mixed, 2, 6), (swap(mixed), 6, 2), (mixed_far, 10, 14), (swap(mixed_far), 14, 10)]
    found += [(send(array, 1, 1), first ^ 1, other ^ 1) for array, first, other in found]
    return [array for array, _, _ in found], [(first, other) for _, first, other in found]


def shards(images, attn_qkv, attn_proj, router, gain_attn, gain_moe, expert_in, expert_out, routes, cotangent):
    experts = lax.axis_size("grp")
    replicas = lax.axis_size("rep")
    mine = lax.axis_index("grp")
    micro, _, seq, width = images.shape
    capacity = max(2, 8 * seq * images.shape[1] // (3 * experts))
    slots = experts * capacity
    split = attn_qkv.shape[1]
    deep = expert_in.shape[2]
    here = (lax.broadcasted_iota(jnp.int32, (1, LANES), 1) == mine).astype(F32)

    tables = slot_tables(routes.reshape(micro, seq, 2), experts, capacity)

    one_block = (experts, 1, capacity, width)
    first_grads = call(
        "pack",
        gather_kernel,
        (1,),
        [of_micro(tables, 0), of_micro(cotangent, 0)],
        [made(one_block, BF)],
        flops=2 * slots * seq * width,
    )[0]
    shard = attn_qkv.shape[0]
    [piece] = call(
        "join",
        join_kernel,
        (1,),
        [whole(a) for a in (attn_qkv, attn_proj, router.T, gain_attn.reshape(1, shard), gain_moe.reshape(1, shard))],
        [made((shard, split + width + LANES), BF)],
    )
    full_shape = (width, piece.shape[1])
    direct = experts == 16 and replicas == 2 and piece.shape[0] % 16 == 0
    place = (jnp.stack([mine, lax.axis_index("rep")]).astype(jnp.int32), None, pltpu.SMEM)
    if direct:
        pieces, differ = gather_pieces(piece, experts, place, first_grads)
        full = None
    else:
        full = lax.all_gather(piece, "grp", axis=0, tiled=True)

    def parts_of(full):
        return [
            (full, (width, split), lambda i: (0, 0)),
            (full, (width, width), lambda i: (0, split // width)),
            (full, (width, LANES), lambda i: (0, (split + width) // LANES)),
        ]

    first_grads = exchange(first_grads)

    saved, sents = [None] * 4, []
    for m in range(micro):
        outs = [
            ((micro,) + shape, dtype, (None,) + shape, lambda i, m=m: (m, 0, 0))
            for shape, dtype in (((seq, width), BF), ((seq, split), BF), ((seq, width), BF), ((seq, width), F32))
        ]
        outs.append(made((experts, min(2, m + 1), capacity, width), BF))
        assembles = full is None
        weights = [place] + [whole(p) for p in pieces] if assembles else parts_of(full)
        made_here = call(
            "attend",
            functools.partial(forward_kernel, split, experts, differ if assembles else None),
            (1,),
            [of_micro(images, m), of_micro(tables, m), of_micro(cotangent, m)] + weights,
            outs + ([made(full_shape, BF)] if assembles and m else []),
            [pltpu.VMEM(full_shape, BF)] if assembles and not m else [],
            flops=(6 if m else FIRST) * 10**9,
            through=sents[1:],
            into=saved,
        )
        saved, sent, handed = made_here[:4], made_here[4], made_here[5:]
        if assembles and m:
            full, *handed = handed
        sents[1:] = handed
        sents.append(sent)
    w_qkv, w_proj, w_router = parts_of(full)

    block = 1024
    swap = [(0, 1), (1, 0)]
    order = [(True, 0), (False, 0), (True, 1), (True, 2), (False, 1), (False, 2)]
    if replicas != 2:
        order = [pair for pair in order if pair[0]]
    sets, groups = len(order), replicas if replicas == 2 else 1
    stacks = [None] * 6

    def part_of(array, at):
        return (array, (experts, None, capacity, width), lambda i: (0, at, 0, 0))

    def expert_call(own, m, arrays, through, after=()):
        place = order.index((own, m))
        ins = [
            part_of(*arrays[0]),
            part_of(*arrays[1]),
            whole(here),
            w_router,
            (expert_in, (None, width, block), lambda i: (0, 0, i)),
            (expert_out, (None, block, width), lambda i: (0, i, 0)),
        ]
        if own and tails:
            ins.append(whole(tails[-1]))
        outs = [
            ((sets, slots, deep), BF, (None, slots, block), lambda i: (place, 0, i)),
            ((sets, slots, deep), BF, (None, slots, block), lambda i: (place, 0, i)),
            ((sets, slots, width), BF, (None, slots, width), lambda i: (place, 0, 0)),
            ((sets, slots, width), BF, (None, slots, width), lambda i: (place, 0, 0)),
        ]
        scratch = []
        if own:
            last = m == micro - 1
            outs += [
                ((experts, micro, capacity, width), BF, (experts, None, capacity, width), lambda i: (0, m, 0, 0)),
                (one_block, BF, (experts, None, capacity, width), lambda i: (0, 0, 0, 0))
                if last
                else ((experts, micro - 1, capacity, width), BF, (experts, None, capacity, width), lambda i: (0, m, 0, 0)),
                made((width, LANES), F32),
            ]
            scratch = [pltpu.VMEM((slots, LANES), F32)] + [pltpu.VMEM((slots, width), F32)] * 2
        count = (5 if last else 6) if own else 4
        made_here = call(
            "expert_own" if own else "expert_other",
            functools.partial(expert_kernel, "later" if own and tails else own, experts),
            (deep // block,),
            ins,
            outs,
            scratch,
            flops=2 * slots * width * deep * (6 if own else 4),
            vmem=56,
            through=through,
            into=stacks[:count],
            after=[corner(a) for a in after],
        )
        stacks[:count] = made_here[:count]
        return made_here[count:]

    def total(lead, early, before, into, through, part=0, parts=1):
        steps = deep // total_block // parts
        first = part * steps
        half = sets // groups if early or before is not None else sets
        at = 0 if early or half == sets else groups - 1
        if lead:
            left = (stacks[0], (half, slots, total_block), lambda i: (at, 0, first + i))
            right = (stacks[2], (half, slots, width), lambda i: (at, 0, 0))
            out = ((1, deep, width), F32, (None, total_block, width), lambda i: (0, first + i, 0))
        else:
            left = (stacks[3], (half, slots, width), lambda i: (at, 0, 0))
            right = (stacks[1], (half, slots, total_block), lambda i: (at, 0, first + i))
            out = ((1, width, deep), F32, (None, width, total_block), lambda i: (0, 0, first + i))
        return call(
            "total_out" if lead else "total_in",
            total_kernel,
            (steps,),
            [left, right] + ([] if before is None else [(before,) + out[2:]]),
            [out],
            flops=2 * half * slots * width * steps * total_block,
            vmem=56,
            through=through,
            into=[into],
        )

    total_block = 512

    def swapped(array):
        return lax.ppermute(array, "rep", swap) if replicas == 2 else None


    def other(m, through):
        return expert_call(False, m, theirs[m], through) if replicas == 2 else through

    def waited(m):
        return [array for array, _ in theirs[m]] if replicas == 2 else []

    arrived = exchange(sents[0])
    ours = [((arrived, 0), (first_grads, 0))]
    theirs = [((swapped(arrived), 0), (swapped(first_grads), 0))]
    tails = []
    for m in range(1, micro):
        arrived = exchange(hold(sents[m], *waited(0)[1:]) if m == 1 else sents[m])
        tail, *handed = expert_call(True, m - 1, ours[m - 1], sents[m + 1 : m + 2] if m > 1 else [])
        tails.append(tail)
        if m == 1:
            handed = other(0, sents[2:3])
        sents[m + 1 : m + 2] = handed
        came = arrived.reshape(sents[1].shape)
        ours.append(((came, 0), (came, 1)))
        came = swapped(came)
        theirs.append(((came, 0), (came, 1)))
    early_in = None
    if groups == 2:
        early_in, stacks[5] = total(False, True, None, None, [stacks[5]])
    backs = exchange(stacks[5])
    last_back, tail = expert_call(True, micro - 1, ours[-1], [], waited(1)[:1])
    tails.append(tail)
    [last_back] = other(1, [last_back])
    last_back = exchange(last_back)

    one_all, packed_all, mix_all, middle_all = saved
    half_shape = (experts // 2, width // experts, full_shape[1])

    def backward_call(last, backs, tail, into, late=(), through=(), after=()):
        start, count = (micro - 1, 1) if last else (0, micro - 1)

        def of(array):
            lead = array.ndim - 2
            return (
                array,
                (None,) * lead + array.shape[-2:],
                lambda i: (start + i,) + (0,) * (array.ndim - 1),
            )

        def each(shape, dtype):
            return ((count,) + shape, dtype, (None,) + shape, lambda i: (i,) + (0,) * len(shape))

        outs = [(images.shape, BF, (None, None, seq, width), lambda i: (start + i, 0, 0, 0))]
        scratch = [pltpu.VMEM((seq, width), BF)]
        if last:
            outs += [made(half_shape, BF)] * 2
            scratch += [pltpu.VMEM((seq, split), BF), pltpu.VMEM((seq, width), BF)]
            scratch += [pltpu.VMEM(full_shape, BF if (width // experts) % 16 == 0 else F32)]
        else:
            outs += [each((seq, split), BF), each((seq, width), BF), made((width, LANES), F32)]
        held = [pltpu.VMEM((width, split), BF)] + [pltpu.VMEM(a.shape, a.dtype) for a in late]
        scratch += held + [pltpu.SemaphoreType.DMA((len(held),))]
        return call(
            "attend_back",
            functools.partial(backward_kernel, experts, last),
            (count,),
            [of(images), of(cotangent), of(middle_all), of(packed_all)]
            + [(backs, (experts, None, capacity, width), lambda i: (0, i, 0, 0)), of(tables), w_proj, w_router]
            + [whole(tail), (full, None, pl.ANY)]
            + ([place] if last else [])
            + [(a, None, pl.ANY) for a in late],
            outs,
            scratch,
            flops=8 * 10**9 * count,
            through=through,
            into=[into],
            after=[corner(a) for a in after],
        )

    input_grads, grads_packed, lows, tail, stacks[4] = backward_call(
        False, backs, tails[-1], None, through=[stacks[4]], after=waited(micro - 1)[:1]
    )
    input_grads, kept, sent = backward_call(
        True, last_back, tail, input_grads, (one_all, mix_all, grads_packed, lows)
    )
    results = exchange(stacks[4])

    made_in = made_out = outputs = None

    def beside_others(m):
        return lambda kept: other(m, [kept])[0]

    def beside_total(lead, part=0, parts=1):
        def run(kept):
            nonlocal made_in, made_out
            if lead:
                made_out, kept = total(True, False, None, made_out, [kept], part, parts)
            else:
                made_in, kept = total(False, False, early_in, made_in, [kept], part, parts)
            return kept

        return run

    def beside_combine(kept):
        nonlocal outputs
        outputs, kept = call(
            "combine",
            combine_kernel,
            (1,),
            [whole(a) for a in (middle_all, tables, results)],
            [made(images.shape, BF)],
            flops=micro * 10**9,
            through=[kept],
        )
        return kept

    def both(*runs):
        def run(kept):
            for r in runs:
                kept = r(kept)
            return kept

        return run

    sums, other_sums = scatter_sums(
        kept,
        sent,
        experts,
        replicas,
        [
            beside_others(2),
            beside_total(False),
            beside_total(True, 0, 3),
            beside_total(True, 1, 3),
            beside_total(True, 2, 3),
            beside_combine,
        ],
    )
    grad_in, grad_out = made_in, made_out
    if replicas != 2:
        grad_in, grad_out = (lax.psum(g.astype(BF), "rep").astype(F32) for g in (grad_in, grad_out))
    if other_sums is None:
        end = split + width
        dense_grads = (
            sums[:, :split],
            sums[:, split:end],
            sums[:, end : end + experts],
            sums[:, end + experts],
            sums[:, end + experts + 1],
        )
    else:
        rows = sums.shape[0]
        *dense_grads, one_gain, two_gain = call(
            "finish",
            functools.partial(finish_kernel, experts),
            (1,),
            [place, whole(sums), whole(other_sums)],
            [made(shape, F32) for shape in ((rows, split), (rows, width), (experts, rows), (1, rows), (1, rows))],
        )
        dense_grads[2] = dense_grads[2].T
        dense_grads += [one_gain.reshape(rows), two_gain.reshape(rows)]
    return (outputs, input_grads, *dense_grads, grad_in, grad_out)


def solution(mesh):
    tokens = P(None, ("rep", "grp"), None, None)
    rows = P("grp", None)
    expert = P("grp", None, None)
    return jax.shard_map(
        shards,
        mesh=mesh,
        in_specs=(tokens, rows, rows, rows, P("grp"), P("grp"), expert, expert, tokens, tokens),
        out_specs=(tokens, tokens, rows, rows, rows, P("grp"), P("grp"), expert, expert),
        check_vma=False,
    )
```
